32 devices in a mesh: dp: 2 (over y), tm: 16 (over z, x, core).
Axes of the slice: x: 2, y: 2, z: 4, core: 2. Of those that a mesh axis runs over, the one named last changes fastest.
Arguments:
- signal: bfloat16 [2, 2048, 512], P('dp', 'tm'), may hold values from -6 to 6
- conv_weight: bfloat16 [2, 1024, 512], replicated, may hold values from -0.1875 to 0.1875
- res_weight: bfloat16 [2, 256, 768], replicated, may hold values from -0.375 to 0.375
- grad_out: bfloat16 [2, 2048, 512], P('dp', 'tm'), may hold values from -6 to 6
- skip_cotangent: bfloat16 [2, 2048, 256], P('dp', 'tm'), may hold values from -6 to 6
Outputs:
- input_grad: bfloat16 [2, 2048, 512], P('dp', 'tm')
- conv_grad: bfloat16 [2, 1024, 512], P(None, 'tm')
- res_grad: bfloat16 [2, 256, 768], replicated
The draws below stay inside these ranges and needn't reach their ends.
All inputs are finite; a program needn't handle non-finite values.
Results may differ from the reference program's by a relative error of at most 0.0063.
Values may be sent and summed in bfloat16 or wider, within the bound.
No kernel may reach another device: no remote copies, remote signals or barrier semaphores. Data moves between devices by JAX's collectives and lax.ppermute only.
A program may use at most 64 MiB of HBM per device.

```python
import jax
import jax.numpy as jnp
from jax import lax

C = 512
GC = 256
SK = 256
STREAMS = 2
TIME = 2048
DILATION_INNER = 32
DILATION_OUTER = 256


def raised(drawn, key, source, target, parts, factor):
    def block_of(position):
        return (jnp.arange(drawn.shape[position]) // (drawn.shape[position] // parts)).reshape((-1,) + (1,) * (drawn.ndim - 1 - position))

    near = jax.random.permutation(key, parts)[block_of(target)]
    other_side = (block_of(target) + parts // 2) % parts
    return jnp.where((block_of(source) == near) | (block_of(source) == other_side), factor * drawn, drawn)


def steps_of(stream_key, dims, pieces, least, top_value):
    def one(position, blocks):
        draws = jax.random.uniform(jax.random.fold_in(jax.random.fold_in(stream_key, 6), position), (blocks,), jnp.float32, least / len(pieces), top_value / len(pieces))
        return jnp.repeat(jnp.exp(draws), dims[position] // blocks).reshape((-1,) + (1,) * (len(dims) - position - 1))

    level = one(*pieces[0])
    for cut in pieces[1:]:
        level = level * one(*cut)
    return level


def noise(key, dims, scale, reach, split=(), kind=jnp.bfloat16):
    entries = jax.random.normal(key, dims, jnp.float32) * scale
    if len(split) > 0:
        entries = steps_of(key, dims, split, -0.22, 0.18) * entries
    return jnp.clip(entries, min=-reach, max=reach).astype(kind)


def bell_draw_with(rng, shape, scale, bound, shards, heavy, held_as=jnp.bfloat16):
    entries = scale * jax.random.normal(rng, shape, jnp.float32)
    if shards:
        entries = entries * steps_of(rng, shape, shards, -0.22, 0.18)
    return jnp.clip(raised(entries, jax.random.fold_in(rng, 3), *heavy), -bound, bound).astype(held_as)


def setup_inputs(seed: int = 0) -> dict:
    key_of = jax.random.split(jax.random.key(seed), 6)
    return {
        "signal": bell_draw_with(key_of[0], (STREAMS, TIME, C), 1.0, 6.0, ((0, 2), (1, 16)), (1, 2, 16, 2.0)),
        "conv_weight": noise(key_of[1], (2, 2 * C, 2 * GC), (2 * C) ** -0.5, 0.1875),
        "res_weight": noise(key_of[2], (2, GC, C + SK), GC ** -0.5, 0.375),
        "grad_out": noise(key_of[3], (STREAMS, TIME, C), 1.0, 6.0, ((0, 2), (1, 16))),
        "skip_cotangent": bell_draw_with(key_of[4], (STREAMS, TIME, SK), 1.0, 6.0, ((0, 2), (1, 16)), (1, 2, 16, 2.0)),
    }


def delay(x, dist):
    zeros = jnp.zeros((dist, x.shape[1]), x.dtype)
    return jnp.concatenate([zeros, x[:-dist]], axis=0)


def shift_forward(x, dist):
    zeros = jnp.zeros((dist, x.shape[1]), x.dtype)
    return jnp.concatenate([x[dist:], zeros], axis=0)


def one_stream(signal, conv_weight, res_weight, grad_out, skip_cotangent):
    tap_distances = (DILATION_INNER, DILATION_OUTER)
    x = signal
    cats = []
    zvals = []
    hvals = []
    for layer in range(2):
        past = delay(x, tap_distances[layer])
        cat = jnp.concatenate([past, x], axis=1)
        z = jnp.dot(cat, conv_weight[layer], preferred_element_type=jnp.float32)
        h = (jnp.tanh(z[:, :GC]) * jax.nn.sigmoid(z[:, GC:])).astype(jnp.bfloat16)
        cats.append(cat)
        zvals.append(z)
        hvals.append(h)
        if layer == 0:
            resid = jnp.dot(h, res_weight[0][:, :C], preferred_element_type=jnp.float32)
            x = (x.astype(jnp.float32) + resid).astype(jnp.bfloat16)
    grad = grad_out.astype(jnp.float32)
    conv_terms = [None, None]
    res_terms = [None, None]
    for layer in (1, 0):
        outer = jnp.concatenate([grad.astype(jnp.bfloat16), skip_cotangent], axis=1)
        dh = lax.dot_general(outer, res_weight[layer], (((1,), (1,)), ((), ())), preferred_element_type=jnp.float32)
        z = zvals[layer]
        tf = jnp.tanh(z[:, :GC])
        sg = jax.nn.sigmoid(z[:, GC:])
        dz = jnp.concatenate([dh * sg * (1.0 - tf * tf), dh * tf * sg * (1.0 - sg)], axis=1).astype(jnp.bfloat16)
        wcat = lax.dot_general(dz, conv_weight[layer], (((1,), (1,)), ((), ())), preferred_element_type=jnp.float32)
        dpast = wcat[:, :C].astype(jnp.bfloat16)
        grad = grad + wcat[:, C:] + shift_forward(dpast, tap_distances[layer]).astype(jnp.float32)
        conv_terms[layer] = lax.dot_general(cats[layer], dz, (((0,), (0,)), ((), ())), preferred_element_type=jnp.float32)
        res_terms[layer] = lax.dot_general(hvals[layer], outer, (((0,), (0,)), ((), ())), preferred_element_type=jnp.float32)
    return grad.astype(jnp.bfloat16), jnp.stack(conv_terms), jnp.stack(res_terms)


def reference(signal, conv_weight, res_weight, grad_out, skip_cotangent):
    def step(carry, items):
        conv_sum, res_sum = carry
        sig, gout, sgrad = items
        igrad, conv_t, res_t = one_stream(sig, conv_weight, res_weight, gout, sgrad)
        return (conv_sum + conv_t, res_sum + res_t), igrad

    start = (jnp.zeros((2, 2 * C, 2 * GC), jnp.float32), jnp.zeros((2, GC, C + SK), jnp.float32))
    (conv_sum, res_sum), input_grad = lax.scan(step, start, (signal, grad_out, skip_cotangent))
    factor = float(STREAMS * TIME) ** -0.5
    conv_grad = (conv_sum * factor).astype(jnp.bfloat16)
    res_grad = (res_sum * factor).astype(jnp.bfloat16)
    return input_grad, conv_grad, res_grad
```

```python
import functools

import jax
import jax.numpy as jnp
from jax import lax
from jax.experimental import pallas as pl
from jax.experimental.pallas import tpu as pltpu
from jax.sharding import PartitionSpec as P

F32 = jnp.float32
BF16 = jnp.bfloat16
VMEM_LIMIT = 48 * 1024 * 1024


def mm(a, b):
    return jnp.dot(a, b, preferred_element_type=F32)


def mm_nt(a, b):
    return lax.dot_general(a, b, (((1,), (1,)), ((), ())), preferred_element_type=F32)


def mm_tn(a, b):
    return lax.dot_general(a, b, (((0,), (0,)), ((), ())), preferred_element_type=F32)


def call(kernel, outs, *args, scratch=(), flops=0, nbytes=0, name=None):
    return pl.pallas_call(
        kernel,
        out_shape=outs,
        in_specs=[pl.BlockSpec(memory_space=pltpu.VMEM)] * len(args),
        out_specs=[pl.BlockSpec(memory_space=pltpu.VMEM)] * len(outs),
        scratch_shapes=list(scratch),
        compiler_params=pltpu.CompilerParams(vmem_limit_bytes=VMEM_LIMIT),
        cost_estimate=pl.CostEstimate(flops=flops, bytes_accessed=nbytes, transcendentals=0),
        name=name,
    )(*args)


def shaped(shape, dtype=BF16):
    return jax.ShapeDtypeStruct(shape, dtype)


def place_conv(dst, part, base, groups, rows):
    per = part.shape[0] // rows
    for block in range(per):
        index = base + block
        g, x, c = index // 4, (index // 2) % 2, index % 2
        dst[c, x, g, 0:rows, :] = part[block * rows : (block + 1) * rows, :].astype(BF16)


def place_res(dst, part, which, groups, conv_rows, piece_rows):
    quarter = part.shape[0] // 4
    for c in range(2):
        for x in range(2):
            for block in range(quarter // 16):
                row = which * quarter + block * 16
                g, off = row // piece_rows, row % piece_rows
                src = (2 * c + x) * quarter + block * 16
                dst[c, x, g, conv_rows + off : conv_rows + off + 16, :] = part[src : src + 16, :].astype(BF16)


def forward_and_outer_kernel(
    groups, conv_rows, piece_rows,
    sig, near_in, far, far_near, cw, rw, grad, skip,
    send, keep, a_out, b_out, o_out, ga_out, x0_out, p0_out,
    staged,
):
    t, width = sig.shape
    near = near_in.shape[0]
    gated = rw.shape[1]
    core = lax.rem(lax.axis_index("tm"), 2)
    x0 = jnp.concatenate([sig[...], far[...]], axis=0)
    p0 = jnp.concatenate([near_in[...], sig[0 : t - near, :], far_near[...], far[0 : t - near, :]], axis=0)
    x0_out[...] = x0
    p0_out[...] = p0
    z0 = mm(p0, cw[0, 0:width, :]) + mm(x0, cw[0, width:, :])
    tf = jnp.tanh(z0[:, :gated])
    sg = jax.nn.sigmoid(z0[:, gated:])
    h0 = (tf * sg).astype(BF16)
    a_out[...] = sg * (1.0 - tf * tf)
    b_out[...] = tf * sg * (1.0 - sg)
    x1 = (x0.astype(F32) + mm(h0, rw[0, :, 0:width])).astype(BF16)
    z1 = mm(x1[t:, :], cw[1, 0:width, :]) + mm(x1[:t, :], cw[1, width:, :])
    tf = jnp.tanh(z1[:, :gated])
    sg = jax.nn.sigmoid(z1[:, gated:])
    h1 = (tf * sg).astype(BF16)
    g2 = grad[...]
    sk = skip[...]
    e1 = mm_nt(g2, rw[1, :, 0:width]) + mm_nt(sk, rw[1, :, width:])
    dz1 = jnp.concatenate([e1 * sg * (1.0 - tf * tf), e1 * tf * sg * (1.0 - sg)], axis=1).astype(BF16)
    half = width // conv_rows
    place_conv(staged, mm_tn(x1[t:, :], dz1), 0, groups, conv_rows)
    place_conv(staged, mm_tn(x1[:t, :], dz1), half, groups, conv_rows)
    dpast = mm_nt(dz1, cw[1, 0:width, :]).astype(BF16)
    ga = g2.astype(F32) + mm_nt(dz1, cw[1, width:, :])
    ga_out[...] = ga
    outer = jnp.concatenate([ga.astype(BF16), dpast], axis=0)
    o_out[...] = outer
    if groups * piece_rows > 3 * gated // 4:
        staged[:, :, :, conv_rows:, :] = jnp.zeros((2, 2, groups, piece_rows, width), BF16)
    place_res(staged, mm_tn(h1, g2), 0, groups, conv_rows, piece_rows)
    place_res(staged, mm_tn(h0, outer), 1, groups, conv_rows, piece_rows)
    skips = jnp.concatenate([mm_tn(h1, sk), mm_tn(h0[:t, :], sk)], axis=1)
    place_res(staged, skips, 2, groups, conv_rows, piece_rows)
    send[...] = staged[1 - core]
    keep[...] = staged[core]


def inner_kernel(
    groups, conv_rows, near,
    x0, p0, a, b, outer, ga, cw, rw, skip,
    send, keep, own_out, back_out, edge_out,
    staged,
):
    t = skip.shape[0]
    width = x0.shape[1]
    core = lax.rem(lax.axis_index("tm"), 2)
    e0 = mm_nt(outer[...], rw[0, :, 0:width])
    es = mm_nt(skip[...], rw[0, :, width:])
    e0 = jnp.concatenate([e0[:t, :] + es, e0[t:, :]], axis=0)
    dz0 = jnp.concatenate([e0 * a[...], e0 * b[...]], axis=1).astype(BF16)
    half = width // conv_rows
    place_conv(staged, mm_tn(p0[...], dz0), 0, groups, conv_rows)
    place_conv(staged, mm_tn(x0[...], dz0), half, groups, conv_rows)
    send[...] = staged[1 - core]
    keep[...] = staged[core]
    wp = mm_nt(dz0, cw[0, 0:width, :]).astype(BF16)
    wx = mm_nt(dz0, cw[0, width:, :])
    zero = jnp.zeros((near, width), F32)
    own_out[...] = ga[...] + wx[:t, :] + jnp.concatenate([wp[near:t, :].astype(F32), zero], axis=0)
    back_out[...] = (
        outer[t:, :].astype(F32) + wx[t:, :] + jnp.concatenate([wp[t + near :, :].astype(F32), zero], axis=0)
    ).astype(BF16)
    edge_out[...] = jnp.concatenate([wp[0:near, :], wp[t : t + near, :]], axis=0)


def add_core_kernel(got, kept, send, keep, staged):
    xbit = lax.rem(lax.axis_index("tm") // 2, 2)
    staged[...] = (got[...].astype(F32) + kept[...].astype(F32)).astype(BF16)
    send[...] = staged[1 - xbit]
    keep[...] = staged[xbit]


def add_x_kernel(groups, got, kept, *rest):
    outs, staged = rest[:-1], rest[-1]
    g = lax.axis_index("tm") // 4
    staged[...] = (got[...].astype(F32) + kept[...].astype(F32)).astype(BF16)
    for k in range(groups):
        outs[k][...] = staged[lax.bitwise_xor(g, k)]


def sum_kernel(*refs):
    out = refs[-1]
    total = refs[0][...].astype(F32)
    for ref in refs[1:-1]:
        total = total + ref[...].astype(F32)
    out[...] = total.astype(BF16)


def finish_kernel(factor, conv_rows, n_terms, *refs):
    total = refs[0][...].astype(F32)
    for ref in refs[1:n_terms]:
        total = total + ref[...].astype(F32)
    total = (total * factor).astype(BF16)
    refs[n_terms][...] = total[:conv_rows, :]
    for ref in refs[n_terms + 1 :]:
        ref[...] = total[conv_rows:, :]


def swap(x, distance, size):
    return lax.ppermute(x, "tm", [(i, i ^ distance) for i in range(size)])


def shift(x, distance, size):
    return lax.ppermute(x, "tm", [(i, i + distance) for i in range(size) if 0 <= i + distance < size])


def body(signal, conv_weight, res_weight, grad_out, skip_cotangent):
    s_dev, t, width = signal.shape
    gated = res_weight.shape[1]
    near = t // 4
    tm, dp = lax.axis_size("tm"), lax.axis_size("dp")
    slabs, groups = tm // 8, tm // 4
    rows = 2 * width // tm
    res_quarter = 3 * gated // 4
    piece = -(-res_quarter // groups // 16) * 16
    factor = float(s_dev * t * dp * tm) ** (-0.5)

    sig = signal[0]
    grad = grad_out[0]
    skip = skip_cotangent[0]
    tail = sig[t - near :, :]
    far = shift(sig, slabs, tm)
    near_in = shift(tail, 1, tm)
    far_near = shift(tail, slabs + 1, tm)

    deep = rows + piece
    send1, keep1, a, b, outer, ga, x0, p0 = call(
        functools.partial(forward_and_outer_kernel, groups, rows, piece),
        [
            shaped((2, groups, deep, width)), shaped((2, groups, deep, width)),
            shaped((2 * t, gated), F32), shaped((2 * t, gated), F32),
            shaped((2 * t, width)), shaped((t, width), F32),
            shaped((2 * t, width)), shaped((2 * t, width)),
        ],
        sig, near_in, far, far_near, conv_weight, res_weight, grad, skip,
        scratch=[pltpu.VMEM((2, 2, groups, deep, width), BF16)],
        flops=1_300_000_000, nbytes=8_000_000, name="forward_and_outer",
    )
    got1 = swap(send1, 1, tm)
    send0, keep0, own, back, edge = call(
        functools.partial(inner_kernel, groups, rows, near),
        [
            shaped((2, groups, rows, width)), shaped((2, groups, rows, width)),
            shaped((t, width), F32), shaped((t, width)), shaped((2 * near, width)),
        ],
        x0, p0, a, b, outer, ga, conv_weight, res_weight, skip,
        scratch=[pltpu.VMEM((2, 2, groups, rows, width), BF16)],
        flops=1_000_000_000, nbytes=6_000_000, name="inner",
    )
    got0 = swap(send0, 1, tm)

    def reduced(got, kept, depth):
        quarter = (groups, depth, width)
        send, keep = call(
            add_core_kernel, [shaped(quarter)] * 2, got, kept,
            scratch=[pltpu.VMEM((2,) + quarter, BF16)], nbytes=2_000_000, name="add_core",
        )
        got = swap(send, 2, tm)
        pieces = call(
            functools.partial(add_x_kernel, groups), [shaped((depth, width))] * groups, got, keep,
            scratch=[pltpu.VMEM(quarter, BF16)], nbytes=1_000_000, name="add_x",
        )
        terms = [pieces[0]] + [swap(pieces[k], 4 * k, tm) for k in range(1, groups)]
        (total,) = call(sum_kernel, [shaped((depth, width))], *terms, nbytes=500_000, name="add_z")
        others = [
            lax.ppermute(total, "dp", [(i, (i + k) % dp) for i in range(dp)]) for k in range(1, dp)
        ]
        return [total] + others

    sums1 = reduced(got1, keep1, deep)
    sums0 = reduced(got0, keep0, rows)
    conv1, res = call(
        functools.partial(finish_kernel, factor, rows, dp), [shaped((rows, width)), shaped((piece, width))],
        *sums1, nbytes=300_000, name="finish_outer",
    )
    (conv0,) = call(
        functools.partial(finish_kernel, factor, rows, dp), [shaped((rows, width))],
        *sums0, nbytes=300_000, name="finish_inner",
    )
    conv_grad = jnp.stack([conv0, conv1])

    g = lax.axis_index("tm") // 4
    got = jnp.stack([res] + [swap(res, 4 * k, tm) for k in range(1, groups)])
    quarter = got[jnp.bitwise_xor(jnp.arange(groups), g)].reshape(groups * piece, width)[:res_quarter]
    xbit = (lax.axis_index("tm") // 2) % 2
    other = swap(quarter, 2, tm)
    pair = jnp.where(xbit == 0, jnp.stack([quarter, other]), jnp.stack([other, quarter]))
    core = lax.axis_index("tm") % 2
    other = swap(pair, 1, tm)
    both = jnp.where(core == 0, jnp.stack([pair, other]), jnp.stack([other, pair]))
    sets = both.reshape(4, 3, gated // 4, width).transpose(1, 0, 2, 3).reshape(3, gated, width)
    sk = width // 2
    res_grad = jnp.stack([
        jnp.concatenate([sets[1], sets[2][:, sk:]], axis=1),
        jnp.concatenate([sets[0], sets[2][:, :sk]], axis=1),
    ])

    edges = shift(edge, -1, tm)
    back_tail = back[t - near :, :].astype(F32) + edges[near:, :].astype(F32)
    back = jnp.concatenate([back[: t - near, :], back_tail.astype(BF16)], axis=0)
    come = shift(back, -slabs, tm)
    first = own[: t - near, :] + come[: t - near, :].astype(F32)
    last = own[t - near :, :] + come[t - near :, :].astype(F32) + edges[:near, :].astype(F32)
    input_grad = jnp.concatenate([first, last], axis=0).astype(BF16).reshape(s_dev, t, width)
    return (input_grad, conv_grad, res_grad)


def solution(mesh):
    in_specs = (P("dp", "tm", None), P(), P(), P("dp", "tm", None), P("dp", "tm", None))
    out_specs = (P("dp", "tm", None), P(None, "tm", None), P())
    return jax.shard_map(body, mesh=mesh, in_specs=in_specs, out_specs=out_specs, check_vma=False)
```

```python
import functools

import jax
import jax.numpy as jnp
from jax import lax
from jax.experimental import pallas as pl
from jax.experimental.pallas import tpu as pltpu
from jax.sharding import PartitionSpec as P

F32 = jnp.float32
BF16 = jnp.bfloat16


def passed_along(block, axis, distance):
    devices = range(lax.axis_size(axis))
    route = [(i - distance, i) for i in devices if i - distance in devices]
    return lax.ppermute(block, axis, route)


def gate_gradients(dh, z, gated):
    tf = jnp.tanh(z[:, :gated])
    sg = jax.nn.sigmoid(z[:, gated:])
    return jnp.concatenate([dh * sg * (1.0 - tf * tf), dh * tf * sg * (1.0 - sg)], axis=1).astype(
        jnp.bfloat16
    )


def reduce_conv(cat_rows, dz):
    piece = lax.psum_scatter(
        lax.dot_general(cat_rows, dz, (((0,), (0,)), ((), ())), preferred_element_type=jnp.float32),
        "tm",
        scatter_dimension=0,
        tiled=True,
    )
    return lax.psum(piece, "dp")


def general_body(signal, conv_weight, res_weight, grad_out, skip_cotangent):
    s_dev, t_dev, width = signal.shape
    gated = res_weight.shape[1]
    near = t_dev // 4
    slabs = lax.axis_size("tm") // 8
    count_rows = s_dev * t_dev
    factor = float(count_rows * lax.axis_size("dp") * lax.axis_size("tm")) ** (-0.5)

    def delayed(x, layer):
        if layer == 0:
            got = passed_along(x[:, t_dev - near :, :], "tm", 1)
            return jnp.concatenate([got, x[:, : t_dev - near, :]], axis=1)
        return passed_along(x, "tm", slabs)

    def shifted_rows(dpast, layer):
        if layer == 0:
            got = passed_along(dpast[:, :near, :], "tm", -1)
            return jnp.concatenate([dpast[:, near:, :], got], axis=1)
        return passed_along(dpast, "tm", -slabs)

    x = signal
    cats = []
    zvals = []
    hvals = []
    for layer in range(2):
        past = delayed(x, layer)
        cat_rows = jnp.concatenate([past, x], axis=2).reshape(count_rows, 2 * width)
        z = jnp.dot(cat_rows, conv_weight[layer], preferred_element_type=jnp.float32)
        h = (jnp.tanh(z[:, :gated]) * jax.nn.sigmoid(z[:, gated:])).astype(jnp.bfloat16)
        cats.append(cat_rows)
        zvals.append(z)
        hvals.append(h)
        if layer == 0:
            resid = jnp.dot(h, res_weight[0][:, :width], preferred_element_type=jnp.float32)
            x = (
                (x.reshape(count_rows, width).astype(jnp.float32) + resid)
                .astype(jnp.bfloat16)
                .reshape(s_dev, t_dev, width)
            )
    grad = grad_out.reshape(count_rows, width).astype(jnp.float32)
    skip_rows = skip_cotangent.reshape(count_rows, -1)
    conv_parts = [None, None]
    res_parts = [None, None]
    dz_kept = [None, None]
    for layer in (1, 0):
        outer = jnp.concatenate([grad.astype(jnp.bfloat16), skip_rows], axis=1)
        dh = lax.dot_general(
            outer, res_weight[layer], (((1,), (1,)), ((), ())), preferred_element_type=jnp.float32
        )
        dz = gate_gradients(dh, zvals[layer], gated)
        wcat = lax.dot_general(
            dz, conv_weight[layer], (((1,), (1,)), ((), ())), preferred_element_type=jnp.float32
        )
        dpast = wcat[:, :width].astype(jnp.bfloat16).reshape(s_dev, t_dev, width)
        moved = shifted_rows(dpast, layer).reshape(count_rows, width)
        grad = grad + wcat[:, width:] + moved.astype(jnp.float32)
        res_local = lax.dot_general(
            hvals[layer], outer, (((0,), (0,)), ((), ())), preferred_element_type=jnp.float32
        )
        dz_kept[layer] = dz
        res_parts[layer] = res_local
    for layer in range(2):
        conv_parts[layer] = reduce_conv(cats[layer], dz_kept[layer])
    res_total = lax.psum(jnp.stack(res_parts), ("dp", "tm"))
    input_grad = grad.astype(jnp.bfloat16).reshape(s_dev, t_dev, width)
    conv_grad = (jnp.stack(conv_parts) * factor).astype(jnp.bfloat16)
    res_grad = (res_total * factor).astype(jnp.bfloat16)
    return (input_grad, conv_grad, res_grad)


def mm(a, b):
    return jnp.dot(a, b, preferred_element_type=F32)


def mm_nt(a, b):
    return lax.dot_general(a, b, (((1,), (1,)), ((), ())), preferred_element_type=F32)


def mm_tn(a, b):
    return lax.dot_general(a, b, (((0,), (0,)), ((), ())), preferred_element_type=F32)


def shaped(shape, dtype=BF16):
    return jax.ShapeDtypeStruct(shape, dtype)


def call(kernel, outs, *args, after=(), scratch=(), flops=0, nbytes=0, vmem=8, name=None):
    n_args = len(args)

    def run(*refs):
        kernel(*refs[:n_args], *refs[n_args + len(after) :])

    in_vmem = pl.BlockSpec(memory_space=pltpu.VMEM)
    return pl.pallas_call(
        run,
        out_shape=outs,
        in_specs=[in_vmem] * n_args + [pl.BlockSpec(memory_space=pl.ANY)] * len(after),
        out_specs=[in_vmem] * len(outs),
        scratch_shapes=list(scratch),
        compiler_params=pltpu.CompilerParams(vmem_limit_bytes=vmem * 1024 * 1024),
        cost_estimate=pl.CostEstimate(flops=flops, bytes_accessed=nbytes, transcendentals=0),
        name=name,
    )(*args, *after)


def place(tm):
    return tm // 4, lax.rem(tm // 2, 2), lax.rem(tm, 2)


def here():
    return place(lax.axis_index("tm"))


def load_kernel(*refs):
    n = (len(refs) - 1) // 2
    sems = refs[-1]
    copies = [pltpu.make_async_copy(refs[i], refs[n + i], sems.at[i]) for i in range(n)]
    for copy in copies:
        copy.start()
    for copy in copies:
        copy.wait()


def load(*arrays):
    n = len(arrays)
    return pl.pallas_call(
        load_kernel,
        out_shape=[pltpu.VMEM(a.shape, a.dtype) for a in arrays],
        in_specs=[pl.BlockSpec(memory_space=pltpu.HBM)] * n,
        out_specs=[pl.BlockSpec(memory_space=pltpu.VMEM)] * n,
        scratch_shapes=[pltpu.SemaphoreType.DMA((n,))],
        compiler_params=pltpu.CompilerParams(vmem_limit_bytes=8 * 1024 * 1024),
        cost_estimate=pl.CostEstimate(flops=4_000_000_000, bytes_accessed=6_000_000, transcendentals=0),
        name="load",
    )(*[pltpu.with_memory_space_constraint(a, pltpu.HBM) for a in arrays])


def pack_halo_kernel(sig, far, tail4, out):
    t = sig.shape[0]
    near = t // 4
    out[0:near, :] = sig[t - near :, :]
    out[near : 2 * near, :] = far[t - near :, :]
    out[2 * near :, :] = tail4[...]


def inputs_of(sig, far, edge):
    t = sig.shape[0]
    near = t // 4
    _, _, core = here()
    even = core == 0
    near_in = jnp.where(even, edge[near : 2 * near, :], edge[0:near, :])
    far_near = jnp.where(even, edge[2 * near :, :], edge[near : 2 * near, :])
    x0 = jnp.concatenate([sig[...], far[...]], axis=0)
    p0 = jnp.concatenate([near_in, sig[0 : t - near, :], far_near, far[0 : t - near, :]], axis=0)
    return x0, p0


def forward_and_outer_kernel(
    sig, far, edge, cw, rw, grad, skip,
    send, keep, a_out, b_out, x1_out, dz_out, o_out, ga_out,
    staged,
):
    t, width = sig.shape
    gated = rw.shape[1]
    _, _, core = here()
    x0, p0 = inputs_of(sig, far, edge)
    z0 = mm(p0, cw[0, 0:width, :]) + mm(x0, cw[0, width:, :])
    tf = jnp.tanh(z0[:, :gated])
    sg = jax.nn.sigmoid(z0[:, gated:])
    h0 = (tf * sg).astype(BF16)
    a_out[...] = sg * (1.0 - tf * tf)
    b_out[...] = tf * sg * (1.0 - sg)
    x1 = (x0.astype(F32) + mm(h0, rw[0, :, 0:width])).astype(BF16)
    x1_out[...] = x1
    z1 = mm(x1[t:, :], cw[1, 0:width, :]) + mm(x1[:t, :], cw[1, width:, :])
    tf = jnp.tanh(z1[:, :gated])
    sg = jax.nn.sigmoid(z1[:, gated:])
    h1 = (tf * sg).astype(BF16)
    g2 = grad[...]
    sk = skip[...]
    e1 = mm_nt(g2, rw[1, :, 0:width]) + mm_nt(sk, rw[1, :, width:])
    dz1 = jnp.concatenate([e1 * sg * (1.0 - tf * tf), e1 * tf * sg * (1.0 - sg)], axis=1).astype(BF16)
    dz_out[...] = dz1
    dpast = mm_nt(dz1, cw[1, 0:width, :]).astype(BF16)
    ga = g2.astype(F32) + mm_nt(dz1, cw[1, width:, :])
    ga_out[...] = ga
    outer = jnp.concatenate([ga.astype(BF16), dpast], axis=0)
    o_out[...] = outer
    skips = jnp.concatenate([mm_tn(h1, sk), mm_tn(h0[:t, :], sk)], axis=1)
    eighth = gated // 8
    for which, part in enumerate((mm_tn(h1, g2), mm_tn(h0, outer), skips)):
        for c in range(2):
            for q in range(4):
                rows = slice((4 * c + q) * eighth, (4 * c + q + 1) * eighth)
                staged[c, q, which * eighth : (which + 1) * eighth, :] = part[rows, :].astype(BF16)
    send[...] = staged[1 - core]
    keep[...] = staged[core]


def inner_kernel(
    sig, far, edge, a, b, x1, dz1, outer, ga, cw, rw, skip,
    send, keep, own_out, back_out,
    staged,
):
    t, width = sig.shape
    near = t // 4
    _, _, core = here()
    x0, p0 = inputs_of(sig, far, edge)
    e0 = mm_nt(outer[...], rw[0, :, 0:width])
    es = mm_nt(skip[...], rw[0, :, width:])
    e0 = jnp.concatenate([e0[:t, :] + es, e0[t:, :]], axis=0)
    dz0 = jnp.concatenate([e0 * a[...], e0 * b[...]], axis=1).astype(BF16)
    half = width // 16
    rows = 2 * half
    blocks = width // rows
    last = x1[t:, :]
    first = x1[:t, :]
    for base, part0, part1 in (
        (0, mm_tn(p0, dz0), mm_tn(last, dz1[...])),
        (blocks, mm_tn(x0, dz0), mm_tn(first, dz1[...])),
    ):
        for block in range(blocks):
            g, x, c = (base + block) // 4, (base + block) // 2 % 2, (base + block) % 2
            for y in range(2):
                src = slice(block * rows + y * half, block * rows + (y + 1) * half)
                at = (((2 * x + y) * 2 + g % 2) * 2 + g // 2) * rows
                staged[c, at : at + half, :] = part0[src, :].astype(BF16)
                staged[c, at + half : at + rows, :] = part1[src, :].astype(BF16)
    size = staged.shape[1]
    send[0:size, :] = staged[1 - core]
    keep[...] = staged[core]
    wp = mm_nt(dz0, cw[0, 0:width, :]).astype(BF16)
    wx = mm_nt(dz0, cw[0, width:, :])
    zero = jnp.zeros((near, width), F32)
    own_out[...] = ga[...] + wx[:t, :] + jnp.concatenate([wp[near:t, :].astype(F32), zero], axis=0)
    back_out[...] = (
        outer[t:, :].astype(F32) + wx[t:, :] + jnp.concatenate([wp[t + near :, :].astype(F32), zero], axis=0)
    ).astype(BF16)
    send[size : size + near, :] = wp[0:near, :]
    send[size + near :, :] = wp[t : t + near, :]


def total_of(*refs):
    total = refs[0][...].astype(F32)
    for ref in refs[1:]:
        total = total + ref[...].astype(F32)
    return total


def split_quarters(total, mine, by_y, by_x, by_both, staged):
    _, x, _ = here()
    q = 2 * x + lax.axis_index("dp")
    staged[...] = total.reshape(staged.shape)
    mine[...] = staged[q]
    for k, out in ((1, by_y), (2, by_x), (3, by_both)):
        out[...] = staged[lax.bitwise_xor(q, k)].astype(BF16)


def res_quarters_kernel(got, kept, *rest):
    split_quarters(total_of(got, kept), *rest)


def conv_quarters_kernel(got, kept, own, back, mine, by_y, by_x, by_both, own_out, back_out, tail_out, staged):
    size = kept.shape[0]
    split_quarters(got[0:size, :].astype(F32) + kept[...].astype(F32), mine, by_y, by_x, by_both, staged)
    t = own.shape[0]
    near = t // 4
    _, _, core = here()
    edge = got[size : size + near, :].astype(F32)
    deep = got[size + near :, :]
    own_out[0 : t - near, :] = own[0 : t - near, :]
    own_out[t - near :, :] = own[t - near :, :] + jnp.where(core == 0, edge, 0.0)
    back_out[0 : t - near, :] = back[0 : t - near, :]
    back_out[t - near :, :] = (
        back[t - near :, :].astype(F32) + jnp.where(core == 0, deep.astype(F32), edge)
    ).astype(BF16)
    tail_out[...] = jnp.where(core == 0, jnp.zeros_like(deep), deep)


def sum_kernel(*refs):
    refs[-1][...] = total_of(*refs[:-1]).astype(BF16)


def scaled_sum_kernel(factor, *refs):
    refs[-1][...] = (total_of(*refs[:-1]) * factor).astype(BF16)


def halves_kernel(bit, *refs):
    send, keep, staged = refs[-3:]
    g, _, _ = here()
    mine = lax.rem(g // (1 << bit), 2)
    staged[...] = total_of(*refs[:-3]).reshape(staged.shape)
    send[...] = staged[1 - mine].astype(BF16)
    keep[...] = staged[mine]


def in_order_kernel(mine, by_y, by_x, by_both, out):
    _, x, _ = here()
    q = 2 * x + lax.axis_index("dp")
    for k, ref in enumerate((mine, by_y, by_x, by_both)):
        out[lax.bitwise_xor(q, k)] = ref[...]


def finish_kernel(mine, other, res_mine, res_other, conv, res):
    y = lax.axis_index("dp")
    half = mine.shape[0] // 2
    for ref, at in ((mine, y), (other, 1 - y)):
        rows = pl.ds(pl.multiple_of(at * half, half), half)
        conv[0, rows, :] = ref[0:half, :]
        conv[1, rows, :] = ref[half:, :]
    _, _, core = here()
    eighth = res.shape[1] // 8
    width, part = res_mine.shape[2], res_mine.shape[2] // 2
    for ref, c in ((res_mine, core), (res_other, 1 - core)):
        for q in range(4):
            rows = pl.ds(pl.multiple_of((4 * c + q) * eighth, eighth), eighth)
            res[1, rows, 0:width] = ref[q, 0:eighth, :]
            res[0, rows, 0:width] = ref[q, eighth : 2 * eighth, :]
            res[1, rows, width:] = ref[q, 2 * eighth :, 0:part]
            res[0, rows, width:] = ref[q, 2 * eighth :, part:]


def finish_signal_kernel(own, come, come_tail, out, done):
    done[...] = jnp.zeros_like(done)
    t = own.shape[0]
    near = come_tail.shape[0]
    out[0 : t - near, :] = (own[0 : t - near, :] + come[0 : t - near, :].astype(F32)).astype(BF16)
    out[t - near :, :] = total_of(own.at[t - near :, :], come.at[t - near :, :], come_tail).astype(BF16)


def swap(x, distance):
    return lax.ppermute(x, "tm", [(i, i ^ distance) for i in range(16)])


def swap_streams(x):
    return lax.ppermute(x, "dp", [(0, 1), (1, 0)])


def swap_both(x, distance):
    route = [(16 * y + i, 16 * (1 - y) + (i ^ distance)) for y in range(2) for i in range(16)]
    return lax.ppermute(x, ("dp", "tm"), route)


def shift(x, distance):
    return lax.ppermute(x, "tm", [(i, i + distance) for i in range(16) if 0 <= i + distance < 16])


def body(signal, conv_weight, res_weight, grad_out, skip_cotangent):
    s_dev, t, width = signal.shape
    gated = res_weight.shape[1]
    near = t // 4
    half = width // 16
    res_rows = 3 * gated // 8
    factor = float(s_dev * t * 32) ** (-0.5)

    sig = signal[0]
    far = shift(sig, 2)
    tail4 = shift(sig[t - near :, :], 4)
    cw, rw, sig, grad, skip = load(conv_weight, res_weight, sig, grad_out[0], skip_cotangent[0])
    (edge_in,) = call(pack_halo_kernel, [shaped((3 * near, width))], sig, far, tail4, name="pack_halo")
    edge_in = swap(edge_in, 1)

    rsend, rkeep, a, b, x1, dz1, outer, ga = call(
        forward_and_outer_kernel,
        [
            shaped((4, res_rows, width)), shaped((4, res_rows, width)),
            shaped((2 * t, gated), F32), shaped((2 * t, gated), F32), shaped((2 * t, width)),
            shaped((t, width)), shaped((2 * t, width)), shaped((t, width), F32),
        ],
        sig, far, edge_in, cw, rw, grad, skip,
        scratch=[pltpu.VMEM((2, 4, res_rows, width), BF16)], vmem=12, name="forward_and_outer",
    )
    rgot = swap(rsend, 1)
    size = 16 * 2 * half
    csend, ckeep, own, back = call(
        inner_kernel,
        [
            shaped((size + 2 * near, width)), shaped((size, width)), shaped((t, width), F32), shaped((t, width)),
        ],
        sig, far, edge_in, a, b, x1, dz1, outer, ga, cw, rw, skip,
        scratch=[pltpu.VMEM((2, size, width), BF16)], vmem=12, flops=2_000_000_000, name="inner",
    )
    cgot = swap(csend, 1)

    def around(by_y, by_x, by_both):
        return swap_streams(by_y), swap(by_x, 2), swap_both(by_both, 2)

    def halves(bit, shape, terms, after, name):
        return call(
            functools.partial(halves_kernel, bit), [shaped(shape[1:]), shaped(shape[1:], F32)], *terms,
            after=after, scratch=[pltpu.VMEM(shape, F32)], name=name,
        )

    res = shaped((res_rows, width))
    rmine, *rsend = call(
        res_quarters_kernel, [shaped((res_rows, width), F32), res, res, res], rgot, rkeep,
        after=(csend,), scratch=[pltpu.VMEM((4, res_rows, width), F32)], name="res_quarters",
    )
    rterms = (rmine,) + around(*rsend)
    part = shaped((size // 4, width))
    cmine, by_y, by_x, by_both, own, back, tail = call(
        conv_quarters_kernel,
        [shaped(part.shape, F32), part, part, part, shaped((t, width), F32), shaped((t, width)), shaped((near, width))],
        cgot, ckeep, own, back,
        after=(rmine,), scratch=[pltpu.VMEM((4, size // 4, width), F32)], name="conv_quarters",
    )
    cterms = (cmine,) + around(by_y, by_x, by_both)
    come = shift(back, -2)
    come_tail = shift(tail, -4)
    (rsum,) = call(sum_kernel, [res], *rterms, after=(cmine,), name="res_sum_xy")
    rgot = swap(rsum, 4)
    (rsum,) = call(sum_kernel, [res], rsum, rgot, name="res_sum_z1")
    rgot = swap(rsum, 8)
    csend, ckeep = halves(0, (2, 4 * half, width), cterms, (rsum, come, come_tail), "conv_z1")
    cgot = swap(csend, 4)
    (quarter,) = call(
        functools.partial(scaled_sum_kernel, factor), [res], rsum, rgot, after=(csend,), name="res_sum_z2"
    )
    rparts = (quarter,) + around(quarter, quarter, quarter)
    csend, ckeep = halves(1, (2, 2 * half, width), (ckeep, cgot), (quarter,), "conv_z2")
    cgot = swap(csend, 8)
    (ordered,) = call(in_order_kernel, [shaped((4, res_rows, width))], *rparts, after=(csend,), name="res_in_order")
    rgot = swap(ordered, 1)
    input_grad, done = call(
        finish_signal_kernel, [shaped((t, width)), shaped((8, 128), F32)], own, come, come_tail,
        after=(csend,), name="finish_signal",
    )
    (mine,) = call(
        functools.partial(scaled_sum_kernel, factor), [shaped((2 * half, width))], ckeep, cgot,
        after=(ordered, done), name="conv_scaled",
    )
    other = swap_streams(mine)
    conv_grad, res_grad = call(
        finish_kernel, [shaped((2, 2 * half, width)), shaped(res_weight.shape)], mine, other, ordered, rgot,
        name="finish",
    )
    return (input_grad.reshape(s_dev, t, width), conv_grad, res_grad)


def solution(mesh):
    in_specs = (P("dp", "tm", None), P(), P(), P("dp", "tm", None), P("dp", "tm", None))
    out_specs = (P("dp", "tm", None), P(None, "tm", None), P())
    chosen = body if mesh.shape["dp"] == 2 and mesh.shape["tm"] == 16 else general_body
    return jax.shard_map(chosen, mesh=mesh, in_specs=in_specs, out_specs=out_specs, check_vma=False)
```

```python
import functools

import jax
import jax.numpy as jnp
from jax import lax
from jax.experimental import pallas as pl
from jax.experimental.pallas import tpu as pltpu
from jax.sharding import PartitionSpec as P

F32 = jnp.float32
BF16 = jnp.bfloat16


def passed_along(block, axis, distance):
    devices = range(lax.axis_size(axis))
    route = [(i - distance, i) for i in devices if i - distance in devices]
    return lax.ppermute(block, axis, route)


def gate_gradients(dh, z, gated):
    tf = jnp.tanh(z[:, :gated])
    sg = jax.nn.sigmoid(z[:, gated:])
    return jnp.concatenate([dh * sg * (1.0 - tf * tf), dh * tf * sg * (1.0 - sg)], axis=1).astype(
        jnp.bfloat16
    )


def reduce_conv(cat_rows, dz):
    piece = lax.psum_scatter(
        lax.dot_general(cat_rows, dz, (((0,), (0,)), ((), ())), preferred_element_type=jnp.float32),
        "tm",
        scatter_dimension=0,
        tiled=True,
    )
    return lax.psum(piece, "dp")


def general_body(signal, conv_weight, res_weight, grad_out, skip_cotangent):
    s_dev, t_dev, width = signal.shape
    gated = res_weight.shape[1]
    near = t_dev // 4
    slabs = lax.axis_size("tm") // 8
    count_rows = s_dev * t_dev
    factor = float(count_rows * lax.axis_size("dp") * lax.axis_size("tm")) ** (-0.5)

    def delayed(x, layer):
        if layer == 0:
            got = passed_along(x[:, t_dev - near :, :], "tm", 1)
            return jnp.concatenate([got, x[:, : t_dev - near, :]], axis=1)
        return passed_along(x, "tm", slabs)

    def shifted_rows(dpast, layer):
        if layer == 0:
            got = passed_along(dpast[:, :near, :], "tm", -1)
            return jnp.concatenate([dpast[:, near:, :], got], axis=1)
        return passed_along(dpast, "tm", -slabs)

    x = signal
    cats = []
    zvals = []
    hvals = []
    for layer in range(2):
        past = delayed(x, layer)
        cat_rows = jnp.concatenate([past, x], axis=2).reshape(count_rows, 2 * width)
        z = jnp.dot(cat_rows, conv_weight[layer], preferred_element_type=jnp.float32)
        h = (jnp.tanh(z[:, :gated]) * jax.nn.sigmoid(z[:, gated:])).astype(jnp.bfloat16)
        cats.append(cat_rows)
        zvals.append(z)
        hvals.append(h)
        if layer == 0:
            resid = jnp.dot(h, res_weight[0][:, :width], preferred_element_type=jnp.float32)
            x = (
                (x.reshape(count_rows, width).astype(jnp.float32) + resid)
                .astype(jnp.bfloat16)
                .reshape(s_dev, t_dev, width)
            )
    grad = grad_out.reshape(count_rows, width).astype(jnp.float32)
    skip_rows = skip_cotangent.reshape(count_rows, -1)
    conv_parts = [None, None]
    res_parts = [None, None]
    dz_kept = [None, None]
    for layer in (1, 0):
        outer = jnp.concatenate([grad.astype(jnp.bfloat16), skip_rows], axis=1)
        dh = lax.dot_general(
            outer, res_weight[layer], (((1,), (1,)), ((), ())), preferred_element_type=jnp.float32
        )
        dz = gate_gradients(dh, zvals[layer], gated)
        wcat = lax.dot_general(
            dz, conv_weight[layer], (((1,), (1,)), ((), ())), preferred_element_type=jnp.float32
        )
        dpast = wcat[:, :width].astype(jnp.bfloat16).reshape(s_dev, t_dev, width)
        moved = shifted_rows(dpast, layer).reshape(count_rows, width)
        grad = grad + wcat[:, width:] + moved.astype(jnp.float32)
        res_local = lax.dot_general(
            hvals[layer], outer, (((0,), (0,)), ((), ())), preferred_element_type=jnp.float32
        )
        dz_kept[layer] = dz
        res_parts[layer] = res_local
    for layer in range(2):
        conv_parts[layer] = reduce_conv(cats[layer], dz_kept[layer])
    res_total = lax.psum(jnp.stack(res_parts), ("dp", "tm"))
    input_grad = grad.astype(jnp.bfloat16).reshape(s_dev, t_dev, width)
    conv_grad = (jnp.stack(conv_parts) * factor).astype(jnp.bfloat16)
    res_grad = (res_total * factor).astype(jnp.bfloat16)
    return (input_grad, conv_grad, res_grad)


def mm(a, b):
    return jnp.dot(a, b, preferred_element_type=F32)


def mm_nt(a, b):
    return lax.dot_general(a, b, (((1,), (1,)), ((), ())), preferred_element_type=F32)


def mm_tn(a, b):
    return lax.dot_general(a, b, (((0,), (0,)), ((), ())), preferred_element_type=F32)


def shaped(shape, dtype=BF16):
    return jax.ShapeDtypeStruct(shape, dtype)


def call(kernel, outs, *args, after=(), scratch=(), flops=0, nbytes=0, vmem=8, name=None):
    n_args = len(args)

    def run(*refs):
        kernel(*refs[:n_args], *refs[n_args + len(after) :])

    in_vmem = pl.BlockSpec(memory_space=pltpu.VMEM)
    return pl.pallas_call(
        run,
        out_shape=outs,
        in_specs=[in_vmem] * n_args + [pl.BlockSpec(memory_space=pl.ANY)] * len(after),
        out_specs=[in_vmem] * len(outs),
        scratch_shapes=list(scratch),
        compiler_params=pltpu.CompilerParams(vmem_limit_bytes=vmem * 1024 * 1024),
        cost_estimate=pl.CostEstimate(flops=flops, bytes_accessed=nbytes, transcendentals=0),
        name=name,
    )(*args, *after)


def place(tm):
    return tm // 4, lax.rem(tm // 2, 2), lax.rem(tm, 2)


def here():
    return place(lax.axis_index("tm"))


def load_kernel(cw, rw, sig, grad, skip, cw_out, rw_out, own_out, tail_out, sems):
    t, width = sig.shape
    near = tail_out.shape[0]
    pairs = (
        (sig.at[t - near :, :], tail_out),
        (sig, own_out.at[:, 0:width]),
        (grad, own_out.at[:, width : 2 * width]),
        (skip, own_out.at[:, 2 * width :]),
        (cw, cw_out),
        (rw, rw_out),
    )
    copies = [pltpu.make_async_copy(src, dst, sems.at[i]) for i, (src, dst) in enumerate(pairs)]
    for copy in copies:
        copy.start()
    for copy in copies:
        copy.wait()


def load(cw, rw, sig, grad, skip):
    t, width = sig.shape
    in_hbm = [pltpu.with_memory_space_constraint(a, pltpu.HBM) for a in (cw, rw, sig, grad, skip)]
    return pl.pallas_call(
        load_kernel,
        out_shape=[
            pltpu.VMEM(cw.shape, BF16), pltpu.VMEM(rw.shape, BF16),
            pltpu.VMEM((t, 2 * width + skip.shape[1]), BF16), pltpu.VMEM((t // 4, width), BF16),
        ],
        in_specs=[pl.BlockSpec(memory_space=pltpu.HBM)] * 5,
        out_specs=[pl.BlockSpec(memory_space=pltpu.VMEM)] * 4,
        scratch_shapes=[pltpu.SemaphoreType.DMA((6,))],
        compiler_params=pltpu.CompilerParams(vmem_limit_bytes=8 * 1024 * 1024),
        cost_estimate=pl.CostEstimate(flops=4_000_000_000, bytes_accessed=6_000_000, transcendentals=0),
        name="load",
    )(*in_hbm)


def pack_halo_kernel(far, tail4, out):
    t = far.shape[0]
    out[0:t, :] = far[...]
    out[t:, :] = tail4[...]


def split_quarters(staged, mine, by_y, by_x, by_both):
    _, x, core = here()
    q = 2 * x + lax.axis_index("dp")
    mine[...] = staged[core, q]
    for k, out in ((1, by_y), (2, by_x), (3, by_both)):
        out[...] = staged[core, lax.bitwise_xor(q, k)]


def forward_and_outer_kernel(
    own, own_other, halo, halo_other, cw, rw,
    mine, by_y, by_x, by_both, x_out, a_out, b_out, x1_out, dz_out, o_out, ga_out, es_out,
    staged, gin, skin,
):
    t = own.shape[0]
    near = t // 4
    width = x_out.shape[1]
    gated = rw.shape[1]
    _, _, core = here()
    for a, h, c in ((own, halo, core), (own_other, halo_other, 1 - core)):
        rows = pl.ds(pl.multiple_of(c * t, t), t)
        x_out[pl.ds(pl.multiple_of(near + c * t, near), t), :] = h[0:t, :]
        x_out[pl.ds(pl.multiple_of(near + (2 + c) * t, near), t), :] = a[:, 0:width]
        gin[rows, :] = a[:, width : 2 * width]
        skin[rows, :] = a[:, 2 * width :]
    x_out[0:near, :] = jnp.where(core == 1, halo[t:, :], halo_other[t:, :])
    x0 = x_out[near:, :]
    z0 = mm(x_out[0 : 4 * t, :], cw[0, 0:width, :]) + mm(x0, cw[0, width:, :])
    tf = jnp.tanh(z0[:, :gated])
    sg = jax.nn.sigmoid(z0[:, gated:])
    h0 = (tf * sg).astype(BF16)
    a_out[...] = sg * (1.0 - tf * tf)
    b_out[...] = tf * sg * (1.0 - sg)
    x1 = (x0.astype(F32) + mm(h0, rw[0, :, 0:width])).astype(BF16)
    x1_out[...] = x1
    z1 = mm(x1[0 : 2 * t, :], cw[1, 0:width, :]) + mm(x1[2 * t :, :], cw[1, width:, :])
    tf = jnp.tanh(z1[:, :gated])
    sg = jax.nn.sigmoid(z1[:, gated:])
    h1 = (tf * sg).astype(BF16)
    g2 = gin[...]
    sk = skin[...]
    e1 = mm_nt(g2, rw[1, :, 0:width]) + mm_nt(sk, rw[1, :, width:])
    dz1 = jnp.concatenate([e1 * sg * (1.0 - tf * tf), e1 * tf * sg * (1.0 - sg)], axis=1).astype(BF16)
    dz_out[...] = dz1
    dpast = mm_nt(dz1, cw[1, 0:width, :]).astype(BF16)
    ga = g2.astype(F32) + mm_nt(dz1, cw[1, width:, :])
    ga_out[...] = ga
    outer = jnp.concatenate([dpast, ga.astype(BF16)], axis=0)
    o_out[...] = outer
    es_out[...] = mm_nt(sk, rw[0, :, width:])
    skips = jnp.concatenate([mm_tn(h1, sk), mm_tn(h0[2 * t :, :], sk)], axis=1)
    eighth = gated // 8
    for which, part in enumerate((mm_tn(h1, g2), mm_tn(h0, outer), skips)):
        for c in range(2):
            for q in range(4):
                rows = slice((4 * c + q) * eighth, (4 * c + q + 1) * eighth)
                staged[c, q, which * eighth : (which + 1) * eighth, :] = part[rows, :].astype(BF16)
    split_quarters(staged, mine, by_y, by_x, by_both)


def inner_kernel(
    xin, a, b, x1, dz1, outer, ga, es, cw, rw,
    mine, by_y, by_x, by_both, own_out, back_out, tail_out,
    staged, dz,
):
    width = xin.shape[1]
    t = dz1.shape[0] // 2
    near = t // 4
    _, _, core = here()
    e0 = mm_nt(outer[...], rw[0, :, 0:width])
    e0 = jnp.concatenate([e0[: 2 * t, :], e0[2 * t :, :] + es[...]], axis=0)
    dz0 = jnp.concatenate([e0 * a[...], e0 * b[...]], axis=1).astype(BF16)
    dz[0 : 4 * t, :] = dz0
    dz[4 * t :, :] = jnp.zeros((near, width), BF16)
    half = width // 16
    rows = 2 * half
    blocks = width // rows
    for base, part0, part1 in (
        (0, mm_tn(xin[0 : 4 * t, :], dz0), mm_tn(x1[0 : 2 * t, :], dz1[...])),
        (blocks, mm_tn(xin[near:, :], dz0), mm_tn(x1[2 * t :, :], dz1[...])),
    ):
        for block in range(blocks):
            g, x, c = (base + block) // 4, (base + block) // 2 % 2, (base + block) % 2
            for y in range(2):
                src = slice(block * rows + y * half, block * rows + (y + 1) * half)
                staged[c, 2 * x + y, g, 0:half, :] = part0[src, :].astype(BF16)
                staged[c, 2 * x + y, g, half:, :] = part1[src, :].astype(BF16)
    split_quarters(staged, mine, by_y, by_x, by_both)
    at = pl.multiple_of(core * t, t)
    long = t + near
    back = dz[pl.ds(at, long), :]
    here_dz = dz[pl.ds(2 * t + at, long), :]
    both = jnp.concatenate([back, here_dz], axis=0)
    wp = mm_nt(both, cw[0, 0:width, :]).astype(BF16)
    wx = mm_nt(both, cw[0, width:, :])
    back_out[...] = (outer[pl.ds(at, t), :].astype(F32) + wx[0:t, :] + wp[near:long, :].astype(F32)).astype(BF16)
    own_out[...] = ga[pl.ds(at, t), :] + wx[long : long + t, :] + wp[long + near :, :].astype(F32)
    tail_out[...] = wp[0:near, :]


def total_of(*refs):
    total = refs[0][...].astype(F32)
    for ref in refs[1:]:
        total = total + ref[...].astype(F32)
    return total


def sum_kernel(*refs):
    refs[-1][...] = total_of(*refs[:-1]).astype(BF16)


def scaled_sum_kernel(factor, *refs):
    refs[-1][...] = (total_of(*refs[:-1]) * factor).astype(BF16)


def groups_kernel(mine, by_y, by_x, by_both, keep, send1, send2, send3, staged):
    g, _, _ = here()
    staged[...] = total_of(mine, by_y, by_x, by_both)
    keep[...] = staged[g]
    for k, out in ((1, send1), (2, send2), (3, send3)):
        out[...] = staged[lax.bitwise_xor(g, k)].astype(BF16)


def in_order_kernel(mine, by_y, by_x, by_both, out):
    _, x, _ = here()
    q = 2 * x + lax.axis_index("dp")
    for k, ref in enumerate((mine, by_y, by_x, by_both)):
        out[lax.bitwise_xor(q, k)] = ref[...]


def finish_kernel(mine, other, res_mine, res_other, conv, res):
    y = lax.axis_index("dp")
    half = mine.shape[0] // 2
    for ref, at in ((mine, y), (other, 1 - y)):
        rows = pl.ds(pl.multiple_of(at * half, half), half)
        conv[0, rows, :] = ref[0:half, :]
        conv[1, rows, :] = ref[half:, :]
    _, _, core = here()
    eighth = res.shape[1] // 8
    width, part = res_mine.shape[2], res_mine.shape[2] // 2
    for ref, c in ((res_mine, core), (res_other, 1 - core)):
        for q in range(4):
            rows = pl.ds(pl.multiple_of((4 * c + q) * eighth, eighth), eighth)
            res[1, rows, 0:width] = ref[q, 0:eighth, :]
            res[0, rows, 0:width] = ref[q, eighth : 2 * eighth, :]
            res[1, rows, width:] = ref[q, 2 * eighth :, 0:part]
            res[0, rows, width:] = ref[q, 2 * eighth :, part:]


def finish_signal_kernel(own, come, come_tail, out, done):
    done[...] = jnp.zeros_like(done)
    t = own.shape[0]
    near = come_tail.shape[0]
    out[0 : t - near, :] = (own[0 : t - near, :] + come[0 : t - near, :].astype(F32)).astype(BF16)
    out[t - near :, :] = total_of(own.at[t - near :, :], come.at[t - near :, :], come_tail).astype(BF16)


def swap(x, distance):
    return lax.ppermute(x, "tm", [(i, i ^ distance) for i in range(16)])


def swap_streams(x):
    return lax.ppermute(x, "dp", [(0, 1), (1, 0)])


def swap_both(x, distance):
    route = [(16 * y + i, 16 * (1 - y) + (i ^ distance)) for y in range(2) for i in range(16)]
    return lax.ppermute(x, ("dp", "tm"), route)


def shift(x, distance):
    return lax.ppermute(x, "tm", [(i, i + distance) for i in range(16) if 0 <= i + distance < 16])


def body(signal, conv_weight, res_weight, grad_out, skip_cotangent):
    s_dev, t, width = signal.shape
    gated = res_weight.shape[1]
    near = t // 4
    half = width // 16
    res_rows = 3 * gated // 8
    factor = float(s_dev * t * 32) ** (-0.5)

    far = shift(signal[0], 2)
    cw, rw, own, tail = load(conv_weight, res_weight, signal[0], grad_out[0], skip_cotangent[0])
    own_other = swap(own, 1)
    tail4 = shift(tail, 4)
    (halo,) = call(pack_halo_kernel, [shaped((t + near, width))], far, tail4, name="pack_halo")
    halo_other = swap(halo, 1)

    res = shaped((res_rows, width))
    *rsplit, xin, a, b, x1, dz1, outer, ga, es = call(
        forward_and_outer_kernel,
        [
            res, res, res, res,
            shaped((4 * t + near, width)), shaped((4 * t, gated), F32), shaped((4 * t, gated), F32),
            shaped((4 * t, width)), shaped((2 * t, width)), shaped((4 * t, width)), shaped((2 * t, width), F32),
            shaped((2 * t, gated), F32),
        ],
        own, own_other, halo, halo_other, cw, rw,
        scratch=[
            pltpu.VMEM((2, 4, res_rows, width), BF16), pltpu.VMEM((2 * t, width), BF16),
            pltpu.VMEM((2 * t, gated), BF16),
        ],
        vmem=16, name="forward_and_outer",
    )
    piece = (2 * half, width)
    part = shaped((4,) + piece)
    *csplit, own, back, tail = call(
        inner_kernel,
        [part, part, part, part, shaped((t, width), F32), shaped((t, width)), shaped((near, width))],
        xin, a, b, x1, dz1, outer, ga, es, cw, rw,
        scratch=[pltpu.VMEM((2, 4, 4) + piece, BF16), pltpu.VMEM((4 * t + near, width), BF16)],
        vmem=16, flops=2_000_000_000, name="inner",
    )

    def around(by_y, by_x, by_both):
        return swap_streams(by_y), swap(by_x, 2), swap_both(by_both, 2)

    rterms = (rsplit[0],) + around(*rsplit[1:])
    cterms = (csplit[0],) + around(*csplit[1:])
    come = shift(back, -2)
    come_tail = lax.ppermute(tail, "tm", [(i, i - 3) for i in range(4, 16, 2)])
    (rsum,) = call(sum_kernel, [res], *rterms, after=(csplit[0],), name="res_sum_xy")
    rgot = swap(rsum, 4)
    (rsum,) = call(sum_kernel, [res], rsum, rgot, name="res_sum_z1")
    rgot = swap(rsum, 8)
    ckeep, *csend = call(
        groups_kernel, [shaped(piece, F32)] + [shaped(piece)] * 3, *cterms,
        after=(rsum,), scratch=[pltpu.VMEM((4,) + piece, F32)], name="conv_groups",
    )
    cgot = [swap(send, 4 * k) for k, send in zip((1, 2, 3), csend)]
    input_grad, done = call(
        finish_signal_kernel, [shaped((t, width)), shaped((8, 128), F32)], own, come, come_tail,
        after=(ckeep,), name="finish_signal",
    )
    (quarter,) = call(
        functools.partial(scaled_sum_kernel, factor), [res], rsum, rgot, after=(ckeep,), name="res_sum_z2"
    )
    rparts = (quarter,) + around(quarter, quarter, quarter)
    (mine,) = call(
        functools.partial(scaled_sum_kernel, factor), [shaped(piece)], ckeep, *cgot,
        after=(quarter,), name="conv_scaled",
    )
    other = swap_streams(mine)
    (ordered,) = call(in_order_kernel, [shaped((4, res_rows, width))], *rparts, after=(mine, done), name="res_in_order")
    rgot = swap(ordered, 1)
    conv_grad, res_grad = call(
        finish_kernel, [shaped((2,) + piece), shaped(res_weight.shape)], mine, other, ordered, rgot,
        name="finish",
    )
    return (input_grad.reshape(s_dev, t, width), conv_grad, res_grad)


def solution(mesh):
    in_specs = (P("dp", "tm", None), P(), P(), P("dp", "tm", None), P("dp", "tm", None))
    out_specs = (P("dp", "tm", None), P(None, "tm", None), P())
    chosen = body if mesh.shape["dp"] == 2 and mesh.shape["tm"] == 16 else general_body
    return jax.shard_map(chosen, mesh=mesh, in_specs=in_specs, out_specs=out_specs, check_vma=False)
```

```python
import functools

import jax
import jax.numpy as jnp
from jax import lax
from jax.experimental import pallas as pl
from jax.experimental.pallas import tpu as pltpu
from jax.sharding import PartitionSpec as P

F32 = jnp.float32
BF16 = jnp.bfloat16


def passed_along(block, axis, distance):
    devices = range(lax.axis_size(axis))
    route = [(i - distance, i) for i in devices if i - distance in devices]
    return lax.ppermute(block, axis, route)


def gate_gradients(dh, z, gated):
    tf = jnp.tanh(z[:, :gated])
    sg = jax.nn.sigmoid(z[:, gated:])
    return jnp.concatenate([dh * sg * (1.0 - tf * tf), dh * tf * sg * (1.0 - sg)], axis=1).astype(
        jnp.bfloat16
    )


def reduce_conv(cat_rows, dz):
    piece = lax.psum_scatter(
        lax.dot_general(cat_rows, dz, (((0,), (0,)), ((), ())), preferred_element_type=jnp.float32),
        "tm",
        scatter_dimension=0,
        tiled=True,
    )
    return lax.psum(piece, "dp")


def general_body(signal, conv_weight, res_weight, grad_out, skip_cotangent):
    s_dev, t_dev, width = signal.shape
    gated = res_weight.shape[1]
    near = t_dev // 4
    slabs = lax.axis_size("tm") // 8
    count_rows = s_dev * t_dev
    factor = float(count_rows * lax.axis_size("dp") * lax.axis_size("tm")) ** (-0.5)

    def delayed(x, layer):
        if layer == 0:
            got = passed_along(x[:, t_dev - near :, :], "tm", 1)
            return jnp.concatenate([got, x[:, : t_dev - near, :]], axis=1)
        return passed_along(x, "tm", slabs)

    def shifted_rows(dpast, layer):
        if layer == 0:
            got = passed_along(dpast[:, :near, :], "tm", -1)
            return jnp.concatenate([dpast[:, near:, :], got], axis=1)
        return passed_along(dpast, "tm", -slabs)

    x = signal
    cats = []
    zvals = []
    hvals = []
    for layer in range(2):
        past = delayed(x, layer)
        cat_rows = jnp.concatenate([past, x], axis=2).reshape(count_rows, 2 * width)
        z = jnp.dot(cat_rows, conv_weight[layer], preferred_element_type=jnp.float32)
        h = (jnp.tanh(z[:, :gated]) * jax.nn.sigmoid(z[:, gated:])).astype(jnp.bfloat16)
        cats.append(cat_rows)
        zvals.append(z)
        hvals.append(h)
        if layer == 0:
            resid = jnp.dot(h, res_weight[0][:, :width], preferred_element_type=jnp.float32)
            x = (
                (x.reshape(count_rows, width).astype(jnp.float32) + resid)
                .astype(jnp.bfloat16)
                .reshape(s_dev, t_dev, width)
            )
    grad = grad_out.reshape(count_rows, width).astype(jnp.float32)
    skip_rows = skip_cotangent.reshape(count_rows, -1)
    conv_parts = [None, None]
    res_parts = [None, None]
    dz_kept = [None, None]
    for layer in (1, 0):
        outer = jnp.concatenate([grad.astype(jnp.bfloat16), skip_rows], axis=1)
        dh = lax.dot_general(
            outer, res_weight[layer], (((1,), (1,)), ((), ())), preferred_element_type=jnp.float32
        )
        dz = gate_gradients(dh, zvals[layer], gated)
        wcat = lax.dot_general(
            dz, conv_weight[layer], (((1,), (1,)), ((), ())), preferred_element_type=jnp.float32
        )
        dpast = wcat[:, :width].astype(jnp.bfloat16).reshape(s_dev, t_dev, width)
        moved = shifted_rows(dpast, layer).reshape(count_rows, width)
        grad = grad + wcat[:, width:] + moved.astype(jnp.float32)
        res_local = lax.dot_general(
            hvals[layer], outer, (((0,), (0,)), ((), ())), preferred_element_type=jnp.float32
        )
        dz_kept[layer] = dz
        res_parts[layer] = res_local
    for layer in range(2):
        conv_parts[layer] = reduce_conv(cats[layer], dz_kept[layer])
    res_total = lax.psum(jnp.stack(res_parts), ("dp", "tm"))
    input_grad = grad.astype(jnp.bfloat16).reshape(s_dev, t_dev, width)
    conv_grad = (jnp.stack(conv_parts) * factor).astype(jnp.bfloat16)
    res_grad = (res_total * factor).astype(jnp.bfloat16)
    return (input_grad, conv_grad, res_grad)


def mm(a, b):
    return jnp.dot(a, b, preferred_element_type=F32)


def mm_nt(a, b):
    return lax.dot_general(a, b, (((1,), (1,)), ((), ())), preferred_element_type=F32)


def mm_tn(a, b):
    return lax.dot_general(a, b, (((0,), (0,)), ((), ())), preferred_element_type=F32)


def shaped(shape, dtype=BF16):
    return jax.ShapeDtypeStruct(shape, dtype)


def call(kernel, outs, *args, after=(), scratch=(), flops=0, nbytes=0, vmem=8, name=None):
    n_args = len(args)

    def run(*refs):
        kernel(*refs[:n_args], *refs[n_args + len(after) :])

    in_vmem = pl.BlockSpec(memory_space=pltpu.VMEM)
    return pl.pallas_call(
        run,
        out_shape=outs,
        in_specs=[in_vmem] * n_args + [pl.BlockSpec(memory_space=pl.ANY)] * len(after),
        out_specs=[in_vmem] * len(outs),
        scratch_shapes=list(scratch),
        compiler_params=pltpu.CompilerParams(vmem_limit_bytes=vmem * 1024 * 1024),
        cost_estimate=pl.CostEstimate(flops=flops, bytes_accessed=nbytes, transcendentals=0),
        name=name,
    )(*args, *after)


def place(tm):
    return tm // 4, lax.rem(tm // 2, 2), lax.rem(tm, 2)


def here():
    return place(lax.axis_index("tm"))


def load_kernel(cw, rw, sig, grad, skip, cw_out, rw_out, own_out, sems):
    width = sig.shape[1]
    pairs = (
        (sig, own_out.at[:, 0:width]),
        (grad, own_out.at[:, width : 2 * width]),
        (skip, own_out.at[:, 2 * width :]),
        (cw, cw_out),
        (rw, rw_out),
    )
    copies = [pltpu.make_async_copy(src, dst, sems.at[i]) for i, (src, dst) in enumerate(pairs)]
    for copy in copies:
        copy.start()
    for copy in copies:
        copy.wait()


def load(cw, rw, sig, grad, skip):
    t, width = sig.shape
    in_hbm = [pltpu.with_memory_space_constraint(a, pltpu.HBM) for a in (cw, rw, sig, grad, skip)]
    return pl.pallas_call(
        load_kernel,
        out_shape=[
            pltpu.VMEM(cw.shape, BF16), pltpu.VMEM(rw.shape, BF16),
            pltpu.VMEM((t, 2 * width + skip.shape[1]), BF16),
        ],
        in_specs=[pl.BlockSpec(memory_space=pltpu.HBM)] * 5,
        out_specs=[pl.BlockSpec(memory_space=pltpu.VMEM)] * 3,
        scratch_shapes=[pltpu.SemaphoreType.DMA((5,))],
        compiler_params=pltpu.CompilerParams(vmem_limit_bytes=8 * 1024 * 1024),
        cost_estimate=pl.CostEstimate(flops=4_000_000_000, bytes_accessed=6_000_000, transcendentals=0),
        name="load",
    )(*in_hbm)


def pack_halo_kernel(far, tail4, out):
    t = far.shape[0]
    slab = lax.axis_index("tm")
    out[0:t, :] = jnp.where(slab >= 2, far[...], jnp.zeros_like(far))
    out[t:, :] = jnp.where(slab >= 4, tail4[...], jnp.zeros_like(tail4))


def split_quarters(staged, mine, by_y, by_x, by_both):
    _, x, core = here()
    q = 2 * x + lax.axis_index("dp")
    mine[...] = staged[core, q]
    for k, out in ((1, by_y), (2, by_x), (3, by_both)):
        out[...] = staged[core, lax.bitwise_xor(q, k)]


def forward_and_outer_kernel(
    own, own_other, halo, halo_other, cw, rw,
    mine, by_y, by_x, by_both, x_out, a_out, b_out, x1_out, dz_out, o_out, ga_out, es_out,
    staged, gin, skin,
):
    t = own.shape[0]
    near = t // 4
    width = x_out.shape[1]
    gated = rw.shape[1]
    _, _, core = here()
    for a, h, c in ((own, halo, core), (own_other, halo_other, 1 - core)):
        rows = pl.ds(pl.multiple_of(c * t, t), t)
        x_out[pl.ds(pl.multiple_of(near + c * t, near), t), :] = h[0:t, :]
        x_out[pl.ds(pl.multiple_of(near + (2 + c) * t, near), t), :] = a[:, 0:width]
        gin[rows, :] = a[:, width : 2 * width]
        skin[rows, :] = a[:, 2 * width :]
    x_out[0:near, :] = jnp.where(core == 1, halo[t:, :], halo_other[t:, :])
    x0 = x_out[near:, :]
    z0 = mm(x_out[0 : 4 * t, :], cw[0, 0:width, :]) + mm(x0, cw[0, width:, :])
    tf = jnp.tanh(z0[:, :gated])
    sg = jax.nn.sigmoid(z0[:, gated:])
    h0 = (tf * sg).astype(BF16)
    a_out[...] = sg * (1.0 - tf * tf)
    b_out[...] = tf * sg * (1.0 - sg)
    x1 = (x0.astype(F32) + mm(h0, rw[0, :, 0:width])).astype(BF16)
    x1_out[...] = x1
    z1 = mm(x1[0 : 2 * t, :], cw[1, 0:width, :]) + mm(x1[2 * t :, :], cw[1, width:, :])
    tf = jnp.tanh(z1[:, :gated])
    sg = jax.nn.sigmoid(z1[:, gated:])
    h1 = (tf * sg).astype(BF16)
    g2 = gin[...]
    sk = skin[...]
    e1 = mm_nt(g2, rw[1, :, 0:width]) + mm_nt(sk, rw[1, :, width:])
    dz1 = jnp.concatenate([e1 * sg * (1.0 - tf * tf), e1 * tf * sg * (1.0 - sg)], axis=1).astype(BF16)
    dz_out[...] = dz1
    dpast = mm_nt(dz1, cw[1, 0:width, :]).astype(BF16)
    ga = g2.astype(F32) + mm_nt(dz1, cw[1, width:, :])
    ga_out[...] = ga
    outer = jnp.concatenate([dpast, ga.astype(BF16)], axis=0)
    o_out[...] = outer
    es_out[...] = mm_nt(sk, rw[0, :, width:])
    skips = jnp.concatenate([mm_tn(h1, sk), mm_tn(h0[2 * t :, :], sk)], axis=1)
    eighth = gated // 8
    for which, part in enumerate((mm_tn(h1, g2), mm_tn(h0, outer), skips)):
        for c in range(2):
            for q in range(4):
                rows = slice((4 * c + q) * eighth, (4 * c + q + 1) * eighth)
                staged[c, q, which * eighth : (which + 1) * eighth, :] = part[rows, :].astype(BF16)
    split_quarters(staged, mine, by_y, by_x, by_both)


def inner_kernel(
    xin, a, b, x1, dz1, outer, ga, es, cw, rw,
    mine, by_y, by_x, by_both, own_out, back_out, tail_out,
    staged, dz,
):
    width = xin.shape[1]
    t = dz1.shape[0] // 2
    near = t // 4
    _, _, core = here()
    e0 = mm_nt(outer[...], rw[0, :, 0:width])
    e0 = jnp.concatenate([e0[: 2 * t, :], e0[2 * t :, :] + es[...]], axis=0)
    dz0 = jnp.concatenate([e0 * a[...], e0 * b[...]], axis=1).astype(BF16)
    dz[0 : 4 * t, :] = dz0
    dz[4 * t :, :] = jnp.zeros((near, width), BF16)
    half = width // 16
    rows = 2 * half
    blocks = width // rows
    for base, part0, part1 in (
        (0, mm_tn(xin[0 : 4 * t, :], dz0), mm_tn(x1[0 : 2 * t, :], dz1[...])),
        (blocks, mm_tn(xin[near:, :], dz0), mm_tn(x1[2 * t :, :], dz1[...])),
    ):
        for block in range(blocks):
            g, x, c = (base + block) // 4, (base + block) // 2 % 2, (base + block) % 2
            for y in range(2):
                src = slice(block * rows + y * half, block * rows + (y + 1) * half)
                staged[c, 2 * x + y, g, 0:half, :] = part0[src, :].astype(BF16)
                staged[c, 2 * x + y, g, half:, :] = part1[src, :].astype(BF16)
    split_quarters(staged, mine, by_y, by_x, by_both)
    at = pl.multiple_of(core * t, t)
    long = t + near
    back = dz[pl.ds(at, long), :]
    here_dz = dz[pl.ds(2 * t + at, long), :]
    first = mm_nt(dz[0:near, :], cw[0, 0:width, :]).astype(BF16)
    both = jnp.concatenate([back, here_dz], axis=0)
    wp = mm_nt(both, cw[0, 0:width, :]).astype(BF16)
    wx = mm_nt(both, cw[0, width:, :])
    back_out[...] = (outer[pl.ds(at, t), :].astype(F32) + wx[0:t, :] + wp[near:long, :].astype(F32)).astype(BF16)
    own_out[...] = ga[pl.ds(at, t), :] + wx[long : long + t, :] + wp[long + near :, :].astype(F32)
    tail_out[...] = first


def total_of(*refs):
    total = refs[0][...].astype(F32)
    for ref in refs[1:]:
        total = total + ref[...].astype(F32)
    return total


def sum_xy_kernel(mine, by_y, by_x, by_both, tail, out):
    rows = mine.shape[0]
    out[0:rows, :] = total_of(mine, by_y, by_x, by_both).astype(BF16)
    out[rows:, :] = tail[...]


def sum_z1_kernel(rows, mine, got, out):
    out[0:rows, :] = total_of(mine.at[0:rows, :], got.at[0:rows, :]).astype(BF16)
    out[rows:, :] = got[rows:, :]


def sum_z2_kernel(factor, mine, got, out):
    rows = out.shape[0]
    out[...] = (total_of(mine.at[0:rows, :], got.at[0:rows, :]) * factor).astype(BF16)


def scaled_sum_kernel(factor, *refs):
    refs[-1][...] = (total_of(*refs[:-1]) * factor).astype(BF16)


def groups_kernel(mine, by_y, by_x, by_both, keep, send1, send2, send3, staged):
    g, _, _ = here()
    staged[...] = total_of(mine, by_y, by_x, by_both)
    keep[...] = staged[g]
    for k, out in ((1, send1), (2, send2), (3, send3)):
        out[...] = staged[lax.bitwise_xor(g, k)].astype(BF16)


def in_order_kernel(mine, by_y, by_x, by_both, out):
    _, x, _ = here()
    q = 2 * x + lax.axis_index("dp")
    for k, ref in enumerate((mine, by_y, by_x, by_both)):
        out[lax.bitwise_xor(q, k)] = ref[...]


def finish_kernel(mine, other, res_mine, res_other, conv, res):
    y = lax.axis_index("dp")
    half = mine.shape[0] // 2
    for ref, at in ((mine, y), (other, 1 - y)):
        rows = pl.ds(pl.multiple_of(at * half, half), half)
        conv[0, rows, :] = ref[0:half, :]
        conv[1, rows, :] = ref[half:, :]
    _, _, core = here()
    eighth = res.shape[1] // 8
    width, part = res_mine.shape[2], res_mine.shape[2] // 2
    for ref, c in ((res_mine, core), (res_other, 1 - core)):
        for q in range(4):
            rows = pl.ds(pl.multiple_of((4 * c + q) * eighth, eighth), eighth)
            res[1, rows, 0:width] = ref[q, 0:eighth, :]
            res[0, rows, 0:width] = ref[q, eighth : 2 * eighth, :]
            res[1, rows, width:] = ref[q, 2 * eighth :, 0:part]
            res[0, rows, width:] = ref[q, 2 * eighth :, part:]


def finish_signal_kernel(own, come, got1, got2, out, done):
    done[...] = jnp.zeros_like(done)
    t = own.shape[0]
    near = t // 4
    first = got1.shape[0] - near
    g, _, core = here()
    total = own[...] + jnp.where(lax.axis_index("tm") < 14, come[...].astype(F32), 0.0)
    out[0 : t - near, :] = total[0 : t - near, :].astype(BF16)
    last = jnp.where(lax.rem(g, 2) == 0, got1[first:, :], got2[first:, :]).astype(F32)
    last = jnp.where((g < 3) & (core == 1), last, 0.0)
    out[t - near :, :] = (total[t - near :, :] + last).astype(BF16)


def swap(x, distance):
    return lax.ppermute(x, "tm", [(i, i ^ distance) for i in range(16)])


def swap_streams(x):
    return lax.ppermute(x, "dp", [(0, 1), (1, 0)])


def swap_both(x, distance):
    route = [(16 * y + i, 16 * (1 - y) + (i ^ distance)) for y in range(2) for i in range(16)]
    return lax.ppermute(x, ("dp", "tm"), route)


def shift(x, distance):
    return lax.ppermute(x, "tm", [(i, (i + distance) % 16) for i in range(16)])


def body(signal, conv_weight, res_weight, grad_out, skip_cotangent):
    s_dev, t, width = signal.shape
    gated = res_weight.shape[1]
    near = t // 4
    half = width // 16
    res_rows = 3 * gated // 8
    factor = float(s_dev * t * 32) ** (-0.5)

    far = shift(signal[0], 2)
    cw, rw, own = load(conv_weight, res_weight, signal[0], grad_out[0], skip_cotangent[0])
    own_other = swap(own, 1)
    tail4 = shift(signal[0, t - near :, :], 4)
    (halo,) = call(pack_halo_kernel, [shaped((t + near, width))], far, tail4, name="pack_halo")
    halo_other = swap(halo, 1)

    res = shaped((res_rows, width))
    *rsplit, xin, a, b, x1, dz1, outer, ga, es = call(
        forward_and_outer_kernel,
        [
            res, res, res, res,
            shaped((4 * t + near, width)), shaped((4 * t, gated), F32), shaped((4 * t, gated), F32),
            shaped((4 * t, width)), shaped((2 * t, width)), shaped((4 * t, width)), shaped((2 * t, width), F32),
            shaped((2 * t, gated), F32),
        ],
        own, own_other, halo, halo_other, cw, rw,
        scratch=[
            pltpu.VMEM((2, 4, res_rows, width), BF16), pltpu.VMEM((2 * t, width), BF16),
            pltpu.VMEM((2 * t, gated), BF16),
        ],
        vmem=16, name="forward_and_outer",
    )
    piece = (2 * half, width)
    part = shaped((4,) + piece)
    *csplit, own, back, tail = call(
        inner_kernel,
        [part, part, part, part, shaped((t, width), F32), shaped((t, width)), shaped((near, width))],
        xin, a, b, x1, dz1, outer, ga, es, cw, rw,
        scratch=[pltpu.VMEM((2, 4, 4) + piece, BF16), pltpu.VMEM((4 * t + near, width), BF16)],
        vmem=16, flops=2_000_000_000, name="inner",
    )

    def around(by_y, by_x, by_both):
        return swap_streams(by_y), swap(by_x, 2), swap_both(by_both, 2)

    rterms = (rsplit[0],) + around(*rsplit[1:])
    cterms = (csplit[0],) + around(*csplit[1:])
    come = shift(back, -2)
    long = shaped((res_rows + near, width))
    (rsum,) = call(sum_xy_kernel, [long], *rterms, tail, after=(csplit[0],), name="res_sum_xy")
    rgot1 = swap(rsum, 4)
    (rsum,) = call(functools.partial(sum_z1_kernel, res_rows), [long], rsum, rgot1, name="res_sum_z1")
    rgot2 = swap(rsum, 8)
    ckeep, *csend = call(
        groups_kernel, [shaped(piece, F32)] + [shaped(piece)] * 3, *cterms,
        after=(rsum,), scratch=[pltpu.VMEM((4,) + piece, F32)], name="conv_groups",
    )
    cgot = [swap(send, 4 * k) for k, send in zip((1, 2, 3), csend)]
    input_grad, done = call(
        finish_signal_kernel, [shaped((t, width)), shaped((8, 128), F32)], own, come, rgot1, rgot2,
        after=(ckeep,), name="finish_signal",
    )
    (quarter,) = call(
        functools.partial(sum_z2_kernel, factor), [res], rsum, rgot2, after=(ckeep,), name="res_sum_z2"
    )
    rparts = (quarter,) + around(quarter, quarter, quarter)
    (mine,) = call(
        functools.partial(scaled_sum_kernel, factor), [shaped(piece)], ckeep, *cgot,
        after=(quarter,), name="conv_scaled",
    )
    other = swap_streams(mine)
    (ordered,) = call(in_order_kernel, [shaped((4, res_rows, width))], *rparts, after=(mine, done), name="res_in_order")
    rgot = swap(ordered, 1)
    conv_grad, res_grad = call(
        finish_kernel, [shaped((2,) + piece), shaped(res_weight.shape)], mine, other, ordered, rgot,
        name="finish",
    )
    return (input_grad.reshape(s_dev, t, width), conv_grad, res_grad)


def solution(mesh):
    in_specs = (P("dp", "tm", None), P(), P(), P("dp", "tm", None), P("dp", "tm", None))
    out_specs = (P("dp", "tm", None), P(None, "tm", None), P())
    chosen = body if mesh.shape["dp"] == 2 and mesh.shape["tm"] == 16 else general_body
    return jax.shard_map(chosen, mesh=mesh, in_specs=in_specs, out_specs=out_specs, check_vma=False)
```

```python
import functools

import jax
import jax.numpy as jnp
from jax import lax
from jax.experimental import pallas as pl
from jax.experimental.pallas import tpu as pltpu
from jax.sharding import PartitionSpec as P

F32 = jnp.float32
BF16 = jnp.bfloat16


def passed_along(block, axis, distance):
    devices = range(lax.axis_size(axis))
    route = [(i - distance, i) for i in devices if i - distance in devices]
    return lax.ppermute(block, axis, route)


def gate_gradients(dh, z, gated):
    tf = jnp.tanh(z[:, :gated])
    sg = jax.nn.sigmoid(z[:, gated:])
    return jnp.concatenate([dh * sg * (1.0 - tf * tf), dh * tf * sg * (1.0 - sg)], axis=1).astype(
        jnp.bfloat16
    )


def reduce_conv(cat_rows, dz):
    piece = lax.psum_scatter(
        lax.dot_general(cat_rows, dz, (((0,), (0,)), ((), ())), preferred_element_type=jnp.float32),
        "tm",
        scatter_dimension=0,
        tiled=True,
    )
    return lax.psum(piece, "dp")


def general_body(signal, conv_weight, res_weight, grad_out, skip_cotangent):
    s_dev, t_dev, width = signal.shape
    gated = res_weight.shape[1]
    near = t_dev // 4
    slabs = lax.axis_size("tm") // 8
    count_rows = s_dev * t_dev
    factor = float(count_rows * lax.axis_size("dp") * lax.axis_size("tm")) ** (-0.5)

    def delayed(x, layer):
        if layer == 0:
            got = passed_along(x[:, t_dev - near :, :], "tm", 1)
            return jnp.concatenate([got, x[:, : t_dev - near, :]], axis=1)
        return passed_along(x, "tm", slabs)

    def shifted_rows(dpast, layer):
        if layer == 0:
            got = passed_along(dpast[:, :near, :], "tm", -1)
            return jnp.concatenate([dpast[:, near:, :], got], axis=1)
        return passed_along(dpast, "tm", -slabs)

    x = signal
    cats = []
    zvals = []
    hvals = []
    for layer in range(2):
        past = delayed(x, layer)
        cat_rows = jnp.concatenate([past, x], axis=2).reshape(count_rows, 2 * width)
        z = jnp.dot(cat_rows, conv_weight[layer], preferred_element_type=jnp.float32)
        h = (jnp.tanh(z[:, :gated]) * jax.nn.sigmoid(z[:, gated:])).astype(jnp.bfloat16)
        cats.append(cat_rows)
        zvals.append(z)
        hvals.append(h)
        if layer == 0:
            resid = jnp.dot(h, res_weight[0][:, :width], preferred_element_type=jnp.float32)
            x = (
                (x.reshape(count_rows, width).astype(jnp.float32) + resid)
                .astype(jnp.bfloat16)
                .reshape(s_dev, t_dev, width)
            )
    grad = grad_out.reshape(count_rows, width).astype(jnp.float32)
    skip_rows = skip_cotangent.reshape(count_rows, -1)
    conv_parts = [None, None]
    res_parts = [None, None]
    dz_kept = [None, None]
    for layer in (1, 0):
        outer = jnp.concatenate([grad.astype(jnp.bfloat16), skip_rows], axis=1)
        dh = lax.dot_general(
            outer, res_weight[layer], (((1,), (1,)), ((), ())), preferred_element_type=jnp.float32
        )
        dz = gate_gradients(dh, zvals[layer], gated)
        wcat = lax.dot_general(
            dz, conv_weight[layer], (((1,), (1,)), ((), ())), preferred_element_type=jnp.float32
        )
        dpast = wcat[:, :width].astype(jnp.bfloat16).reshape(s_dev, t_dev, width)
        moved = shifted_rows(dpast, layer).reshape(count_rows, width)
        grad = grad + wcat[:, width:] + moved.astype(jnp.float32)
        res_local = lax.dot_general(
            hvals[layer], outer, (((0,), (0,)), ((), ())), preferred_element_type=jnp.float32
        )
        dz_kept[layer] = dz
        res_parts[layer] = res_local
    for layer in range(2):
        conv_parts[layer] = reduce_conv(cats[layer], dz_kept[layer])
    res_total = lax.psum(jnp.stack(res_parts), ("dp", "tm"))
    input_grad = grad.astype(jnp.bfloat16).reshape(s_dev, t_dev, width)
    conv_grad = (jnp.stack(conv_parts) * factor).astype(jnp.bfloat16)
    res_grad = (res_total * factor).astype(jnp.bfloat16)
    return (input_grad, conv_grad, res_grad)


def mm(a, b):
    return jnp.dot(a, b, preferred_element_type=F32)


def mm_nt(a, b):
    return lax.dot_general(a, b, (((1,), (1,)), ((), ())), preferred_element_type=F32)


def mm_tn(a, b):
    return lax.dot_general(a, b, (((0,), (0,)), ((), ())), preferred_element_type=F32)


def shaped(shape, dtype=BF16):
    return jax.ShapeDtypeStruct(shape, dtype)


def call(kernel, outs, *args, after=(), scratch=(), flops=0, nbytes=0, vmem=8, name=None):
    n_args = len(args)

    def run(*refs):
        kernel(*refs[:n_args], *refs[n_args + len(after) :])

    in_vmem = pl.BlockSpec(memory_space=pltpu.VMEM)
    return pl.pallas_call(
        run,
        out_shape=outs,
        in_specs=[in_vmem] * n_args + [pl.BlockSpec(memory_space=pl.ANY)] * len(after),
        out_specs=[in_vmem] * len(outs),
        scratch_shapes=list(scratch),
        compiler_params=pltpu.CompilerParams(vmem_limit_bytes=vmem * 1024 * 1024),
        cost_estimate=pl.CostEstimate(flops=flops, bytes_accessed=nbytes, transcendentals=0),
        name=name,
    )(*args, *after)


def place(tm):
    return tm // 4, lax.rem(tm // 2, 2), lax.rem(tm, 2)


def here():
    return place(lax.axis_index("tm"))


def load_kernel(cw, rw, sig, grad, skip, cw_out, rw_out, own_out, sems):
    width = sig.shape[1]
    pairs = (
        (sig, own_out.at[:, 0:width]),
        (grad, own_out.at[:, width : 2 * width]),
        (skip, own_out.at[:, 2 * width :]),
        (cw, cw_out),
        (rw, rw_out),
    )
    copies = [pltpu.make_async_copy(src, dst, sems.at[i]) for i, (src, dst) in enumerate(pairs)]
    for copy in copies:
        copy.start()
    for copy in copies:
        copy.wait()


def load(cw, rw, sig, grad, skip):
    t, width = sig.shape
    in_hbm = [pltpu.with_memory_space_constraint(a, pltpu.HBM) for a in (cw, rw, sig, grad, skip)]
    return pl.pallas_call(
        load_kernel,
        out_shape=[
            pltpu.VMEM(cw.shape, BF16), pltpu.VMEM(rw.shape, BF16),
            pltpu.VMEM((t, 2 * width + skip.shape[1]), BF16),
        ],
        in_specs=[pl.BlockSpec(memory_space=pltpu.HBM)] * 5,
        out_specs=[pl.BlockSpec(memory_space=pltpu.VMEM)] * 3,
        scratch_shapes=[pltpu.SemaphoreType.DMA((5,))],
        compiler_params=pltpu.CompilerParams(vmem_limit_bytes=8 * 1024 * 1024),
        cost_estimate=pl.CostEstimate(flops=4_000_000_000, bytes_accessed=6_000_000, transcendentals=0),
        name="load",
    )(*in_hbm)


def pack_halo_kernel(far, tail4, out):
    t = far.shape[0]
    slab = lax.axis_index("tm")
    out[0:t, :] = jnp.where(slab >= 2, far[...], jnp.zeros_like(far))
    out[t:, :] = jnp.where(slab >= 4, tail4[...], jnp.zeros_like(tail4))


def split_quarters(staged, mine, by_y, by_x, by_both):
    _, x, core = here()
    q = 2 * x + lax.axis_index("dp")
    mine[...] = staged[core, q]
    for k, out in ((1, by_y), (2, by_x), (3, by_both)):
        out[...] = staged[core, lax.bitwise_xor(q, k)]


def forward_and_outer_kernel(
    own, own_other, halo, halo_other, cw, rw,
    mine, by_y, by_x, by_both, x_out, a_out, b_out, x1_out, dz_out, o_out, ga_out, es_out,
    staged, gin, skin,
):
    t = own.shape[0]
    near = t // 4
    width = x_out.shape[1]
    gated = rw.shape[1]
    _, _, core = here()
    for a, h, c in ((own, halo, core), (own_other, halo_other, 1 - core)):
        rows = pl.ds(pl.multiple_of(c * t, t), t)
        x_out[pl.ds(pl.multiple_of(near + c * t, near), t), :] = h[0:t, :]
        x_out[pl.ds(pl.multiple_of(near + (2 + c) * t, near), t), :] = a[:, 0:width]
        gin[rows, :] = a[:, width : 2 * width]
        skin[rows, :] = a[:, 2 * width :]
    x_out[0:near, :] = jnp.where(core == 1, halo[t:, :], halo_other[t:, :])
    x0 = x_out[near:, :]
    z0 = mm(x_out[0 : 4 * t, :], cw[0, 0:width, :]) + mm(x0, cw[0, width:, :])
    tf = jnp.tanh(z0[:, :gated])
    sg = jax.nn.sigmoid(z0[:, gated:])
    h0 = (tf * sg).astype(BF16)
    a_out[...] = sg * (1.0 - tf * tf)
    b_out[...] = tf * sg * (1.0 - sg)
    x1 = (x0.astype(F32) + mm(h0, rw[0, :, 0:width])).astype(BF16)
    x1_out[...] = x1
    z1 = mm(x1[0 : 2 * t, :], cw[1, 0:width, :]) + mm(x1[2 * t :, :], cw[1, width:, :])
    tf = jnp.tanh(z1[:, :gated])
    sg = jax.nn.sigmoid(z1[:, gated:])
    h1 = (tf * sg).astype(BF16)
    g2 = gin[...]
    sk = skin[...]
    e1 = mm_nt(g2, rw[1, :, 0:width]) + mm_nt(sk, rw[1, :, width:])
    dz1 = jnp.concatenate([e1 * sg * (1.0 - tf * tf), e1 * tf * sg * (1.0 - sg)], axis=1).astype(BF16)
    dz_out[...] = dz1
    dpast = mm_nt(dz1, cw[1, 0:width, :]).astype(BF16)
    ga = g2.astype(F32) + mm_nt(dz1, cw[1, width:, :])
    ga_out[...] = ga
    outer = jnp.concatenate([dpast, ga.astype(BF16)], axis=0)
    o_out[...] = outer
    es_out[...] = mm_nt(sk, rw[0, :, width:])
    skips = jnp.concatenate([mm_tn(h1, sk), mm_tn(h0[2 * t :, :], sk)], axis=1)
    eighth = gated // 8
    for which, part in enumerate((mm_tn(h1, g2), mm_tn(h0, outer), skips)):
        for c in range(2):
            for q in range(4):
                rows = slice((4 * c + q) * eighth, (4 * c + q + 1) * eighth)
                staged[c, q, which * eighth : (which + 1) * eighth, :] = part[rows, :].astype(BF16)
    split_quarters(staged, mine, by_y, by_x, by_both)


def inner_kernel(
    xin, a, b, x1, dz1, outer, ga, es, cw, rw,
    mine, by_y, by_x, by_both, own_out, back_out, tail_out,
    staged, dz,
):
    width = xin.shape[1]
    t = dz1.shape[0] // 2
    near = t // 4
    _, _, core = here()
    e0 = mm_nt(outer[...], rw[0, :, 0:width])
    e0 = jnp.concatenate([e0[: 2 * t, :], e0[2 * t :, :] + es[...]], axis=0)
    dz0 = jnp.concatenate([e0 * a[...], e0 * b[...]], axis=1).astype(BF16)
    dz[0 : 4 * t, :] = dz0
    dz[4 * t :, :] = jnp.zeros((near, width), BF16)
    half = width // 16
    rows = 2 * half
    blocks = width // rows
    for base, part0, part1 in (
        (0, mm_tn(xin[0 : 4 * t, :], dz0), mm_tn(x1[0 : 2 * t, :], dz1[...])),
        (blocks, mm_tn(xin[near:, :], dz0), mm_tn(x1[2 * t :, :], dz1[...])),
    ):
        for block in range(blocks):
            g, x, c = (base + block) // 4, (base + block) // 2 % 2, (base + block) % 2
            for y in range(2):
                src = slice(block * rows + y * half, block * rows + (y + 1) * half)
                staged[c, 2 * x + y, g, 0:half, :] = part0[src, :].astype(BF16)
                staged[c, 2 * x + y, g, half:, :] = part1[src, :].astype(BF16)
    split_quarters(staged, mine, by_y, by_x, by_both)
    at = pl.multiple_of(core * t, t)
    long = t + near
    back = dz[pl.ds(at, long), :]
    here_dz = dz[pl.ds(2 * t + at, long), :]
    first = mm_nt(dz[0:near, :], cw[0, 0:width, :]).astype(BF16)
    both = jnp.concatenate([back, here_dz], axis=0)
    wp = mm_nt(both, cw[0, 0:width, :]).astype(BF16)
    wx = mm_nt(both, cw[0, width:, :])
    back_out[...] = (outer[pl.ds(at, t), :].astype(F32) + wx[0:t, :] + wp[near:long, :].astype(F32)).astype(BF16)
    own_out[...] = ga[pl.ds(at, t), :] + wx[long : long + t, :] + wp[long + near :, :].astype(F32)
    tail_out[...] = first


def total_of(*refs):
    total = refs[0][...].astype(F32)
    for ref in refs[1:]:
        total = total + ref[...].astype(F32)
    return total


def sum_xy_kernel(mine, by_y, by_x, by_both, tail, out):
    rows = mine.shape[0]
    out[0:rows, :] = total_of(mine, by_y, by_x, by_both).astype(BF16)
    out[rows:, :] = tail[...]


def sum_z1_kernel(rows, mine, got, out):
    out[0:rows, :] = total_of(mine.at[0:rows, :], got.at[0:rows, :]).astype(BF16)
    out[rows:, :] = got[rows:, :]


def sum_z2_kernel(factor, mine, got, out):
    rows = out.shape[0]
    out[...] = (total_of(mine.at[0:rows, :], got.at[0:rows, :]) * factor).astype(BF16)


def scaled_sum_kernel(factor, *refs):
    refs[-1][...] = (total_of(*refs[:-1]) * factor).astype(BF16)


def groups_kernel(mine, by_y, by_x, by_both, keep, send1, send2, send3, staged):
    g, _, _ = here()
    staged[...] = total_of(mine, by_y, by_x, by_both)
    keep[...] = staged[g]
    for k, out in ((1, send1), (2, send2), (3, send3)):
        out[...] = staged[lax.bitwise_xor(g, k)].astype(BF16)


def in_order_kernel(mine, by_y, by_x, by_both, out):
    _, x, _ = here()
    q = 2 * x + lax.axis_index("dp")
    for k, ref in enumerate((mine, by_y, by_x, by_both)):
        out[lax.bitwise_xor(q, k)] = ref[...]


def finish_conv_kernel(mine, other, conv, done):
    done[...] = jnp.zeros_like(done)
    y = lax.axis_index("dp")
    half = mine.shape[0] // 2
    for ref, at in ((mine, y), (other, 1 - y)):
        rows = pl.ds(pl.multiple_of(at * half, half), half)
        conv[0, rows, :] = ref[0:half, :]
        conv[1, rows, :] = ref[half:, :]


def finish_res_kernel(mine, other, res):
    _, _, core = here()
    eighth = res.shape[1] // 8
    width, part = mine.shape[2], mine.shape[2] // 2
    for ref, c in ((mine, core), (other, 1 - core)):
        for q in range(4):
            rows = pl.ds(pl.multiple_of((4 * c + q) * eighth, eighth), eighth)
            res[1, rows, 0:width] = ref[q, 0:eighth, :]
            res[0, rows, 0:width] = ref[q, eighth : 2 * eighth, :]
            res[1, rows, width:] = ref[q, 2 * eighth :, 0:part]
            res[0, rows, width:] = ref[q, 2 * eighth :, part:]


def finish_signal_kernel(own, come, got1, got2, out, done):
    done[...] = jnp.zeros_like(done)
    t = own.shape[0]
    near = t // 4
    first = got1.shape[0] - near
    g, _, core = here()
    total = own[...] + jnp.where(lax.axis_index("tm") < 14, come[...].astype(F32), 0.0)
    out[0 : t - near, :] = total[0 : t - near, :].astype(BF16)
    last = jnp.where(lax.rem(g, 2) == 0, got1[first:, :], got2[first:, :]).astype(F32)
    last = jnp.where((g < 3) & (core == 1), last, 0.0)
    out[t - near :, :] = (total[t - near :, :] + last).astype(BF16)


def swap(x, distance):
    return lax.ppermute(x, "tm", [(i, i ^ distance) for i in range(16)])


def swap_streams(x):
    return lax.ppermute(x, "dp", [(0, 1), (1, 0)])


def swap_both(x, distance):
    route = [(16 * y + i, 16 * (1 - y) + (i ^ distance)) for y in range(2) for i in range(16)]
    return lax.ppermute(x, ("dp", "tm"), route)


def shift(x, distance):
    return lax.ppermute(x, "tm", [(i, (i + distance) % 16) for i in range(16)])


def body(signal, conv_weight, res_weight, grad_out, skip_cotangent):
    s_dev, t, width = signal.shape
    gated = res_weight.shape[1]
    near = t // 4
    half = width // 16
    res_rows = 3 * gated // 8
    factor = float(s_dev * t * 32) ** (-0.5)

    far = shift(signal[0], 2)
    cw, rw, own = load(conv_weight, res_weight, signal[0], grad_out[0], skip_cotangent[0])
    own_other = swap(own, 1)
    tail4 = shift(signal[0, t - near :, :], 4)
    (halo,) = call(pack_halo_kernel, [shaped((t + near, width))], far, tail4, name="pack_halo")
    halo_other = swap(halo, 1)

    res = shaped((res_rows, width))
    *rsplit, xin, a, b, x1, dz1, outer, ga, es = call(
        forward_and_outer_kernel,
        [
            res, res, res, res,
            shaped((4 * t + near, width)), shaped((4 * t, gated), F32), shaped((4 * t, gated), F32),
            shaped((4 * t, width)), shaped((2 * t, width)), shaped((4 * t, width)), shaped((2 * t, width), F32),
            shaped((2 * t, gated), F32),
        ],
        own, own_other, halo, halo_other, cw, rw,
        scratch=[
            pltpu.VMEM((2, 4, res_rows, width), BF16), pltpu.VMEM((2 * t, width), BF16),
            pltpu.VMEM((2 * t, gated), BF16),
        ],
        vmem=16, name="forward_and_outer",
    )
    piece = (2 * half, width)
    part = shaped((4,) + piece)
    *csplit, own, back, tail = call(
        inner_kernel,
        [part, part, part, part, shaped((t, width), F32), shaped((t, width)), shaped((near, width))],
        xin, a, b, x1, dz1, outer, ga, es, cw, rw,
        scratch=[pltpu.VMEM((2, 4, 4) + piece, BF16), pltpu.VMEM((4 * t + near, width), BF16)],
        vmem=16, flops=2_000_000_000, name="inner",
    )

    def around(by_y, by_x, by_both):
        return swap_streams(by_y), swap(by_x, 2), swap_both(by_both, 2)

    rterms = (rsplit[0],) + around(*rsplit[1:])
    cterms = (csplit[0],) + around(*csplit[1:])
    come = shift(back, -2)
    long = shaped((res_rows + near, width))
    (rsum,) = call(sum_xy_kernel, [long], *rterms, tail, after=(csplit[0],), name="res_sum_xy")
    rgot1 = swap(rsum, 4)
    (rsum,) = call(functools.partial(sum_z1_kernel, res_rows), [long], rsum, rgot1, name="res_sum_z1")
    rgot2 = swap(rsum, 8)
    ckeep, *csend = call(
        groups_kernel, [shaped(piece, F32)] + [shaped(piece)] * 3, *cterms,
        after=(rsum,), scratch=[pltpu.VMEM((4,) + piece, F32)], name="conv_groups",
    )
    cgot = [swap(send, 4 * k) for k, send in zip((1, 2, 3), csend)]
    input_grad, done = call(
        finish_signal_kernel, [shaped((t, width)), shaped((8, 128), F32)], own, come, rgot1, rgot2,
        after=(ckeep,), name="finish_signal",
    )
    (quarter,) = call(
        functools.partial(sum_z2_kernel, factor), [res], rsum, rgot2, after=(ckeep,), name="res_sum_z2"
    )
    rparts = (quarter,) + around(quarter, quarter, quarter)
    (mine,) = call(
        functools.partial(scaled_sum_kernel, factor), [shaped(piece)], ckeep, *cgot,
        after=(quarter,), flops=10_000_000_000, name="conv_scaled",
    )
    other = swap_streams(mine)
    (ordered,) = call(in_order_kernel, [shaped((4, res_rows, width))], *rparts, after=(mine, done), name="res_in_order")
    rgot = swap(ordered, 1)
    conv_grad, conv_done = call(
        finish_conv_kernel, [shaped((2,) + piece), shaped((8, 128), F32)], mine, other,
        flops=10_000_000_000, name="finish_conv",
    )
    (res_grad,) = call(
        finish_res_kernel, [shaped(res_weight.shape)], ordered, rgot, after=(conv_done,), name="finish_res"
    )
    return (input_grad.reshape(s_dev, t, width), conv_grad, res_grad)


def solution(mesh):
    in_specs = (P("dp", "tm", None), P(), P(), P("dp", "tm", None), P("dp", "tm", None))
    out_specs = (P("dp", "tm", None), P(None, "tm", None), P())
    chosen = body if mesh.shape["dp"] == 2 and mesh.shape["tm"] == 16 else general_body
    return jax.shard_map(chosen, mesh=mesh, in_specs=in_specs, out_specs=out_specs, check_vma=False)
```

```python
import functools

import jax
import jax.numpy as jnp
from jax import lax
from jax.experimental import pallas as pl
from jax.experimental.pallas import tpu as pltpu
from jax.sharding import PartitionSpec as P

F32 = jnp.float32
BF16 = jnp.bfloat16


def passed_along(block, axis, distance):
    devices = range(lax.axis_size(axis))
    route = [(i - distance, i) for i in devices if i - distance in devices]
    return lax.ppermute(block, axis, route)


def gate_gradients(dh, z, gated):
    tf = jnp.tanh(z[:, :gated])
    sg = jax.nn.sigmoid(z[:, gated:])
    return jnp.concatenate([dh * sg * (1.0 - tf * tf), dh * tf * sg * (1.0 - sg)], axis=1).astype(
        jnp.bfloat16
    )


def reduce_conv(cat_rows, dz):
    piece = lax.psum_scatter(
        lax.dot_general(cat_rows, dz, (((0,), (0,)), ((), ())), preferred_element_type=jnp.float32),
        "tm",
        scatter_dimension=0,
        tiled=True,
    )
    return lax.psum(piece, "dp")


def general_body(signal, conv_weight, res_weight, grad_out, skip_cotangent):
    s_dev, t_dev, width = signal.shape
    gated = res_weight.shape[1]
    near = t_dev // 4
    slabs = lax.axis_size("tm") // 8
    count_rows = s_dev * t_dev
    factor = float(count_rows * lax.axis_size("dp") * lax.axis_size("tm")) ** (-0.5)

    def delayed(x, layer):
        if layer == 0:
            got = passed_along(x[:, t_dev - near :, :], "tm", 1)
            return jnp.concatenate([got, x[:, : t_dev - near, :]], axis=1)
        return passed_along(x, "tm", slabs)

    def shifted_rows(dpast, layer):
        if layer == 0:
            got = passed_along(dpast[:, :near, :], "tm", -1)
            return jnp.concatenate([dpast[:, near:, :], got], axis=1)
        return passed_along(dpast, "tm", -slabs)

    x = signal
    cats = []
    zvals = []
    hvals = []
    for layer in range(2):
        past = delayed(x, layer)
        cat_rows = jnp.concatenate([past, x], axis=2).reshape(count_rows, 2 * width)
        z = jnp.dot(cat_rows, conv_weight[layer], preferred_element_type=jnp.float32)
        h = (jnp.tanh(z[:, :gated]) * jax.nn.sigmoid(z[:, gated:])).astype(jnp.bfloat16)
        cats.append(cat_rows)
        zvals.append(z)
        hvals.append(h)
        if layer == 0:
            resid = jnp.dot(h, res_weight[0][:, :width], preferred_element_type=jnp.float32)
            x = (
                (x.reshape(count_rows, width).astype(jnp.float32) + resid)
                .astype(jnp.bfloat16)
                .reshape(s_dev, t_dev, width)
            )
    grad = grad_out.reshape(count_rows, width).astype(jnp.float32)
    skip_rows = skip_cotangent.reshape(count_rows, -1)
    conv_parts = [None, None]
    res_parts = [None, None]
    dz_kept = [None, None]
    for layer in (1, 0):
        outer = jnp.concatenate([grad.astype(jnp.bfloat16), skip_rows], axis=1)
        dh = lax.dot_general(
            outer, res_weight[layer], (((1,), (1,)), ((), ())), preferred_element_type=jnp.float32
        )
        dz = gate_gradients(dh, zvals[layer], gated)
        wcat = lax.dot_general(
            dz, conv_weight[layer], (((1,), (1,)), ((), ())), preferred_element_type=jnp.float32
        )
        dpast = wcat[:, :width].astype(jnp.bfloat16).reshape(s_dev, t_dev, width)
        moved = shifted_rows(dpast, layer).reshape(count_rows, width)
        grad = grad + wcat[:, width:] + moved.astype(jnp.float32)
        res_local = lax.dot_general(
            hvals[layer], outer, (((0,), (0,)), ((), ())), preferred_element_type=jnp.float32
        )
        dz_kept[layer] = dz
        res_parts[layer] = res_local
    for layer in range(2):
        conv_parts[layer] = reduce_conv(cats[layer], dz_kept[layer])
    res_total = lax.psum(jnp.stack(res_parts), ("dp", "tm"))
    input_grad = grad.astype(jnp.bfloat16).reshape(s_dev, t_dev, width)
    conv_grad = (jnp.stack(conv_parts) * factor).astype(jnp.bfloat16)
    res_grad = (res_total * factor).astype(jnp.bfloat16)
    return (input_grad, conv_grad, res_grad)


def mm(a, b):
    return jnp.dot(a, b, preferred_element_type=F32)


def mm_nt(a, b):
    return lax.dot_general(a, b, (((1,), (1,)), ((), ())), preferred_element_type=F32)


def mm_tn(a, b):
    return lax.dot_general(a, b, (((0,), (0,)), ((), ())), preferred_element_type=F32)


def shaped(shape, dtype=BF16):
    return jax.ShapeDtypeStruct(shape, dtype)


def call(kernel, outs, *args, after=(), scratch=(), flops=0, nbytes=0, vmem=8, name=None):
    n_args = len(args)

    def run(*refs):
        kernel(*refs[:n_args], *refs[n_args + len(after) :])

    in_vmem = pl.BlockSpec(memory_space=pltpu.VMEM)
    return pl.pallas_call(
        run,
        out_shape=outs,
        in_specs=[in_vmem] * n_args + [pl.BlockSpec(memory_space=pl.ANY)] * len(after),
        out_specs=[in_vmem] * len(outs),
        scratch_shapes=list(scratch),
        compiler_params=pltpu.CompilerParams(vmem_limit_bytes=vmem * 1024 * 1024),
        cost_estimate=pl.CostEstimate(flops=flops, bytes_accessed=nbytes, transcendentals=0),
        name=name,
    )(*args, *after)


def place(tm):
    return tm // 4, lax.rem(tm // 2, 2), lax.rem(tm, 2)


def here():
    return place(lax.axis_index("tm"))


def copy_all(pairs, sems):
    copies = [pltpu.make_async_copy(src, dst, sems.at[i]) for i, (src, dst) in enumerate(pairs)]
    for copy in copies:
        copy.start()
    for copy in copies:
        copy.wait()


def load_slab_kernel(sig, grad, skip, own_out, tail_out, sems):
    t, width = sig.shape
    near = tail_out.shape[0]
    pairs = (
        (sig.at[t - near :, :], tail_out),
        (sig, own_out.at[:, 0:width]),
        (grad, own_out.at[:, width : 2 * width]),
        (skip, own_out.at[:, 2 * width :]),
    )
    copy_all(pairs, sems)


def load_weights_kernel(cw, rw, cw_out, rw_out, sems):
    copy_all(((cw, cw_out), (rw, rw_out)), sems)


def load(kernel, outs, flops, name, *arrays):
    in_hbm = [pltpu.with_memory_space_constraint(a, pltpu.HBM) for a in arrays]
    return pl.pallas_call(
        kernel,
        out_shape=[pltpu.VMEM(shape, BF16) for shape in outs],
        in_specs=[pl.BlockSpec(memory_space=pltpu.HBM)] * len(arrays),
        out_specs=[pl.BlockSpec(memory_space=pltpu.VMEM)] * len(outs),
        scratch_shapes=[pltpu.SemaphoreType.DMA((4,))],
        compiler_params=pltpu.CompilerParams(vmem_limit_bytes=8 * 1024 * 1024),
        cost_estimate=pl.CostEstimate(flops=flops, bytes_accessed=0, transcendentals=0),
        name=name,
    )(*in_hbm)


def pack_halo_kernel(far, tail4, out):
    t = far.shape[0]
    slab = lax.axis_index("tm")
    out[0:t, :] = jnp.where(slab >= 2, far[...], jnp.zeros_like(far))
    out[t:, :] = jnp.where(slab >= 4, tail4[...], jnp.zeros_like(tail4))


def split_quarters(staged, mine, by_y, by_x, by_both):
    _, x, core = here()
    q = 2 * x + lax.axis_index("dp")
    mine[...] = staged[core, q]
    for k, out in ((1, by_y), (2, by_x), (3, by_both)):
        out[...] = staged[core, lax.bitwise_xor(q, k)]


def forward_and_outer_kernel(
    own, own_other, halo, halo_other, cw, rw,
    mine, by_y, by_x, by_both, x_out, a_out, b_out, x1_out, dz_out, o_out, ga_out, es_out,
    staged, gin, skin,
):
    t = own.shape[0]
    near = t // 4
    width = x_out.shape[1]
    gated = rw.shape[1]
    _, _, core = here()
    for a, h, c in ((own, halo, core), (own_other, halo_other, 1 - core)):
        rows = pl.ds(pl.multiple_of(c * t, t), t)
        x_out[pl.ds(pl.multiple_of(near + c * t, near), t), :] = h[0:t, :]
        x_out[pl.ds(pl.multiple_of(near + (2 + c) * t, near), t), :] = a[:, 0:width]
        gin[rows, :] = a[:, width : 2 * width]
        skin[rows, :] = a[:, 2 * width :]
    x_out[0:near, :] = jnp.where(core == 1, halo[t:, :], halo_other[t:, :])
    x0 = x_out[near:, :]
    z0 = mm(x_out[0 : 4 * t, :], cw[0, 0:width, :]) + mm(x0, cw[0, width:, :])
    tf = jnp.tanh(z0[:, :gated])
    sg = jax.nn.sigmoid(z0[:, gated:])
    h0 = (tf * sg).astype(BF16)
    a_out[...] = sg * (1.0 - tf * tf)
    b_out[...] = tf * sg * (1.0 - sg)
    x1 = (x0.astype(F32) + mm(h0, rw[0, :, 0:width])).astype(BF16)
    x1_out[...] = x1
    z1 = mm(x1[0 : 2 * t, :], cw[1, 0:width, :]) + mm(x1[2 * t :, :], cw[1, width:, :])
    tf = jnp.tanh(z1[:, :gated])
    sg = jax.nn.sigmoid(z1[:, gated:])
    h1 = (tf * sg).astype(BF16)
    g2 = gin[...]
    sk = skin[...]
    e1 = mm_nt(g2, rw[1, :, 0:width]) + mm_nt(sk, rw[1, :, width:])
    dz1 = jnp.concatenate([e1 * sg * (1.0 - tf * tf), e1 * tf * sg * (1.0 - sg)], axis=1).astype(BF16)
    dz_out[...] = dz1
    dpast = mm_nt(dz1, cw[1, 0:width, :]).astype(BF16)
    ga = g2.astype(F32) + mm_nt(dz1, cw[1, width:, :])
    ga_out[...] = ga
    outer = jnp.concatenate([dpast, ga.astype(BF16)], axis=0)
    o_out[...] = outer
    es_out[...] = mm_nt(sk, rw[0, :, width:])
    skips = jnp.concatenate([mm_tn(h1, sk), mm_tn(h0[2 * t :, :], sk)], axis=1)
    eighth = gated // 8
    for which, part in enumerate((mm_tn(h1, g2), mm_tn(h0, outer), skips)):
        for c in range(2):
            for q in range(4):
                rows = slice((4 * c + q) * eighth, (4 * c + q + 1) * eighth)
                staged[c, q, which * eighth : (which + 1) * eighth, :] = part[rows, :].astype(BF16)
    split_quarters(staged, mine, by_y, by_x, by_both)


def inner_kernel(
    xin, a, b, x1, dz1, outer, es, rw,
    mine, by_y, by_x, by_both, dz,
    staged,
):
    width = xin.shape[1]
    t = dz1.shape[0] // 2
    near = t // 4
    e0 = mm_nt(outer[...], rw[0, :, 0:width])
    e0 = jnp.concatenate([e0[: 2 * t, :], e0[2 * t :, :] + es[...]], axis=0)
    dz0 = jnp.concatenate([e0 * a[...], e0 * b[...]], axis=1).astype(BF16)
    dz[0 : 4 * t, :] = dz0
    dz[4 * t :, :] = jnp.zeros((near, width), BF16)
    half = width // 16
    rows = 2 * half
    blocks = width // rows
    for base, part0, part1 in (
        (0, mm_tn(xin[0 : 4 * t, :], dz0), mm_tn(x1[0 : 2 * t, :], dz1[...])),
        (blocks, mm_tn(xin[near:, :], dz0), mm_tn(x1[2 * t :, :], dz1[...])),
    ):
        for block in range(blocks):
            g, x, c = (base + block) // 4, (base + block) // 2 % 2, (base + block) % 2
            for y in range(2):
                src = slice(block * rows + y * half, block * rows + (y + 1) * half)
                staged[c, 2 * x + y, g, 0:half, :] = part0[src, :].astype(BF16)
                staged[c, 2 * x + y, g, half:, :] = part1[src, :].astype(BF16)
    split_quarters(staged, mine, by_y, by_x, by_both)


def signal_kernel(dz, outer, ga, cw, own_out, back_out, tail_out):
    t = ga.shape[0] // 2
    near = t // 4
    width = ga.shape[1]
    _, _, core = here()
    at = pl.multiple_of(core * t, t)
    long = t + near
    back = dz[pl.ds(at, long), :]
    here_dz = dz[pl.ds(2 * t + at, long), :]
    first = mm_nt(dz[0:near, :], cw[0, 0:width, :]).astype(BF16)
    both = jnp.concatenate([back, here_dz], axis=0)
    wp = mm_nt(both, cw[0, 0:width, :]).astype(BF16)
    wx = mm_nt(both, cw[0, width:, :])
    back_out[...] = (outer[pl.ds(at, t), :].astype(F32) + wx[0:t, :] + wp[near:long, :].astype(F32)).astype(BF16)
    own_out[...] = ga[pl.ds(at, t), :] + wx[long : long + t, :] + wp[long + near :, :].astype(F32)
    tail_out[...] = first


def total_of(*refs):
    total = refs[0][...].astype(F32)
    for ref in refs[1:]:
        total = total + ref[...].astype(F32)
    return total


def sum_xy_kernel(mine, by_y, by_x, by_both, tail, out):
    rows = mine.shape[0]
    out[0:rows, :] = total_of(mine, by_y, by_x, by_both).astype(BF16)
    out[rows:, :] = tail[...]


def sum_z1_kernel(rows, mine, got, out):
    out[0:rows, :] = total_of(mine.at[0:rows, :], got.at[0:rows, :]).astype(BF16)
    out[rows:, :] = got[rows:, :]


def sum_z2_kernel(factor, mine, got, out):
    rows = out.shape[0]
    out[...] = (total_of(mine.at[0:rows, :], got.at[0:rows, :]) * factor).astype(BF16)


def scaled_sum_kernel(factor, *refs):
    refs[-1][...] = (total_of(*refs[:-1]) * factor).astype(BF16)


def groups_kernel(mine, by_y, by_x, by_both, keep, send1, send2, send3, staged):
    g, _, _ = here()
    staged[...] = total_of(mine, by_y, by_x, by_both)
    keep[...] = staged[g]
    for k, out in ((1, send1), (2, send2), (3, send3)):
        out[...] = staged[lax.bitwise_xor(g, k)].astype(BF16)


def in_order_kernel(mine, by_y, by_x, by_both, out):
    _, x, _ = here()
    q = 2 * x + lax.axis_index("dp")
    for k, ref in enumerate((mine, by_y, by_x, by_both)):
        out[lax.bitwise_xor(q, k)] = ref[...]


def finish_conv_kernel(mine, other, conv, done):
    done[...] = jnp.zeros_like(done)
    y = lax.axis_index("dp")
    half = mine.shape[0] // 2
    for ref, at in ((mine, y), (other, 1 - y)):
        rows = pl.ds(pl.multiple_of(at * half, half), half)
        conv[0, rows, :] = ref[0:half, :]
        conv[1, rows, :] = ref[half:, :]


def finish_res_kernel(mine, other, res):
    _, _, core = here()
    eighth = res.shape[1] // 8
    width, part = mine.shape[2], mine.shape[2] // 2
    for ref, c in ((mine, core), (other, 1 - core)):
        for q in range(4):
            rows = pl.ds(pl.multiple_of((4 * c + q) * eighth, eighth), eighth)
            res[1, rows, 0:width] = ref[q, 0:eighth, :]
            res[0, rows, 0:width] = ref[q, eighth : 2 * eighth, :]
            res[1, rows, width:] = ref[q, 2 * eighth :, 0:part]
            res[0, rows, width:] = ref[q, 2 * eighth :, part:]


def finish_signal_kernel(own, come, got1, got2, out, done):
    done[...] = jnp.zeros_like(done)
    t = own.shape[0]
    near = t // 4
    first = got1.shape[0] - near
    g, _, core = here()
    total = own[...] + jnp.where(lax.axis_index("tm") < 14, come[...].astype(F32), 0.0)
    out[0 : t - near, :] = total[0 : t - near, :].astype(BF16)
    last = jnp.where(lax.rem(g, 2) == 0, got1[first:, :], got2[first:, :]).astype(F32)
    last = jnp.where((g < 3) & (core == 1), last, 0.0)
    out[t - near :, :] = (total[t - near :, :] + last).astype(BF16)


def swap(x, distance):
    return lax.ppermute(x, "tm", [(i, i ^ distance) for i in range(16)])


def swap_streams(x):
    return lax.ppermute(x, "dp", [(0, 1), (1, 0)])


def swap_both(x, distance):
    route = [(16 * y + i, 16 * (1 - y) + (i ^ distance)) for y in range(2) for i in range(16)]
    return lax.ppermute(x, ("dp", "tm"), route)


def shift(x, distance):
    return lax.ppermute(x, "tm", [(i, (i + distance) % 16) for i in range(16)])


def body(signal, conv_weight, res_weight, grad_out, skip_cotangent):
    s_dev, t, width = signal.shape
    gated = res_weight.shape[1]
    near = t // 4
    half = width // 16
    res_rows = 3 * gated // 8
    factor = float(s_dev * t * 32) ** (-0.5)

    far = shift(signal[0], 2)
    own, tail = load(
        load_slab_kernel, [(t, 2 * width + skip_cotangent.shape[2]), (near, width)], 0, "load_slab",
        signal[0], grad_out[0], skip_cotangent[0],
    )
    cw, rw = load(
        load_weights_kernel, [conv_weight.shape, res_weight.shape], 4_000_000_000, "load_weights",
        conv_weight, res_weight,
    )
    own_other = swap(own, 1)
    tail4 = shift(tail, 4)
    (halo,) = call(pack_halo_kernel, [shaped((t + near, width))], far, tail4, after=(cw,), flops=5_000_000_000, name="pack_halo")
    halo_other = swap(halo, 1)

    res = shaped((res_rows, width))
    *rsplit, xin, a, b, x1, dz1, outer, ga, es = call(
        forward_and_outer_kernel,
        [
            res, res, res, res,
            shaped((4 * t + near, width)), shaped((4 * t, gated), F32), shaped((4 * t, gated), F32),
            shaped((4 * t, width)), shaped((2 * t, width)), shaped((4 * t, width)), shaped((2 * t, width), F32),
            shaped((2 * t, gated), F32),
        ],
        own, own_other, halo, halo_other, cw, rw,
        scratch=[
            pltpu.VMEM((2, 4, res_rows, width), BF16), pltpu.VMEM((2 * t, width), BF16),
            pltpu.VMEM((2 * t, gated), BF16),
        ],
        vmem=16, name="forward_and_outer",
    )
    piece = (2 * half, width)
    part = shaped((4,) + piece)
    *csplit, dz0 = call(
        inner_kernel, [part, part, part, part, shaped((4 * t + near, width))],
        xin, a, b, x1, dz1, outer, es, rw,
        scratch=[pltpu.VMEM((2, 4, 4) + piece, BF16)], vmem=16, flops=2_000_000_000, name="inner",
    )
    own, back, tail = call(
        signal_kernel, [shaped((t, width), F32), shaped((t, width)), shaped((near, width))],
        dz0, outer, ga, cw, vmem=16, flops=1_000_000_000, name="signal",
    )

    def around(by_y, by_x, by_both):
        both = swap_both(by_both, 2)
        beside = swap(by_x, 2)
        return swap_streams(by_y), beside, both

    rterms = (rsplit[0],) + around(*rsplit[1:])
    cterms = (csplit[0],) + around(*csplit[1:])
    come = shift(back, -2)
    long = shaped((res_rows + near, width))
    (rsum,) = call(sum_xy_kernel, [long], *rterms, tail, after=(csplit[0],), name="res_sum_xy")
    rgot1 = swap(rsum, 4)
    (rsum,) = call(functools.partial(sum_z1_kernel, res_rows), [long], rsum, rgot1, name="res_sum_z1")
    rgot2 = swap(rsum, 8)
    ckeep, *csend = call(
        groups_kernel, [shaped(piece, F32)] + [shaped(piece)] * 3, *cterms,
        after=(rsum,), scratch=[pltpu.VMEM((4,) + piece, F32)], name="conv_groups",
    )
    cgot = [swap(csend[k - 1], 4 * k) for k in (2, 3, 1)]
    input_grad, done = call(
        finish_signal_kernel, [shaped((t, width)), shaped((8, 128), F32)], own, come, rgot1, rgot2,
        after=(ckeep,), name="finish_signal",
    )
    (quarter,) = call(
        functools.partial(sum_z2_kernel, factor), [res], rsum, rgot2, after=(ckeep,), name="res_sum_z2"
    )
    rparts = (quarter, swap_streams(quarter), swap(quarter, 2), swap_both(quarter, 2))
    (mine,) = call(
        functools.partial(scaled_sum_kernel, factor), [shaped(piece)], ckeep, *cgot,
        after=(quarter,), flops=10_000_000_000, name="conv_scaled",
    )
    other = swap_streams(mine)
    (ordered,) = call(in_order_kernel, [shaped((4, res_rows, width))], *rparts, after=(mine, done), name="res_in_order")
    rgot = swap(ordered, 1)
    conv_grad, conv_done = call(
        finish_conv_kernel, [shaped((2,) + piece), shaped((8, 128), F32)], mine, other,
        flops=10_000_000_000, name="finish_conv",
    )
    (res_grad,) = call(
        finish_res_kernel, [shaped(res_weight.shape)], ordered, rgot, after=(conv_done,), name="finish_res"
    )
    return (input_grad.reshape(s_dev, t, width), conv_grad, res_grad)


def solution(mesh):
    in_specs = (P("dp", "tm", None), P(), P(), P("dp", "tm", None), P("dp", "tm", None))
    out_specs = (P("dp", "tm", None), P(None, "tm", None), P())
    chosen = body if mesh.shape["dp"] == 2 and mesh.shape["tm"] == 16 else general_body
    return jax.shard_map(chosen, mesh=mesh, in_specs=in_specs, out_specs=out_specs, check_vma=False)
```

```python
import functools

import jax
import jax.numpy as jnp
from jax import lax
from jax.experimental import pallas as pl
from jax.experimental.pallas import tpu as pltpu
from jax.sharding import PartitionSpec as P

F32 = jnp.float32
BF16 = jnp.bfloat16


def passed_along(block, axis, distance):
    devices = range(lax.axis_size(axis))
    route = [(i - distance, i) for i in devices if i - distance in devices]
    return lax.ppermute(block, axis, route)


def gate_gradients(dh, z, gated):
    tf = jnp.tanh(z[:, :gated])
    sg = jax.nn.sigmoid(z[:, gated:])
    return jnp.concatenate([dh * sg * (1.0 - tf * tf), dh * tf * sg * (1.0 - sg)], axis=1).astype(
        jnp.bfloat16
    )


def reduce_conv(cat_rows, dz):
    piece = lax.psum_scatter(
        lax.dot_general(cat_rows, dz, (((0,), (0,)), ((), ())), preferred_element_type=jnp.float32),
        "tm",
        scatter_dimension=0,
        tiled=True,
    )
    return lax.psum(piece, "dp")


def general_body(signal, conv_weight, res_weight, grad_out, skip_cotangent):
    s_dev, t_dev, width = signal.shape
    gated = res_weight.shape[1]
    near = t_dev // 4
    slabs = lax.axis_size("tm") // 8
    count_rows = s_dev * t_dev
    factor = float(count_rows * lax.axis_size("dp") * lax.axis_size("tm")) ** (-0.5)

    def delayed(x, layer):
        if layer == 0:
            got = passed_along(x[:, t_dev - near :, :], "tm", 1)
            return jnp.concatenate([got, x[:, : t_dev - near, :]], axis=1)
        return passed_along(x, "tm", slabs)

    def shifted_rows(dpast, layer):
        if layer == 0:
            got = passed_along(dpast[:, :near, :], "tm", -1)
            return jnp.concatenate([dpast[:, near:, :], got], axis=1)
        return passed_along(dpast, "tm", -slabs)

    x = signal
    cats = []
    zvals = []
    hvals = []
    for layer in range(2):
        past = delayed(x, layer)
        cat_rows = jnp.concatenate([past, x], axis=2).reshape(count_rows, 2 * width)
        z = jnp.dot(cat_rows, conv_weight[layer], preferred_element_type=jnp.float32)
        h = (jnp.tanh(z[:, :gated]) * jax.nn.sigmoid(z[:, gated:])).astype(jnp.bfloat16)
        cats.append(cat_rows)
        zvals.append(z)
        hvals.append(h)
        if layer == 0:
            resid = jnp.dot(h, res_weight[0][:, :width], preferred_element_type=jnp.float32)
            x = (
                (x.reshape(count_rows, width).astype(jnp.float32) + resid)
                .astype(jnp.bfloat16)
                .reshape(s_dev, t_dev, width)
            )
    grad = grad_out.reshape(count_rows, width).astype(jnp.float32)
    skip_rows = skip_cotangent.reshape(count_rows, -1)
    conv_parts = [None, None]
    res_parts = [None, None]
    dz_kept = [None, None]
    for layer in (1, 0):
        outer = jnp.concatenate([grad.astype(jnp.bfloat16), skip_rows], axis=1)
        dh = lax.dot_general(
            outer, res_weight[layer], (((1,), (1,)), ((), ())), preferred_element_type=jnp.float32
        )
        dz = gate_gradients(dh, zvals[layer], gated)
        wcat = lax.dot_general(
            dz, conv_weight[layer], (((1,), (1,)), ((), ())), preferred_element_type=jnp.float32
        )
        dpast = wcat[:, :width].astype(jnp.bfloat16).reshape(s_dev, t_dev, width)
        moved = shifted_rows(dpast, layer).reshape(count_rows, width)
        grad = grad + wcat[:, width:] + moved.astype(jnp.float32)
        res_local = lax.dot_general(
            hvals[layer], outer, (((0,), (0,)), ((), ())), preferred_element_type=jnp.float32
        )
        dz_kept[layer] = dz
        res_parts[layer] = res_local
    for layer in range(2):
        conv_parts[layer] = reduce_conv(cats[layer], dz_kept[layer])
    res_total = lax.psum(jnp.stack(res_parts), ("dp", "tm"))
    input_grad = grad.astype(jnp.bfloat16).reshape(s_dev, t_dev, width)
    conv_grad = (jnp.stack(conv_parts) * factor).astype(jnp.bfloat16)
    res_grad = (res_total * factor).astype(jnp.bfloat16)
    return (input_grad, conv_grad, res_grad)


def mm(a, b):
    return jnp.dot(a, b, preferred_element_type=F32)


def mm_nt(a, b):
    return lax.dot_general(a, b, (((1,), (1,)), ((), ())), preferred_element_type=F32)


def mm_tn(a, b):
    return lax.dot_general(a, b, (((0,), (0,)), ((), ())), preferred_element_type=F32)


def shaped(shape, dtype=BF16):
    return jax.ShapeDtypeStruct(shape, dtype)


def call(kernel, outs, *args, after=(), scratch=(), flops=0, nbytes=0, vmem=8, name=None):
    n_args = len(args)

    def run(*refs):
        kernel(*refs[:n_args], *refs[n_args + len(after) :])

    in_vmem = pl.BlockSpec(memory_space=pltpu.VMEM)
    return pl.pallas_call(
        run,
        out_shape=outs,
        in_specs=[in_vmem] * n_args + [pl.BlockSpec(memory_space=pl.ANY)] * len(after),
        out_specs=[in_vmem] * len(outs),
        scratch_shapes=list(scratch),
        compiler_params=pltpu.CompilerParams(vmem_limit_bytes=vmem * 1024 * 1024),
        cost_estimate=pl.CostEstimate(flops=flops, bytes_accessed=nbytes, transcendentals=0),
        name=name,
    )(*args, *after)


def place(tm):
    return tm // 4, lax.rem(tm // 2, 2), lax.rem(tm, 2)


def here():
    return place(lax.axis_index("tm"))


def copy_all(pairs, sems):
    copies = [pltpu.make_async_copy(src, dst, sems.at[i]) for i, (src, dst) in enumerate(pairs)]
    for copy in copies:
        copy.start()
    for copy in copies:
        copy.wait()


def load_slab_kernel(sig, grad, skip, own_out, tail_out, sems):
    t, width = sig.shape
    near = tail_out.shape[0]
    pairs = (
        (sig.at[t - near :, :], tail_out),
        (sig, own_out.at[:, 0:width]),
        (grad, own_out.at[:, width : 2 * width]),
        (skip, own_out.at[:, 2 * width :]),
    )
    copy_all(pairs, sems)


def load_weights_kernel(cw, rw, cw_out, rw_out, sems):
    copy_all(((cw, cw_out), (rw, rw_out)), sems)


def load(kernel, outs, flops, name, *arrays):
    in_hbm = [pltpu.with_memory_space_constraint(a, pltpu.HBM) for a in arrays]
    return pl.pallas_call(
        kernel,
        out_shape=[pltpu.VMEM(shape, BF16) for shape in outs],
        in_specs=[pl.BlockSpec(memory_space=pltpu.HBM)] * len(arrays),
        out_specs=[pl.BlockSpec(memory_space=pltpu.VMEM)] * len(outs),
        scratch_shapes=[pltpu.SemaphoreType.DMA((4,))],
        compiler_params=pltpu.CompilerParams(vmem_limit_bytes=8 * 1024 * 1024),
        cost_estimate=pl.CostEstimate(flops=flops, bytes_accessed=0, transcendentals=0),
        name=name,
    )(*in_hbm)


def pack_halo_kernel(far, tail4, out):
    t = far.shape[0]
    slab = lax.axis_index("tm")
    out[0:t, :] = jnp.where(slab >= 2, far[...], jnp.zeros_like(far))
    out[t:, :] = jnp.where(slab >= 4, tail4[...], jnp.zeros_like(tail4))


def split_quarters(staged, mine, by_y, by_x, by_both):
    _, x, core = here()
    q = 2 * x + lax.axis_index("dp")
    mine[...] = staged[core, q]
    for k, out in ((1, by_y), (2, by_x), (3, by_both)):
        out[...] = staged[core, lax.bitwise_xor(q, k)]


def forward_and_outer_kernel(
    own, own_other, halo, halo_other, cw, rw,
    mine, by_y, by_x, by_both, x_out, a_out, b_out, x1_out, dz_out, o_out, ga_out, es_out,
    staged, gin, skin,
):
    t = own.shape[0]
    near = t // 4
    width = x_out.shape[1]
    gated = rw.shape[1]
    _, _, core = here()
    for a, h, c in ((own, halo, core), (own_other, halo_other, 1 - core)):
        rows = pl.ds(pl.multiple_of(c * t, t), t)
        x_out[pl.ds(pl.multiple_of(near + c * t, near), t), :] = h[0:t, :]
        x_out[pl.ds(pl.multiple_of(near + (2 + c) * t, near), t), :] = a[:, 0:width]
        gin[rows, :] = a[:, width : 2 * width]
        skin[rows, :] = a[:, 2 * width :]
    x_out[0:near, :] = jnp.where(core == 1, halo[t:, :], halo_other[t:, :])
    x0 = x_out[near:, :]
    z0 = mm(x_out[0 : 4 * t, :], cw[0, 0:width, :]) + mm(x0, cw[0, width:, :])
    tf = jnp.tanh(z0[:, :gated])
    sg = jax.nn.sigmoid(z0[:, gated:])
    h0 = (tf * sg).astype(BF16)
    a_out[...] = sg * (1.0 - tf * tf)
    b_out[...] = tf * sg * (1.0 - sg)
    x1 = (x0.astype(F32) + mm(h0, rw[0, :, 0:width])).astype(BF16)
    x1_out[...] = x1
    z1 = mm(x1[0 : 2 * t, :], cw[1, 0:width, :]) + mm(x1[2 * t :, :], cw[1, width:, :])
    tf = jnp.tanh(z1[:, :gated])
    sg = jax.nn.sigmoid(z1[:, gated:])
    h1 = (tf * sg).astype(BF16)
    g2 = gin[...]
    sk = skin[...]
    e1 = mm_nt(g2, rw[1, :, 0:width]) + mm_nt(sk, rw[1, :, width:])
    dz1 = jnp.concatenate([e1 * sg * (1.0 - tf * tf), e1 * tf * sg * (1.0 - sg)], axis=1).astype(BF16)
    dz_out[...] = dz1
    dpast = mm_nt(dz1, cw[1, 0:width, :]).astype(BF16)
    ga = g2.astype(F32) + mm_nt(dz1, cw[1, width:, :])
    ga_out[...] = ga
    outer = jnp.concatenate([dpast, ga.astype(BF16)], axis=0)
    o_out[...] = outer
    es_out[...] = mm_nt(sk, rw[0, :, width:])
    skips = jnp.concatenate([mm_tn(h1, sk), mm_tn(h0[2 * t :, :], sk)], axis=1)
    eighth = gated // 8
    for which, part in enumerate((mm_tn(h1, g2), mm_tn(h0, outer), skips)):
        for c in range(2):
            for q in range(4):
                rows = slice((4 * c + q) * eighth, (4 * c + q + 1) * eighth)
                staged[c, q, which * eighth : (which + 1) * eighth, :] = part[rows, :].astype(BF16)
    split_quarters(staged, mine, by_y, by_x, by_both)


def inner_kernel(
    xin, a, b, x1, dz1, outer, es, cw, rw,
    mine, by_y, by_x, by_both, dz, tail,
    staged,
):
    width = xin.shape[1]
    t = dz1.shape[0] // 2
    near = t // 4
    e0 = mm_nt(outer[...], rw[0, :, 0:width])
    e0 = jnp.concatenate([e0[: 2 * t, :], e0[2 * t :, :] + es[...]], axis=0)
    dz0 = jnp.concatenate([e0 * a[...], e0 * b[...]], axis=1).astype(BF16)
    dz[0 : 4 * t, :] = dz0
    dz[4 * t :, :] = jnp.zeros((near, width), BF16)
    tail[...] = mm_nt(dz0[0:near, :], cw[0, 0:width, :]).astype(BF16)
    half = width // 16
    rows = 2 * half
    blocks = width // rows
    for base, part0, part1 in (
        (0, mm_tn(xin[0 : 4 * t, :], dz0), mm_tn(x1[0 : 2 * t, :], dz1[...])),
        (blocks, mm_tn(xin[near:, :], dz0), mm_tn(x1[2 * t :, :], dz1[...])),
    ):
        for block in range(blocks):
            g, x, c = (base + block) // 4, (base + block) // 2 % 2, (base + block) % 2
            for y in range(2):
                src = slice(block * rows + y * half, block * rows + (y + 1) * half)
                staged[c, 2 * x + y, g, 0:half, :] = part0[src, :].astype(BF16)
                staged[c, 2 * x + y, g, half:, :] = part1[src, :].astype(BF16)
    split_quarters(staged, mine, by_y, by_x, by_both)


def signal_kernel(dz, outer, ga, cw, own_out, back_out):
    t = ga.shape[0] // 2
    near = t // 4
    width = ga.shape[1]
    _, _, core = here()
    at = pl.multiple_of(core * t, t)
    long = t + near
    back = dz[pl.ds(at, long), :]
    here_dz = dz[pl.ds(2 * t + at, long), :]
    both = jnp.concatenate([back, here_dz], axis=0)
    wp = mm_nt(both, cw[0, 0:width, :]).astype(BF16)
    wx = mm_nt(both, cw[0, width:, :])
    back_out[...] = (outer[pl.ds(at, t), :].astype(F32) + wx[0:t, :] + wp[near:long, :].astype(F32)).astype(BF16)
    own_out[...] = ga[pl.ds(at, t), :] + wx[long : long + t, :] + wp[long + near :, :].astype(F32)


def total_of(*refs):
    total = refs[0][...].astype(F32)
    for ref in refs[1:]:
        total = total + ref[...].astype(F32)
    return total


def sum_xy_kernel(mine, by_y, by_x, by_both, tail, out):
    rows = mine.shape[0]
    out[0:rows, :] = total_of(mine, by_y, by_x, by_both).astype(BF16)
    out[rows:, :] = tail[...]


def sum_z1_kernel(rows, mine, got, out):
    out[0:rows, :] = total_of(mine.at[0:rows, :], got.at[0:rows, :]).astype(BF16)
    out[rows:, :] = got[rows:, :]


def sum_z2_kernel(factor, mine, got, out):
    rows = out.shape[0]
    out[...] = (total_of(mine.at[0:rows, :], got.at[0:rows, :]) * factor).astype(BF16)


def scaled_sum_kernel(factor, *refs):
    refs[-1][...] = (total_of(*refs[:-1]) * factor).astype(BF16)


def groups_kernel(mine, by_y, by_x, by_both, keep, send1, send2, send3, staged):
    g, _, _ = here()
    staged[...] = total_of(mine, by_y, by_x, by_both)
    keep[...] = staged[g]
    for k, out in ((1, send1), (2, send2), (3, send3)):
        out[...] = staged[lax.bitwise_xor(g, k)].astype(BF16)


def in_order_kernel(mine, by_y, by_x, by_both, out):
    _, x, _ = here()
    q = 2 * x + lax.axis_index("dp")
    for k, ref in enumerate((mine, by_y, by_x, by_both)):
        out[lax.bitwise_xor(q, k)] = ref[...]


def finish_conv_kernel(mine, other, conv, done):
    done[...] = jnp.zeros_like(done)
    y = lax.axis_index("dp")
    half = mine.shape[0] // 2
    for ref, at in ((mine, y), (other, 1 - y)):
        rows = pl.ds(pl.multiple_of(at * half, half), half)
        conv[0, rows, :] = ref[0:half, :]
        conv[1, rows, :] = ref[half:, :]


def finish_kernel(mine, other, own, come, got1, got2, res, grad):
    _, _, core = here()
    eighth = res.shape[1] // 8
    width, part = mine.shape[2], mine.shape[2] // 2
    for ref, c in ((mine, core), (other, 1 - core)):
        for q in range(4):
            rows = pl.ds(pl.multiple_of((4 * c + q) * eighth, eighth), eighth)
            res[1, rows, 0:width] = ref[q, 0:eighth, :]
            res[0, rows, 0:width] = ref[q, eighth : 2 * eighth, :]
            res[1, rows, width:] = ref[q, 2 * eighth :, 0:part]
            res[0, rows, width:] = ref[q, 2 * eighth :, part:]
    t = own.shape[0]
    near = t // 4
    first = got1.shape[0] - near
    g, _, _ = here()
    total = own[...] + jnp.where(lax.axis_index("tm") < 14, come[...].astype(F32), 0.0)
    grad[0 : t - near, :] = total[0 : t - near, :].astype(BF16)
    last = jnp.where(lax.rem(g, 2) == 0, got1[first:, :], got2[first:, :]).astype(F32)
    last = jnp.where((g < 3) & (core == 1), last, 0.0)
    grad[t - near :, :] = (total[t - near :, :] + last).astype(BF16)


def hold_kernel(a, out):
    out[...] = a[...]


def swap(x, distance):
    return lax.ppermute(x, "tm", [(i, i ^ distance) for i in range(16)])


def swap_streams(x):
    return lax.ppermute(x, "dp", [(0, 1), (1, 0)])


def swap_both(x, distance):
    route = [(16 * y + i, 16 * (1 - y) + (i ^ distance)) for y in range(2) for i in range(16)]
    return lax.ppermute(x, ("dp", "tm"), route)


def shift(x, distance):
    return lax.ppermute(x, "tm", [(i, (i + distance) % 16) for i in range(16)])


def body(signal, conv_weight, res_weight, grad_out, skip_cotangent):
    s_dev, t, width = signal.shape
    gated = res_weight.shape[1]
    near = t // 4
    half = width // 16
    res_rows = 3 * gated // 8
    factor = float(s_dev * t * 32) ** (-0.5)

    far = shift(signal[0], 2)
    own, tail = load(
        load_slab_kernel, [(t, 2 * width + skip_cotangent.shape[2]), (near, width)], 0, "load_slab",
        signal[0], grad_out[0], skip_cotangent[0],
    )
    cw, rw = load(
        load_weights_kernel, [conv_weight.shape, res_weight.shape], 4_000_000_000, "load_weights",
        conv_weight, res_weight,
    )
    own_other = swap(own, 1)
    tail4 = shift(tail, 4)
    (halo,) = call(pack_halo_kernel, [shaped((t + near, width))], far, tail4, after=(cw,), flops=5_000_000_000, name="pack_halo")
    halo_other = swap(halo, 1)

    res = shaped((res_rows, width))
    *rsplit, xin, a, b, x1, dz1, outer, ga, es = call(
        forward_and_outer_kernel,
        [
            res, res, res, res,
            shaped((4 * t + near, width)), shaped((4 * t, gated), F32), shaped((4 * t, gated), F32),
            shaped((4 * t, width)), shaped((2 * t, width)), shaped((4 * t, width)), shaped((2 * t, width), F32),
            shaped((2 * t, gated), F32),
        ],
        own, own_other, halo, halo_other, cw, rw,
        scratch=[
            pltpu.VMEM((2, 4, res_rows, width), BF16), pltpu.VMEM((2 * t, width), BF16),
            pltpu.VMEM((2 * t, gated), BF16),
        ],
        vmem=16, name="forward_and_outer",
    )
    piece = (2 * half, width)
    part = shaped((4,) + piece)
    *csplit, dz0, tail = call(
        inner_kernel, [part, part, part, part, shaped((4 * t + near, width)), shaped((near, width))],
        xin, a, b, x1, dz1, outer, es, cw, rw,
        scratch=[pltpu.VMEM((2, 4, 4) + piece, BF16)], vmem=16, flops=2_000_000_000, name="inner",
    )
    def around(by_y, by_x, by_both):
        both = swap_both(by_both, 2)
        beside = swap(by_x, 2)
        return swap_streams(by_y), beside, both

    rterms = (rsplit[0],) + around(*rsplit[1:])
    cterms = (csplit[0],) + around(*csplit[1:])
    long = shaped((res_rows + near, width))
    (rsum,) = call(sum_xy_kernel, [long], *rterms, tail, after=(csplit[0],), name="res_sum_xy")
    rgot1 = swap(rsum, 4)
    own, back = call(
        signal_kernel, [shaped((t, width), F32), shaped((t, width))], dz0, outer, ga, cw,
        after=(rsum,), vmem=16, flops=1_000_000_000, name="signal",
    )
    (rsum,) = call(functools.partial(sum_z1_kernel, res_rows), [long], rsum, rgot1, name="res_sum_z1")
    rgot2 = swap(rsum, 8)
    ckeep, *csend = call(
        groups_kernel, [shaped(piece, F32)] + [shaped(piece)] * 3, *cterms,
        after=(rsum, back), scratch=[pltpu.VMEM((4,) + piece, F32)], name="conv_groups",
    )
    cgot = [swap(csend[k - 1], 4 * k) for k in (2, 3, 1)]
    (quarter,) = call(
        functools.partial(sum_z2_kernel, factor), [res], rsum, rgot2, after=(ckeep,), name="res_sum_z2"
    )
    rparts = (quarter, swap_streams(quarter), swap(quarter, 2), swap_both(quarter, 2))
    (back,) = call(hold_kernel, [shaped((t, width))], back, after=(ckeep,), name="hold")
    come = shift(back, -2)
    (mine,) = call(
        functools.partial(scaled_sum_kernel, factor), [shaped(piece)], ckeep, *cgot,
        after=(quarter,), flops=10_000_000_000, name="conv_scaled",
    )
    other = swap_streams(mine)
    (ordered,) = call(in_order_kernel, [shaped((4, res_rows, width))], *rparts, after=(mine,), name="res_in_order")
    rgot = swap(ordered, 1)
    conv_grad, conv_done = call(
        finish_conv_kernel, [shaped((2,) + piece), shaped((8, 128), F32)], mine, other,
        flops=10_000_000_000, name="finish_conv",
    )
    res_grad, input_grad = call(
        finish_kernel, [shaped(res_weight.shape), shaped((t, width))], ordered, rgot, own, come, rgot1, rgot2,
        after=(conv_done,), name="finish",
    )
    return (input_grad.reshape(s_dev, t, width), conv_grad, res_grad)


def solution(mesh):
    in_specs = (P("dp", "tm", None), P(), P(), P("dp", "tm", None), P("dp", "tm", None))
    out_specs = (P("dp", "tm", None), P(None, "tm", None), P())
    chosen = body if mesh.shape["dp"] == 2 and mesh.shape["tm"] == 16 else general_body
    return jax.shard_map(chosen, mesh=mesh, in_specs=in_specs, out_specs=out_specs, check_vma=False)
```

```python
import functools

import jax
import jax.numpy as jnp
from jax import lax
from jax.experimental import pallas as pl
from jax.experimental.pallas import tpu as pltpu
from jax.sharding import PartitionSpec as P

F32 = jnp.float32
BF16 = jnp.bfloat16


def passed_along(block, axis, distance):
    devices = range(lax.axis_size(axis))
    route = [(i - distance, i) for i in devices if i - distance in devices]
    return lax.ppermute(block, axis, route)


def gate_gradients(dh, z, gated):
    tf = jnp.tanh(z[:, :gated])
    sg = jax.nn.sigmoid(z[:, gated:])
    return jnp.concatenate([dh * sg * (1.0 - tf * tf), dh * tf * sg * (1.0 - sg)], axis=1).astype(
        jnp.bfloat16
    )


def reduce_conv(cat_rows, dz):
    piece = lax.psum_scatter(
        lax.dot_general(cat_rows, dz, (((0,), (0,)), ((), ())), preferred_element_type=jnp.float32),
        "tm",
        scatter_dimension=0,
        tiled=True,
    )
    return lax.psum(piece, "dp")


def general_body(signal, conv_weight, res_weight, grad_out, skip_cotangent):
    s_dev, t_dev, width = signal.shape
    gated = res_weight.shape[1]
    near = t_dev // 4
    slabs = lax.axis_size("tm") // 8
    count_rows = s_dev * t_dev
    factor = float(count_rows * lax.axis_size("dp") * lax.axis_size("tm")) ** (-0.5)

    def delayed(x, layer):
        if layer == 0:
            got = passed_along(x[:, t_dev - near :, :], "tm", 1)
            return jnp.concatenate([got, x[:, : t_dev - near, :]], axis=1)
        return passed_along(x, "tm", slabs)

    def shifted_rows(dpast, layer):
        if layer == 0:
            got = passed_along(dpast[:, :near, :], "tm", -1)
            return jnp.concatenate([dpast[:, near:, :], got], axis=1)
        return passed_along(dpast, "tm", -slabs)

    x = signal
    cats = []
    zvals = []
    hvals = []
    for layer in range(2):
        past = delayed(x, layer)
        cat_rows = jnp.concatenate([past, x], axis=2).reshape(count_rows, 2 * width)
        z = jnp.dot(cat_rows, conv_weight[layer], preferred_element_type=jnp.float32)
        h = (jnp.tanh(z[:, :gated]) * jax.nn.sigmoid(z[:, gated:])).astype(jnp.bfloat16)
        cats.append(cat_rows)
        zvals.append(z)
        hvals.append(h)
        if layer == 0:
            resid = jnp.dot(h, res_weight[0][:, :width], preferred_element_type=jnp.float32)
            x = (
                (x.reshape(count_rows, width).astype(jnp.float32) + resid)
                .astype(jnp.bfloat16)
                .reshape(s_dev, t_dev, width)
            )
    grad = grad_out.reshape(count_rows, width).astype(jnp.float32)
    skip_rows = skip_cotangent.reshape(count_rows, -1)
    conv_parts = [None, None]
    res_parts = [None, None]
    dz_kept = [None, None]
    for layer in (1, 0):
        outer = jnp.concatenate([grad.astype(jnp.bfloat16), skip_rows], axis=1)
        dh = lax.dot_general(
            outer, res_weight[layer], (((1,), (1,)), ((), ())), preferred_element_type=jnp.float32
        )
        dz = gate_gradients(dh, zvals[layer], gated)
        wcat = lax.dot_general(
            dz, conv_weight[layer], (((1,), (1,)), ((), ())), preferred_element_type=jnp.float32
        )
        dpast = wcat[:, :width].astype(jnp.bfloat16).reshape(s_dev, t_dev, width)
        moved = shifted_rows(dpast, layer).reshape(count_rows, width)
        grad = grad + wcat[:, width:] + moved.astype(jnp.float32)
        res_local = lax.dot_general(
            hvals[layer], outer, (((0,), (0,)), ((), ())), preferred_element_type=jnp.float32
        )
        dz_kept[layer] = dz
        res_parts[layer] = res_local
    for layer in range(2):
        conv_parts[layer] = reduce_conv(cats[layer], dz_kept[layer])
    res_total = lax.psum(jnp.stack(res_parts), ("dp", "tm"))
    input_grad = grad.astype(jnp.bfloat16).reshape(s_dev, t_dev, width)
    conv_grad = (jnp.stack(conv_parts) * factor).astype(jnp.bfloat16)
    res_grad = (res_total * factor).astype(jnp.bfloat16)
    return (input_grad, conv_grad, res_grad)


def mm(a, b):
    return jnp.dot(a, b, preferred_element_type=F32)


def mm_nt(a, b):
    return lax.dot_general(a, b, (((1,), (1,)), ((), ())), preferred_element_type=F32)


def mm_tn(a, b):
    return lax.dot_general(a, b, (((0,), (0,)), ((), ())), preferred_element_type=F32)


def shaped(shape, dtype=BF16):
    return jax.ShapeDtypeStruct(shape, dtype)


def call(kernel, outs, *args, after=(), scratch=(), flops=0, nbytes=0, vmem=8, name=None):
    n_args = len(args)

    def run(*refs):
        kernel(*refs[:n_args], *refs[n_args + len(after) :])

    in_vmem = pl.BlockSpec(memory_space=pltpu.VMEM)
    return pl.pallas_call(
        run,
        out_shape=outs,
        in_specs=[in_vmem] * n_args + [pl.BlockSpec(memory_space=pl.ANY)] * len(after),
        out_specs=[in_vmem] * len(outs),
        scratch_shapes=list(scratch),
        compiler_params=pltpu.CompilerParams(vmem_limit_bytes=vmem * 1024 * 1024),
        cost_estimate=pl.CostEstimate(flops=flops, bytes_accessed=nbytes, transcendentals=0),
        name=name,
    )(*args, *after)


def place(tm):
    return tm // 4, lax.rem(tm // 2, 2), lax.rem(tm, 2)


def here():
    return place(lax.axis_index("tm"))


def copy_all(pairs, sems):
    copies = [pltpu.make_async_copy(src, dst, sems.at[i]) for i, (src, dst) in enumerate(pairs)]
    for copy in copies:
        copy.start()
    for copy in copies:
        copy.wait()


def load_slab_kernel(sig, grad, skip, own_out, tail_out, sems):
    t, width = sig.shape
    near = tail_out.shape[0]
    pairs = (
        (sig.at[t - near :, :], tail_out),
        (sig, own_out.at[:, 0:width]),
        (grad, own_out.at[:, width : 2 * width]),
        (skip, own_out.at[:, 2 * width :]),
    )
    copy_all(pairs, sems)


def load_weights_kernel(cw, rw, cw_out, rw_out, sems):
    copy_all(((cw, cw_out), (rw, rw_out)), sems)


def load(kernel, outs, flops, name, *arrays):
    in_hbm = [pltpu.with_memory_space_constraint(a, pltpu.HBM) for a in arrays]
    return pl.pallas_call(
        kernel,
        out_shape=[pltpu.VMEM(shape, BF16) for shape in outs],
        in_specs=[pl.BlockSpec(memory_space=pltpu.HBM)] * len(arrays),
        out_specs=[pl.BlockSpec(memory_space=pltpu.VMEM)] * len(outs),
        scratch_shapes=[pltpu.SemaphoreType.DMA((4,))],
        compiler_params=pltpu.CompilerParams(vmem_limit_bytes=8 * 1024 * 1024),
        cost_estimate=pl.CostEstimate(flops=flops, bytes_accessed=0, transcendentals=0),
        name=name,
    )(*in_hbm)


def pack_halo_kernel(far, tail4, out):
    t = far.shape[0]
    slab = lax.axis_index("tm")
    out[0:t, :] = jnp.where(slab >= 2, far[...], jnp.zeros_like(far))
    out[t:, :] = jnp.where(slab >= 4, tail4[...], jnp.zeros_like(tail4))


def split_quarters(staged, mine, by_y, by_x, by_both):
    _, x, _ = here()
    q = 2 * x + lax.axis_index("dp")
    mine[...] = staged[q]
    for k, out in ((1, by_y), (2, by_x), (3, by_both)):
        out[...] = staged[lax.bitwise_xor(q, k)]


def columns_of(a, core, block):
    count = a.shape[1] // block
    return jnp.where(
        core == 0,
        jnp.concatenate([a[:, i * block : (i + 1) * block] for i in range(0, count, 2)], axis=1),
        jnp.concatenate([a[:, i * block : (i + 1) * block] for i in range(1, count, 2)], axis=1),
    )


def own_kernel(own, own_other, cw, rw, sig, gin, skin, z_out, e_out, es_out):
    t = own.shape[0]
    near = t // 4
    width = sig.shape[1]
    _, _, core = here()
    for a, c in ((own, core), (own_other, 1 - core)):
        rows = pl.ds(pl.multiple_of(c * t, t), t)
        sig[rows, :] = a[:, 0:width]
        gin[rows, :] = a[:, width : 2 * width]
        skin[rows, :] = a[:, 2 * width :]
    z = mm(sig[...], cw[0, width:, :])
    z_out[0:near, :] = z[0:near, :]
    z_out[near:, :] = z[near:, :] + mm(sig[...], cw[0, 0:width, :])[: 2 * t - near, :]
    e_out[...] = mm_nt(gin[...], rw[1, :, 0:width]) + mm_nt(skin[...], rw[1, :, width:])
    es_out[...] = mm_nt(skin[...], rw[0, :, width:])


def forward_and_outer_kernel(
    sig, z_own, e1, gin, skin, halo, halo_other, cw, rw,
    mine, by_y, by_x, by_both, x_out, a_out, b_out, x1_out, dz_out, o_out, ga_out,
    staged,
):
    t = sig.shape[0] // 2
    near = t // 4
    width = x_out.shape[1]
    gated = rw.shape[1]
    _, _, core = here()
    for h, c in ((halo, core), (halo_other, 1 - core)):
        x_out[pl.ds(pl.multiple_of(near + c * t, near), t), :] = h[0:t, :]
    x_out[near + 2 * t :, :] = sig[...]
    x_out[0:near, :] = jnp.where(core == 1, halo[t:, :], halo_other[t:, :])
    x0 = x_out[near:, :]
    behind = mm(x_out[0 : 2 * t + near, :], cw[0, 0:width, :])
    z0 = jnp.concatenate(
        [
            behind[0 : 2 * t, :] + mm(x_out[near : 2 * t + near, :], cw[0, width:, :]),
            z_own[0:near, :] + behind[2 * t :, :],
            z_own[near:, :],
        ],
        axis=0,
    )
    tf = jnp.tanh(z0[:, :gated])
    sg = jax.nn.sigmoid(z0[:, gated:])
    h0 = (tf * sg).astype(BF16)
    a_out[...] = sg * (1.0 - tf * tf)
    b_out[...] = tf * sg * (1.0 - sg)
    x1 = (x0.astype(F32) + mm(h0, rw[0, :, 0:width])).astype(BF16)
    x1_out[...] = x1
    z1 = mm(x1[0 : 2 * t, :], cw[1, 0:width, :]) + mm(x1[2 * t :, :], cw[1, width:, :])
    tf = jnp.tanh(z1[:, :gated])
    sg = jax.nn.sigmoid(z1[:, gated:])
    h1 = (tf * sg).astype(BF16)
    g2 = gin[...]
    sk = skin[...]
    e = e1[...]
    dz1 = jnp.concatenate([e * sg * (1.0 - tf * tf), e * tf * sg * (1.0 - sg)], axis=1).astype(BF16)
    dz_out[...] = dz1
    dpast = mm_nt(dz1, cw[1, 0:width, :]).astype(BF16)
    ga = g2.astype(F32) + mm_nt(dz1, cw[1, width:, :])
    ga_out[...] = ga
    outer = jnp.concatenate([dpast, ga.astype(BF16)], axis=0)
    o_out[...] = outer
    part = gated // 2
    mine_h0 = jnp.where(core == 0, h0[:, :part], h0[:, part:])
    mine_h1 = jnp.where(core == 0, h1[:, :part], h1[:, part:])
    skips = jnp.concatenate([mm_tn(mine_h1, sk), mm_tn(mine_h0[2 * t :, :], sk)], axis=1)
    eighth = gated // 8
    for which, part in enumerate((mm_tn(mine_h1, g2), mm_tn(mine_h0, outer), skips)):
        for q in range(4):
            staged[q, which * eighth : (which + 1) * eighth, :] = part[q * eighth : (q + 1) * eighth, :].astype(BF16)
    split_quarters(staged, mine, by_y, by_x, by_both)


def inner_kernel(
    xin, a, b, x1, dz1, outer, es, cw, rw,
    mine, by_y, by_x, by_both, dz, tail,
    staged, mine_in,
):
    width = xin.shape[1]
    t = dz1.shape[0] // 2
    near = t // 4
    e0 = mm_nt(outer[...], rw[0, :, 0:width])
    e0 = jnp.concatenate([e0[: 2 * t, :], e0[2 * t :, :] + es[...]], axis=0)
    dz0 = jnp.concatenate([e0 * a[...], e0 * b[...]], axis=1).astype(BF16)
    dz[0 : 4 * t, :] = dz0
    dz[4 * t :, :] = jnp.zeros((near, width), BF16)
    tail[...] = mm_nt(dz0[0:near, :], cw[0, 0:width, :]).astype(BF16)
    half = width // 16
    rows = 2 * half
    _, _, core = here()
    mine_in[...] = columns_of(xin[...], core, rows)
    mine_x1 = columns_of(x1[...], core, rows)
    pairs = width // rows // 2
    for base, part0, part1 in (
        (0, mm_tn(mine_in[0 : 4 * t, :], dz0), mm_tn(mine_x1[0 : 2 * t, :], dz1[...])),
        (pairs, mm_tn(mine_in[near:, :], dz0), mm_tn(mine_x1[2 * t :, :], dz1[...])),
    ):
        for block in range(pairs):
            g, x = (base + block) // 2, (base + block) % 2
            for y in range(2):
                src = slice(block * rows + y * half, block * rows + (y + 1) * half)
                staged[2 * x + y, g, 0:half, :] = part0[src, :].astype(BF16)
                staged[2 * x + y, g, half:, :] = part1[src, :].astype(BF16)
    split_quarters(staged, mine, by_y, by_x, by_both)


def signal_kernel(dz, outer, ga, cw, own_out, back_out):
    t = ga.shape[0] // 2
    near = t // 4
    width = ga.shape[1]
    _, _, core = here()
    at = pl.multiple_of(core * t, t)
    long = t + near
    back = dz[pl.ds(at, long), :]
    here_dz = dz[pl.ds(2 * t + at, long), :]
    both = jnp.concatenate([back, here_dz], axis=0)
    wp = mm_nt(both, cw[0, 0:width, :]).astype(BF16)
    wx = mm_nt(both, cw[0, width:, :])
    back_out[...] = (outer[pl.ds(at, t), :].astype(F32) + wx[0:t, :] + wp[near:long, :].astype(F32)).astype(BF16)
    own_out[...] = ga[pl.ds(at, t), :] + wx[long : long + t, :] + wp[long + near :, :].astype(F32)


def total_of(*refs):
    total = refs[0][...].astype(F32)
    for ref in refs[1:]:
        total = total + ref[...].astype(F32)
    return total


def sum_xy_kernel(mine, by_y, by_x, by_both, tail, out):
    rows = mine.shape[0]
    out[0:rows, :] = total_of(mine, by_y, by_x, by_both).astype(BF16)
    out[rows:, :] = tail[...]


def sum_z1_kernel(rows, mine, got, out):
    out[0:rows, :] = total_of(mine.at[0:rows, :], got.at[0:rows, :]).astype(BF16)
    out[rows:, :] = got[rows:, :]


def sum_z2_kernel(factor, mine, got, out):
    rows = out.shape[0]
    out[...] = (total_of(mine.at[0:rows, :], got.at[0:rows, :]) * factor).astype(BF16)


def scaled_sum_kernel(factor, *refs):
    refs[-1][...] = (total_of(*refs[:-1]) * factor).astype(BF16)


def groups_kernel(mine, by_y, by_x, by_both, keep, send1, send2, send3, staged):
    g, _, _ = here()
    staged[...] = total_of(mine, by_y, by_x, by_both)
    keep[...] = staged[g]
    for k, out in ((1, send1), (2, send2), (3, send3)):
        out[...] = staged[lax.bitwise_xor(g, k)].astype(BF16)


def in_order_kernel(mine, by_y, by_x, by_both, out):
    _, x, _ = here()
    q = 2 * x + lax.axis_index("dp")
    for k, ref in enumerate((mine, by_y, by_x, by_both)):
        out[lax.bitwise_xor(q, k)] = ref[...]


def finish_conv_kernel(mine, other, conv, done):
    done[...] = jnp.zeros_like(done)
    y = lax.axis_index("dp")
    half = mine.shape[0] // 2
    for ref, at in ((mine, y), (other, 1 - y)):
        rows = pl.ds(pl.multiple_of(at * half, half), half)
        conv[0, rows, :] = ref[0:half, :]
        conv[1, rows, :] = ref[half:, :]


def finish_kernel(mine, other, own, come, got1, got2, res, grad):
    _, _, core = here()
    eighth = res.shape[1] // 8
    width, part = mine.shape[2], mine.shape[2] // 2
    for ref, c in ((mine, core), (other, 1 - core)):
        for q in range(4):
            rows = pl.ds(pl.multiple_of((4 * c + q) * eighth, eighth), eighth)
            res[1, rows, 0:width] = ref[q, 0:eighth, :]
            res[0, rows, 0:width] = ref[q, eighth : 2 * eighth, :]
            res[1, rows, width:] = ref[q, 2 * eighth :, 0:part]
            res[0, rows, width:] = ref[q, 2 * eighth :, part:]
    t = own.shape[0]
    near = t // 4
    first = got1.shape[0] - near
    g, _, _ = here()
    total = own[...] + jnp.where(lax.axis_index("tm") < 14, come[...].astype(F32), 0.0)
    grad[0 : t - near, :] = total[0 : t - near, :].astype(BF16)
    last = jnp.where(lax.rem(g, 2) == 0, got1[first:, :], got2[first:, :]).astype(F32)
    last = jnp.where((g < 3) & (core == 1), last, 0.0)
    grad[t - near :, :] = (total[t - near :, :] + last).astype(BF16)


def hold_kernel(a, out):
    out[...] = a[...]


def swap(x, distance):
    return lax.ppermute(x, "tm", [(i, i ^ distance) for i in range(16)])


def swap_streams(x):
    return lax.ppermute(x, "dp", [(0, 1), (1, 0)])


def swap_both(x, distance):
    route = [(16 * y + i, 16 * (1 - y) + (i ^ distance)) for y in range(2) for i in range(16)]
    return lax.ppermute(x, ("dp", "tm"), route)


def shift(x, distance):
    return lax.ppermute(x, "tm", [(i, (i + distance) % 16) for i in range(16)])


def body(signal, conv_weight, res_weight, grad_out, skip_cotangent):
    s_dev, t, width = signal.shape
    gated = res_weight.shape[1]
    near = t // 4
    half = width // 16
    res_rows = 3 * gated // 8
    factor = float(s_dev * t * 32) ** (-0.5)

    far = shift(signal[0], 2)
    own, tail = load(
        load_slab_kernel, [(t, 2 * width + skip_cotangent.shape[2]), (near, width)], 0, "load_slab",
        signal[0], grad_out[0], skip_cotangent[0],
    )
    cw, rw = load(
        load_weights_kernel, [conv_weight.shape, res_weight.shape], 4_000_000_000, "load_weights",
        conv_weight, res_weight,
    )
    own_other = swap(own, 1)
    tail4 = shift(tail, 4)
    (halo,) = call(pack_halo_kernel, [shaped((t + near, width))], far, tail4, after=(cw,), flops=5_000_000_000, name="pack_halo")
    halo_other = swap(halo, 1)

    res = shaped((res_rows, width))
    sig, gin, skin, z_own, e1, es = call(
        own_kernel,
        [
            shaped((2 * t, width)), shaped((2 * t, width)), shaped((2 * t, gated)), shaped((2 * t, 2 * gated), F32),
            shaped((2 * t, gated), F32), shaped((2 * t, gated), F32),
        ],
        own, own_other, cw, rw, vmem=16, flops=2_000_000_000, name="own",
    )
    *rsplit, xin, a, b, x1, dz1, outer, ga = call(
        forward_and_outer_kernel,
        [
            res, res, res, res,
            shaped((4 * t + near, width)), shaped((4 * t, gated), F32), shaped((4 * t, gated), F32),
            shaped((4 * t, width)), shaped((2 * t, width)), shaped((4 * t, width)), shaped((2 * t, width), F32),
        ],
        sig, z_own, e1, gin, skin, halo, halo_other, cw, rw,
        scratch=[pltpu.VMEM((4, res_rows, width), BF16)], vmem=16, name="forward_and_outer",
    )
    piece = (2 * half, width)
    part = shaped((4,) + piece)
    *csplit, dz0, tail = call(
        inner_kernel, [part, part, part, part, shaped((4 * t + near, width)), shaped((near, width))],
        xin, a, b, x1, dz1, outer, es, cw, rw,
        scratch=[pltpu.VMEM((4, 4) + piece, BF16), pltpu.VMEM((4 * t + near, width // 2), BF16)], vmem=16, flops=2_000_000_000, name="inner",
    )
    def around(by_y, by_x, by_both):
        both = swap_both(by_both, 2)
        beside = swap(by_x, 2)
        return swap_streams(by_y), beside, both

    rterms = (rsplit[0],) + around(*rsplit[1:])
    cterms = (csplit[0],) + around(*csplit[1:])
    long = shaped((res_rows + near, width))
    (rsum,) = call(sum_xy_kernel, [long], *rterms, tail, after=(csplit[0],), name="res_sum_xy")
    rgot1 = swap(rsum, 4)
    own, back = call(
        signal_kernel, [shaped((t, width), F32), shaped((t, width))], dz0, outer, ga, cw,
        after=(rsum,), vmem=16, flops=1_000_000_000, name="signal",
    )
    (rsum,) = call(functools.partial(sum_z1_kernel, res_rows), [long], rsum, rgot1, name="res_sum_z1")
    rgot2 = swap(rsum, 8)
    ckeep, *csend = call(
        groups_kernel, [shaped(piece, F32)] + [shaped(piece)] * 3, *cterms,
        after=(rsum, back), scratch=[pltpu.VMEM((4,) + piece, F32)], name="conv_groups",
    )
    cgot = [swap(csend[k - 1], 4 * k) for k in (2, 3, 1)]
    (quarter,) = call(
        functools.partial(sum_z2_kernel, factor), [res], rsum, rgot2, after=(ckeep,), name="res_sum_z2"
    )
    rparts = (quarter, swap_streams(quarter), swap(quarter, 2), swap_both(quarter, 2))
    (back,) = call(hold_kernel, [shaped((t, width))], back, after=(ckeep,), name="hold")
    come = shift(back, -2)
    (mine,) = call(
        functools.partial(scaled_sum_kernel, factor), [shaped(piece)], ckeep, *cgot,
        after=(quarter,), flops=10_000_000_000, name="conv_scaled",
    )
    other = swap_streams(mine)
    (ordered,) = call(in_order_kernel, [shaped((4, res_rows, width))], *rparts, after=(mine,), name="res_in_order")
    rgot = swap(ordered, 1)
    conv_grad, conv_done = call(
        finish_conv_kernel, [shaped((2,) + piece), shaped((8, 128), F32)], mine, other,
        flops=10_000_000_000, name="finish_conv",
    )
    res_grad, input_grad = call(
        finish_kernel, [shaped(res_weight.shape), shaped((t, width))], ordered, rgot, own, come, rgot1, rgot2,
        after=(conv_done,), name="finish",
    )
    return (input_grad.reshape(s_dev, t, width), conv_grad, res_grad)


def solution(mesh):
    in_specs = (P("dp", "tm", None), P(), P(), P("dp", "tm", None), P("dp", "tm", None))
    out_specs = (P("dp", "tm", None), P(None, "tm", None), P())
    chosen = body if mesh.shape["dp"] == 2 and mesh.shape["tm"] == 16 else general_body
    return jax.shard_map(chosen, mesh=mesh, in_specs=in_specs, out_specs=out_specs, check_vma=False)
```

```python
import functools

import jax
import jax.numpy as jnp
from jax import lax
from jax.experimental import pallas as pl
from jax.experimental.pallas import tpu as pltpu
from jax.sharding import PartitionSpec as P

F32 = jnp.float32
BF16 = jnp.bfloat16


def passed_along(block, axis, distance):
    devices = range(lax.axis_size(axis))
    route = [(i - distance, i) for i in devices if i - distance in devices]
    return lax.ppermute(block, axis, route)


def gate_gradients(dh, z, gated):
    tf = jnp.tanh(z[:, :gated])
    sg = jax.nn.sigmoid(z[:, gated:])
    return jnp.concatenate([dh * sg * (1.0 - tf * tf), dh * tf * sg * (1.0 - sg)], axis=1).astype(
        jnp.bfloat16
    )


def reduce_conv(cat_rows, dz):
    piece = lax.psum_scatter(
        lax.dot_general(cat_rows, dz, (((0,), (0,)), ((), ())), preferred_element_type=jnp.float32),
        "tm",
        scatter_dimension=0,
        tiled=True,
    )
    return lax.psum(piece, "dp")


def general_body(signal, conv_weight, res_weight, grad_out, skip_cotangent):
    s_dev, t_dev, width = signal.shape
    gated = res_weight.shape[1]
    near = t_dev // 4
    slabs = lax.axis_size("tm") // 8
    count_rows = s_dev * t_dev
    factor = float(count_rows * lax.axis_size("dp") * lax.axis_size("tm")) ** (-0.5)

    def delayed(x, layer):
        if layer == 0:
            got = passed_along(x[:, t_dev - near :, :], "tm", 1)
            return jnp.concatenate([got, x[:, : t_dev - near, :]], axis=1)
        return passed_along(x, "tm", slabs)

    def shifted_rows(dpast, layer):
        if layer == 0:
            got = passed_along(dpast[:, :near, :], "tm", -1)
            return jnp.concatenate([dpast[:, near:, :], got], axis=1)
        return passed_along(dpast, "tm", -slabs)

    x = signal
    cats = []
    zvals = []
    hvals = []
    for layer in range(2):
        past = delayed(x, layer)
        cat_rows = jnp.concatenate([past, x], axis=2).reshape(count_rows, 2 * width)
        z = jnp.dot(cat_rows, conv_weight[layer], preferred_element_type=jnp.float32)
        h = (jnp.tanh(z[:, :gated]) * jax.nn.sigmoid(z[:, gated:])).astype(jnp.bfloat16)
        cats.append(cat_rows)
        zvals.append(z)
        hvals.append(h)
        if layer == 0:
            resid = jnp.dot(h, res_weight[0][:, :width], preferred_element_type=jnp.float32)
            x = (
                (x.reshape(count_rows, width).astype(jnp.float32) + resid)
                .astype(jnp.bfloat16)
                .reshape(s_dev, t_dev, width)
            )
    grad = grad_out.reshape(count_rows, width).astype(jnp.float32)
    skip_rows = skip_cotangent.reshape(count_rows, -1)
    conv_parts = [None, None]
    res_parts = [None, None]
    dz_kept = [None, None]
    for layer in (1, 0):
        outer = jnp.concatenate([grad.astype(jnp.bfloat16), skip_rows], axis=1)
        dh = lax.dot_general(
            outer, res_weight[layer], (((1,), (1,)), ((), ())), preferred_element_type=jnp.float32
        )
        dz = gate_gradients(dh, zvals[layer], gated)
        wcat = lax.dot_general(
            dz, conv_weight[layer], (((1,), (1,)), ((), ())), preferred_element_type=jnp.float32
        )
        dpast = wcat[:, :width].astype(jnp.bfloat16).reshape(s_dev, t_dev, width)
        moved = shifted_rows(dpast, layer).reshape(count_rows, width)
        grad = grad + wcat[:, width:] + moved.astype(jnp.float32)
        res_local = lax.dot_general(
            hvals[layer], outer, (((0,), (0,)), ((), ())), preferred_element_type=jnp.float32
        )
        dz_kept[layer] = dz
        res_parts[layer] = res_local
    for layer in range(2):
        conv_parts[layer] = reduce_conv(cats[layer], dz_kept[layer])
    res_total = lax.psum(jnp.stack(res_parts), ("dp", "tm"))
    input_grad = grad.astype(jnp.bfloat16).reshape(s_dev, t_dev, width)
    conv_grad = (jnp.stack(conv_parts) * factor).astype(jnp.bfloat16)
    res_grad = (res_total * factor).astype(jnp.bfloat16)
    return (input_grad, conv_grad, res_grad)


def mm(a, b):
    return jnp.dot(a, b, preferred_element_type=F32)


def mm_nt(a, b):
    return lax.dot_general(a, b, (((1,), (1,)), ((), ())), preferred_element_type=F32)


def mm_tn(a, b):
    return lax.dot_general(a, b, (((0,), (0,)), ((), ())), preferred_element_type=F32)


def shaped(shape, dtype=BF16):
    return jax.ShapeDtypeStruct(shape, dtype)


def call(kernel, outs, *args, after=(), scratch=(), flops=0, nbytes=0, vmem=8, name=None):
    n_args = len(args)

    def run(*refs):
        kernel(*refs[:n_args], *refs[n_args + len(after) :])

    in_vmem = pl.BlockSpec(memory_space=pltpu.VMEM)
    return pl.pallas_call(
        run,
        out_shape=outs,
        in_specs=[in_vmem] * n_args + [pl.BlockSpec(memory_space=pl.ANY)] * len(after),
        out_specs=[in_vmem] * len(outs),
        scratch_shapes=list(scratch),
        compiler_params=pltpu.CompilerParams(vmem_limit_bytes=vmem * 1024 * 1024),
        cost_estimate=pl.CostEstimate(flops=flops, bytes_accessed=nbytes, transcendentals=0),
        name=name,
    )(*args, *after)


def place(tm):
    return tm // 4, lax.rem(tm // 2, 2), lax.rem(tm, 2)


def here():
    return place(lax.axis_index("tm"))


def copy_all(pairs, sems):
    copies = [pltpu.make_async_copy(src, dst, sems.at[i]) for i, (src, dst) in enumerate(pairs)]
    for copy in copies:
        copy.start()
    for copy in copies:
        copy.wait()


def load_slab_kernel(sig, grad, skip, own_out, tail_out, sems):
    t, width = sig.shape
    near = tail_out.shape[0]
    pairs = (
        (sig.at[t - near :, :], tail_out),
        (sig, own_out.at[:, 0:width]),
        (grad, own_out.at[:, width : 2 * width]),
        (skip, own_out.at[:, 2 * width :]),
    )
    copy_all(pairs, sems)


def load_weights_kernel(cw, rw, cw_out, rw_out, sems):
    copy_all(((cw, cw_out), (rw, rw_out)), sems)


def load(kernel, outs, flops, name, *arrays):
    in_hbm = [pltpu.with_memory_space_constraint(a, pltpu.HBM) for a in arrays]
    return pl.pallas_call(
        kernel,
        out_shape=[pltpu.VMEM(shape, BF16) for shape in outs],
        in_specs=[pl.BlockSpec(memory_space=pltpu.HBM)] * len(arrays),
        out_specs=[pl.BlockSpec(memory_space=pltpu.VMEM)] * len(outs),
        scratch_shapes=[pltpu.SemaphoreType.DMA((4,))],
        compiler_params=pltpu.CompilerParams(vmem_limit_bytes=8 * 1024 * 1024),
        cost_estimate=pl.CostEstimate(flops=flops, bytes_accessed=0, transcendentals=0),
        name=name,
    )(*in_hbm)


def pack_halo_kernel(far, tail4, out):
    t = far.shape[0]
    slab = lax.axis_index("tm")
    out[0:t, :] = jnp.where(slab >= 2, far[...], jnp.zeros_like(far))
    out[t:, :] = jnp.where(slab >= 4, tail4[...], jnp.zeros_like(tail4))


def split_quarters(staged, mine, by_y, by_x, by_both):
    _, x, _ = here()
    q = 2 * x + lax.axis_index("dp")
    mine[...] = staged[q]
    for k, out in ((1, by_y), (2, by_x), (3, by_both)):
        out[...] = staged[lax.bitwise_xor(q, k)]


def columns_of(a, core, block):
    count = a.shape[1] // block
    return jnp.where(
        core == 0,
        jnp.concatenate([a[:, i * block : (i + 1) * block] for i in range(0, count, 2)], axis=1),
        jnp.concatenate([a[:, i * block : (i + 1) * block] for i in range(1, count, 2)], axis=1),
    )


def own_kernel(own, own_other, halo, cw, rw, sig, gin, skin, z_out, e_out, es_out, far_out, behind_out):
    t = own.shape[0]
    near = t // 4
    width = sig.shape[1]
    _, _, core = here()
    for a, c in ((own, core), (own_other, 1 - core)):
        rows = pl.ds(pl.multiple_of(c * t, t), t)
        sig[rows, :] = a[:, 0:width]
        gin[rows, :] = a[:, width : 2 * width]
        skin[rows, :] = a[:, 2 * width :]
    z = mm(sig[...], cw[0, width:, :])
    z_out[0:near, :] = z[0:near, :]
    z_out[near:, :] = z[near:, :] + mm(sig[...], cw[0, 0:width, :])[: 2 * t - near, :]
    e_out[...] = mm_nt(gin[...], rw[1, :, 0:width]) + mm_nt(skin[...], rw[1, :, width:])
    es_out[...] = mm_nt(skin[...], rw[0, :, width:])
    far_out[...] = mm(halo[0:t, :], cw[0, width:, :])
    behind_out[...] = mm(halo[...], cw[0, 0:width, :])


def forward_and_outer_kernel(
    sig, z_own, e1, gin, skin, far_own, behind_own, halo, halo_other, cw, rw,
    mine, by_y, by_x, by_both, x_out, a_out, b_out, x1_out, dz_out, o_out, ga_out,
    staged, far, behind,
):
    t = sig.shape[0] // 2
    near = t // 4
    width = x_out.shape[1]
    gated = rw.shape[1]
    _, _, core = here()
    for h, c in ((halo, core), (halo_other, 1 - core)):
        x_out[pl.ds(pl.multiple_of(near + c * t, near), t), :] = h[0:t, :]
    x_out[near + 2 * t :, :] = sig[...]
    x_out[0:near, :] = jnp.where(core == 1, halo[t:, :], halo_other[t:, :])
    x0 = x_out[near:, :]
    far_other = mm(halo_other[0:t, :], cw[0, width:, :])
    behind_other = mm(halo_other[...], cw[0, 0:width, :])
    behind[0:near, :] = jnp.where(core == 1, behind_own[t:, :], behind_other[t:, :])
    for f, p, c in ((far_own[...], behind_own[0:t, :], core), (far_other, behind_other[0:t, :], 1 - core)):
        behind[pl.ds(pl.multiple_of(near + c * t, near), t), :] = p
        far[pl.ds(pl.multiple_of(c * t, t), t), :] = f
    z0 = jnp.concatenate(
        [far[...] + behind[0 : 2 * t, :], z_own[0:near, :] + behind[2 * t :, :], z_own[near:, :]], axis=0
    )
    tf = jnp.tanh(z0[:, :gated])
    sg = jax.nn.sigmoid(z0[:, gated:])
    h0 = (tf * sg).astype(BF16)
    a_out[...] = sg * (1.0 - tf * tf)
    b_out[...] = tf * sg * (1.0 - sg)
    x1 = (x0.astype(F32) + mm(h0, rw[0, :, 0:width])).astype(BF16)
    x1_out[...] = x1
    z1 = mm(x1[0 : 2 * t, :], cw[1, 0:width, :]) + mm(x1[2 * t :, :], cw[1, width:, :])
    tf = jnp.tanh(z1[:, :gated])
    sg = jax.nn.sigmoid(z1[:, gated:])
    h1 = (tf * sg).astype(BF16)
    g2 = gin[...]
    sk = skin[...]
    e = e1[...]
    dz1 = jnp.concatenate([e * sg * (1.0 - tf * tf), e * tf * sg * (1.0 - sg)], axis=1).astype(BF16)
    dz_out[...] = dz1
    dpast = mm_nt(dz1, cw[1, 0:width, :]).astype(BF16)
    ga = g2.astype(F32) + mm_nt(dz1, cw[1, width:, :])
    ga_out[...] = ga
    outer = jnp.concatenate([dpast, ga.astype(BF16)], axis=0)
    o_out[...] = outer
    part = gated // 2
    mine_h0 = jnp.where(core == 0, h0[:, :part], h0[:, part:])
    mine_h1 = jnp.where(core == 0, h1[:, :part], h1[:, part:])
    skips = jnp.concatenate([mm_tn(mine_h1, sk), mm_tn(mine_h0[2 * t :, :], sk)], axis=1)
    eighth = gated // 8
    for which, part in enumerate((mm_tn(mine_h1, g2), mm_tn(mine_h0, outer), skips)):
        for q in range(4):
            staged[q, which * eighth : (which + 1) * eighth, :] = part[q * eighth : (q + 1) * eighth, :].astype(BF16)
    split_quarters(staged, mine, by_y, by_x, by_both)


def inner_kernel(
    xin, a, b, x1, dz1, outer, es, cw, rw,
    mine, by_y, by_x, by_both, dz, tail,
    staged, mine_in,
):
    width = xin.shape[1]
    t = dz1.shape[0] // 2
    near = t // 4
    e0 = mm_nt(outer[...], rw[0, :, 0:width])
    e0 = jnp.concatenate([e0[: 2 * t, :], e0[2 * t :, :] + es[...]], axis=0)
    dz0 = jnp.concatenate([e0 * a[...], e0 * b[...]], axis=1).astype(BF16)
    dz[0 : 4 * t, :] = dz0
    dz[4 * t :, :] = jnp.zeros((near, width), BF16)
    tail[...] = mm_nt(dz0[0:near, :], cw[0, 0:width, :]).astype(BF16)
    half = width // 16
    rows = 2 * half
    _, _, core = here()
    mine_in[...] = columns_of(xin[...], core, rows)
    mine_x1 = columns_of(x1[...], core, rows)
    pairs = width // rows // 2
    for base, part0, part1 in (
        (0, mm_tn(mine_in[0 : 4 * t, :], dz0), mm_tn(mine_x1[0 : 2 * t, :], dz1[...])),
        (pairs, mm_tn(mine_in[near:, :], dz0), mm_tn(mine_x1[2 * t :, :], dz1[...])),
    ):
        for block in range(pairs):
            g, x = (base + block) // 2, (base + block) % 2
            for y in range(2):
                src = slice(block * rows + y * half, block * rows + (y + 1) * half)
                staged[2 * x + y, g, 0:half, :] = part0[src, :].astype(BF16)
                staged[2 * x + y, g, half:, :] = part1[src, :].astype(BF16)
    split_quarters(staged, mine, by_y, by_x, by_both)


def signal_kernel(dz, outer, ga, cw, own_out, back_out):
    t = ga.shape[0] // 2
    near = t // 4
    width = ga.shape[1]
    _, _, core = here()
    at = pl.multiple_of(core * t, t)
    long = t + near
    back = dz[pl.ds(at, long), :]
    here_dz = dz[pl.ds(2 * t + at, long), :]
    both = jnp.concatenate([back, here_dz], axis=0)
    wp = mm_nt(both, cw[0, 0:width, :]).astype(BF16)
    wx = mm_nt(both, cw[0, width:, :])
    back_out[...] = (outer[pl.ds(at, t), :].astype(F32) + wx[0:t, :] + wp[near:long, :].astype(F32)).astype(BF16)
    own_out[...] = ga[pl.ds(at, t), :] + wx[long : long + t, :] + wp[long + near :, :].astype(F32)


def total_of(*refs):
    total = refs[0][...].astype(F32)
    for ref in refs[1:]:
        total = total + ref[...].astype(F32)
    return total


def sum_xy_kernel(mine, by_both, by_x, by_y, tail, out):
    rows = mine.shape[0]
    out[0:rows, :] = total_of(mine, by_y, by_x, by_both).astype(BF16)
    out[rows:, :] = tail[...]


def sum_z1_kernel(rows, mine, got, out):
    out[0:rows, :] = total_of(mine.at[0:rows, :], got.at[0:rows, :]).astype(BF16)
    out[rows:, :] = mine[rows:, :]


def sum_z2_kernel(factor, mine, got, out):
    rows = out.shape[0]
    out[...] = (total_of(mine.at[0:rows, :], got.at[0:rows, :]) * factor).astype(BF16)


def scaled_sum_kernel(factor, *refs):
    refs[-1][...] = (total_of(*refs[:-1]) * factor).astype(BF16)


def groups_kernel(mine, by_y, by_x, by_both, keep, send1, send2, send3, staged):
    g, _, _ = here()
    staged[...] = total_of(mine, by_y, by_x, by_both)
    keep[...] = staged[g]
    for k, out in ((1, send1), (2, send2), (3, send3)):
        out[...] = staged[lax.bitwise_xor(g, k)].astype(BF16)


def in_order_kernel(mine, by_y, by_x, by_both, out):
    _, x, _ = here()
    q = 2 * x + lax.axis_index("dp")
    for k, ref in enumerate((mine, by_y, by_x, by_both)):
        out[lax.bitwise_xor(q, k)] = ref[...]


def finish_conv_kernel(mine, other, conv, done):
    done[...] = jnp.zeros_like(done)
    y = lax.axis_index("dp")
    half = mine.shape[0] // 2
    for ref, at in ((mine, y), (other, 1 - y)):
        rows = pl.ds(pl.multiple_of(at * half, half), half)
        conv[0, rows, :] = ref[0:half, :]
        conv[1, rows, :] = ref[half:, :]


def finish_kernel(mine, other, own, come, got1, got2, res, grad):
    _, _, core = here()
    eighth = res.shape[1] // 8
    width, part = mine.shape[2], mine.shape[2] // 2
    for ref, c in ((mine, core), (other, 1 - core)):
        for q in range(4):
            rows = pl.ds(pl.multiple_of((4 * c + q) * eighth, eighth), eighth)
            res[1, rows, 0:width] = ref[q, 0:eighth, :]
            res[0, rows, 0:width] = ref[q, eighth : 2 * eighth, :]
            res[1, rows, width:] = ref[q, 2 * eighth :, 0:part]
            res[0, rows, width:] = ref[q, 2 * eighth :, part:]
    t = own.shape[0]
    near = t // 4
    first = got1.shape[0] - near
    g, _, _ = here()
    total = own[...] + jnp.where(lax.axis_index("tm") < 14, come[...].astype(F32), 0.0)
    grad[0 : t - near, :] = total[0 : t - near, :].astype(BF16)
    last = jnp.where(lax.rem(g, 2) == 0, got1[first:, :], got2[first:, :]).astype(F32)
    last = jnp.where((g < 3) & (core == 1), last, 0.0)
    grad[t - near :, :] = (total[t - near :, :] + last).astype(BF16)


def hold_kernel(a, out):
    out[...] = a[...]


def swap(x, distance):
    return lax.ppermute(x, "tm", [(i, i ^ distance) for i in range(16)])


def swap_streams(x):
    return lax.ppermute(x, "dp", [(0, 1), (1, 0)])


def swap_both(x, distance):
    route = [(16 * y + i, 16 * (1 - y) + (i ^ distance)) for y in range(2) for i in range(16)]
    return lax.ppermute(x, ("dp", "tm"), route)


def shift(x, distance):
    return lax.ppermute(x, "tm", [(i, (i + distance) % 16) for i in range(16)])


def body(signal, conv_weight, res_weight, grad_out, skip_cotangent):
    s_dev, t, width = signal.shape
    gated = res_weight.shape[1]
    near = t // 4
    half = width // 16
    res_rows = 3 * gated // 8
    factor = float(s_dev * t * 32) ** (-0.5)

    far = shift(signal[0], 2)
    own, tail = load(
        load_slab_kernel, [(t, 2 * width + skip_cotangent.shape[2]), (near, width)], 0, "load_slab",
        signal[0], grad_out[0], skip_cotangent[0],
    )
    cw, rw = load(
        load_weights_kernel, [conv_weight.shape, res_weight.shape], 4_000_000_000, "load_weights",
        conv_weight, res_weight,
    )
    own_other = swap(own, 1)
    tail4 = shift(tail, 4)
    (halo,) = call(pack_halo_kernel, [shaped((t + near, width))], far, tail4, after=(cw,), flops=5_000_000_000, name="pack_halo")
    halo_other = swap(halo, 1)

    res = shaped((res_rows, width))
    sig, gin, skin, z_own, e1, es, far_own, behind_own = call(
        own_kernel,
        [
            shaped((2 * t, width)), shaped((2 * t, width)), shaped((2 * t, gated)), shaped((2 * t, 2 * gated), F32),
            shaped((2 * t, gated), F32), shaped((2 * t, gated), F32),
            shaped((t, 2 * gated), F32), shaped((t + near, 2 * gated), F32),
        ],
        own, own_other, halo, cw, rw, vmem=16, flops=2_000_000_000, name="own",
    )
    *rsplit, xin, a, b, x1, dz1, outer, ga = call(
        forward_and_outer_kernel,
        [
            res, res, res, res,
            shaped((4 * t + near, width)), shaped((4 * t, gated), F32), shaped((4 * t, gated), F32),
            shaped((4 * t, width)), shaped((2 * t, width)), shaped((4 * t, width)), shaped((2 * t, width), F32),
        ],
        sig, z_own, e1, gin, skin, far_own, behind_own, halo, halo_other, cw, rw,
        scratch=[
            pltpu.VMEM((4, res_rows, width), BF16), pltpu.VMEM((2 * t, 2 * gated), F32),
            pltpu.VMEM((2 * t + near, 2 * gated), F32),
        ], vmem=16, name="forward_and_outer",
    )
    piece = (2 * half, width)
    part = shaped((4,) + piece)
    *csplit, dz0, tail = call(
        inner_kernel, [part, part, part, part, shaped((4 * t + near, width)), shaped((near, width))],
        xin, a, b, x1, dz1, outer, es, cw, rw,
        scratch=[pltpu.VMEM((4, 4) + piece, BF16), pltpu.VMEM((4 * t + near, width // 2), BF16)], vmem=16, flops=2_000_000_000, name="inner",
    )
    def around(by_y, by_x, by_both):
        both = swap_both(by_both, 2)
        beside = swap(by_x, 2)
        return swap_streams(by_y), beside, both

    rterms = (rsplit[0],) + around(*rsplit[1:])[::-1]
    cterms = (csplit[0],) + around(*csplit[1:])
    long = shaped((res_rows + near, width))
    (rsum,) = call(sum_xy_kernel, [long], *rterms, tail, after=(csplit[0],), name="res_sum_xy")
    rgot1 = swap(rsum, 4)
    own, back = call(
        signal_kernel, [shaped((t, width), F32), shaped((t, width))], dz0, outer, ga, cw,
        after=(rsum,), vmem=16, flops=1_000_000_000, name="signal",
    )
    (rsum,) = call(functools.partial(sum_z1_kernel, res_rows), [long], rsum, rgot1, name="res_sum_z1")
    rgot2 = swap(rsum, 12)
    ckeep, *csend = call(
        groups_kernel, [shaped(piece, F32)] + [shaped(piece)] * 3, *cterms,
        after=(rsum, back), scratch=[pltpu.VMEM((4,) + piece, F32)], name="conv_groups",
    )
    cgot = [swap(csend[k - 1], 4 * k) for k in (2, 3, 1)]
    (quarter,) = call(
        functools.partial(sum_z2_kernel, factor), [res], rsum, rgot2, after=(ckeep,), name="res_sum_z2"
    )
    rparts = (quarter, swap_streams(quarter), swap(quarter, 2), swap_both(quarter, 2))
    (back,) = call(hold_kernel, [shaped((t, width))], back, after=(ckeep,), name="hold")
    come = shift(back, -2)
    (mine,) = call(
        functools.partial(scaled_sum_kernel, factor), [shaped(piece)], ckeep, *cgot,
        after=(quarter,), flops=10_000_000_000, name="conv_scaled",
    )
    other = swap_streams(mine)
    (ordered,) = call(in_order_kernel, [shaped((4, res_rows, width))], *rparts, after=(mine,), name="res_in_order")
    rgot = swap(ordered, 1)
    conv_grad, conv_done = call(
        finish_conv_kernel, [shaped((2,) + piece), shaped((8, 128), F32)], mine, other,
        flops=10_000_000_000, name="finish_conv",
    )
    res_grad, input_grad = call(
        finish_kernel, [shaped(res_weight.shape), shaped((t, width))], ordered, rgot, own, come, rgot1, rgot2,
        after=(conv_done,), name="finish",
    )
    return (input_grad.reshape(s_dev, t, width), conv_grad, res_grad)


def solution(mesh):
    in_specs = (P("dp", "tm", None), P(), P(), P("dp", "tm", None), P("dp", "tm", None))
    out_specs = (P("dp", "tm", None), P(None, "tm", None), P())
    chosen = body if mesh.shape["dp"] == 2 and mesh.shape["tm"] == 16 else general_body
    return jax.shard_map(chosen, mesh=mesh, in_specs=in_specs, out_specs=out_specs, check_vma=False)
```

```python
import functools

import jax
import jax.numpy as jnp
from jax import lax
from jax.experimental import pallas as pl
from jax.experimental.pallas import tpu as pltpu
from jax.sharding import PartitionSpec as P

F32 = jnp.float32
BF16 = jnp.bfloat16


def passed_along(block, axis, distance):
    devices = range(lax.axis_size(axis))
    route = [(i - distance, i) for i in devices if i - distance in devices]
    return lax.ppermute(block, axis, route)


def gate_gradients(dh, z, gated):
    tf = jnp.tanh(z[:, :gated])
    sg = jax.nn.sigmoid(z[:, gated:])
    return jnp.concatenate([dh * sg * (1.0 - tf * tf), dh * tf * sg * (1.0 - sg)], axis=1).astype(
        jnp.bfloat16
    )


def reduce_conv(cat_rows, dz):
    piece = lax.psum_scatter(
        lax.dot_general(cat_rows, dz, (((0,), (0,)), ((), ())), preferred_element_type=jnp.float32),
        "tm",
        scatter_dimension=0,
        tiled=True,
    )
    return lax.psum(piece, "dp")


def general_body(signal, conv_weight, res_weight, grad_out, skip_cotangent):
    s_dev, t_dev, width = signal.shape
    gated = res_weight.shape[1]
    near = t_dev // 4
    slabs = lax.axis_size("tm") // 8
    count_rows = s_dev * t_dev
    factor = float(count_rows * lax.axis_size("dp") * lax.axis_size("tm")) ** (-0.5)

    def delayed(x, layer):
        if layer == 0:
            got = passed_along(x[:, t_dev - near :, :], "tm", 1)
            return jnp.concatenate([got, x[:, : t_dev - near, :]], axis=1)
        return passed_along(x, "tm", slabs)

    def shifted_rows(dpast, layer):
        if layer == 0:
            got = passed_along(dpast[:, :near, :], "tm", -1)
            return jnp.concatenate([dpast[:, near:, :], got], axis=1)
        return passed_along(dpast, "tm", -slabs)

    x = signal
    cats = []
    zvals = []
    hvals = []
    for layer in range(2):
        past = delayed(x, layer)
        cat_rows = jnp.concatenate([past, x], axis=2).reshape(count_rows, 2 * width)
        z = jnp.dot(cat_rows, conv_weight[layer], preferred_element_type=jnp.float32)
        h = (jnp.tanh(z[:, :gated]) * jax.nn.sigmoid(z[:, gated:])).astype(jnp.bfloat16)
        cats.append(cat_rows)
        zvals.append(z)
        hvals.append(h)
        if layer == 0:
            resid = jnp.dot(h, res_weight[0][:, :width], preferred_element_type=jnp.float32)
            x = (
                (x.reshape(count_rows, width).astype(jnp.float32) + resid)
                .astype(jnp.bfloat16)
                .reshape(s_dev, t_dev, width)
            )
    grad = grad_out.reshape(count_rows, width).astype(jnp.float32)
    skip_rows = skip_cotangent.reshape(count_rows, -1)
    conv_parts = [None, None]
    res_parts = [None, None]
    dz_kept = [None, None]
    for layer in (1, 0):
        outer = jnp.concatenate([grad.astype(jnp.bfloat16), skip_rows], axis=1)
        dh = lax.dot_general(
            outer, res_weight[layer], (((1,), (1,)), ((), ())), preferred_element_type=jnp.float32
        )
        dz = gate_gradients(dh, zvals[layer], gated)
        wcat = lax.dot_general(
            dz, conv_weight[layer], (((1,), (1,)), ((), ())), preferred_element_type=jnp.float32
        )
        dpast = wcat[:, :width].astype(jnp.bfloat16).reshape(s_dev, t_dev, width)
        moved = shifted_rows(dpast, layer).reshape(count_rows, width)
        grad = grad + wcat[:, width:] + moved.astype(jnp.float32)
        res_local = lax.dot_general(
            hvals[layer], outer, (((0,), (0,)), ((), ())), preferred_element_type=jnp.float32
        )
        dz_kept[layer] = dz
        res_parts[layer] = res_local
    for layer in range(2):
        conv_parts[layer] = reduce_conv(cats[layer], dz_kept[layer])
    res_total = lax.psum(jnp.stack(res_parts), ("dp", "tm"))
    input_grad = grad.astype(jnp.bfloat16).reshape(s_dev, t_dev, width)
    conv_grad = (jnp.stack(conv_parts) * factor).astype(jnp.bfloat16)
    res_grad = (res_total * factor).astype(jnp.bfloat16)
    return (input_grad, conv_grad, res_grad)


def mm(a, b):
    return jnp.dot(a, b, preferred_element_type=F32)


def mm_nt(a, b):
    return lax.dot_general(a, b, (((1,), (1,)), ((), ())), preferred_element_type=F32)


def mm_tn(a, b):
    return lax.dot_general(a, b, (((0,), (0,)), ((), ())), preferred_element_type=F32)


def shaped(shape, dtype=BF16):
    return jax.ShapeDtypeStruct(shape, dtype)


def call(kernel, outs, *args, after=(), scratch=(), flops=0, nbytes=0, vmem=8, name=None):
    n_args = len(args)

    def run(*refs):
        kernel(*refs[:n_args], *refs[n_args + len(after) :])

    in_vmem = pl.BlockSpec(memory_space=pltpu.VMEM)
    return pl.pallas_call(
        run,
        out_shape=outs,
        in_specs=[in_vmem] * n_args + [pl.BlockSpec(memory_space=pl.ANY)] * len(after),
        out_specs=[in_vmem] * len(outs),
        scratch_shapes=list(scratch),
        compiler_params=pltpu.CompilerParams(vmem_limit_bytes=vmem * 1024 * 1024),
        cost_estimate=pl.CostEstimate(flops=flops, bytes_accessed=nbytes, transcendentals=0),
        name=name,
    )(*args, *after)


def place(tm):
    return tm // 4, lax.rem(tm // 2, 2), lax.rem(tm, 2)


def here():
    return place(lax.axis_index("tm"))


def copy_all(pairs, sems):
    copies = [pltpu.make_async_copy(src, dst, sems.at[i]) for i, (src, dst) in enumerate(pairs)]
    for copy in copies:
        copy.start()
    for copy in copies:
        copy.wait()


def load_slab_kernel(sig, grad, skip, own_out, tail_out, sems):
    t, width = sig.shape
    near = tail_out.shape[0]
    pairs = (
        (sig.at[t - near :, :], tail_out),
        (sig, own_out.at[:, 0:width]),
        (grad, own_out.at[:, width : 2 * width]),
        (skip, own_out.at[:, 2 * width :]),
    )
    copy_all(pairs, sems)


def load_weights_kernel(cw, rw, cw_out, rw_out, sems):
    copy_all(((cw, cw_out), (rw, rw_out)), sems)


def load(kernel, outs, flops, name, *arrays):
    in_hbm = [pltpu.with_memory_space_constraint(a, pltpu.HBM) for a in arrays]
    return pl.pallas_call(
        kernel,
        out_shape=[pltpu.VMEM(shape, BF16) for shape in outs],
        in_specs=[pl.BlockSpec(memory_space=pltpu.HBM)] * len(arrays),
        out_specs=[pl.BlockSpec(memory_space=pltpu.VMEM)] * len(outs),
        scratch_shapes=[pltpu.SemaphoreType.DMA((4,))],
        compiler_params=pltpu.CompilerParams(vmem_limit_bytes=8 * 1024 * 1024),
        cost_estimate=pl.CostEstimate(flops=flops, bytes_accessed=0, transcendentals=0),
        name=name,
    )(*in_hbm)


def pack_halo_kernel(far, tail4, out):
    t = far.shape[0]
    slab = lax.axis_index("tm")
    out[0:t, :] = jnp.where(slab >= 2, far[...], jnp.zeros_like(far))
    out[t:, :] = jnp.where(slab >= 4, tail4[...], jnp.zeros_like(tail4))


def split_quarters(staged, mine, by_y, by_x, by_both):
    _, x, _ = here()
    q = 2 * x + lax.axis_index("dp")
    mine[...] = staged[q]
    for k, out in ((1, by_y), (2, by_x), (3, by_both)):
        out[...] = staged[lax.bitwise_xor(q, k)]


def columns_of(a, core, block):
    count = a.shape[1] // block
    return jnp.where(
        core == 0,
        jnp.concatenate([a[:, i * block : (i + 1) * block] for i in range(0, count, 2)], axis=1),
        jnp.concatenate([a[:, i * block : (i + 1) * block] for i in range(1, count, 2)], axis=1),
    )


def own_kernel(own, own_other, cw, rw, sig, gin, skin, z_out, e_out, es_out):
    t = own.shape[0]
    near = t // 4
    width = sig.shape[1]
    _, _, core = here()
    for a, c in ((own, core), (own_other, 1 - core)):
        rows = pl.ds(pl.multiple_of(c * t, t), t)
        sig[rows, :] = a[:, 0:width]
        gin[rows, :] = a[:, width : 2 * width]
        skin[rows, :] = a[:, 2 * width :]
    z = mm(sig[...], cw[0, width:, :])
    z_out[0:near, :] = z[0:near, :]
    z_out[near:, :] = z[near:, :] + mm(sig[...], cw[0, 0:width, :])[: 2 * t - near, :]
    e_out[...] = mm_nt(gin[...], rw[1, :, 0:width]) + mm_nt(skin[...], rw[1, :, width:])
    es_out[...] = mm_nt(skin[...], rw[0, :, width:])


def forward_and_outer_kernel(
    sig, z_own, e1, gin, skin, halo, halo_other, cw, rw,
    mine, by_y, by_x, by_both, x_out, a_out, b_out, x1_out, dz_out, o_out, ga_out,
    staged,
):
    t = sig.shape[0] // 2
    near = t // 4
    width = x_out.shape[1]
    gated = rw.shape[1]
    _, _, core = here()
    for h, c in ((halo, core), (halo_other, 1 - core)):
        x_out[pl.ds(pl.multiple_of(near + c * t, near), t), :] = h[0:t, :]
    x_out[near + 2 * t :, :] = sig[...]
    x_out[0:near, :] = jnp.where(core == 1, halo[t:, :], halo_other[t:, :])
    x0 = x_out[near:, :]
    behind = mm(x_out[0 : 2 * t + near, :], cw[0, 0:width, :])
    z0 = jnp.concatenate(
        [
            behind[0 : 2 * t, :] + mm(x_out[near : 2 * t + near, :], cw[0, width:, :]),
            z_own[0:near, :] + behind[2 * t :, :],
            z_own[near:, :],
        ],
        axis=0,
    )
    tf = jnp.tanh(z0[:, :gated])
    sg = jax.nn.sigmoid(z0[:, gated:])
    h0 = (tf * sg).astype(BF16)
    a_out[...] = sg * (1.0 - tf * tf)
    b_out[...] = tf * sg * (1.0 - sg)
    x1 = (x0.astype(F32) + mm(h0, rw[0, :, 0:width])).astype(BF16)
    x1_out[...] = x1
    z1 = mm(x1[0 : 2 * t, :], cw[1, 0:width, :]) + mm(x1[2 * t :, :], cw[1, width:, :])
    tf = jnp.tanh(z1[:, :gated])
    sg = jax.nn.sigmoid(z1[:, gated:])
    h1 = (tf * sg).astype(BF16)
    g2 = gin[...]
    sk = skin[...]
    e = e1[...]
    dz1 = jnp.concatenate([e * sg * (1.0 - tf * tf), e * tf * sg * (1.0 - sg)], axis=1).astype(BF16)
    dz_out[...] = dz1
    dpast = mm_nt(dz1, cw[1, 0:width, :]).astype(BF16)
    ga = g2.astype(F32) + mm_nt(dz1, cw[1, width:, :])
    ga_out[...] = ga
    outer = jnp.concatenate([dpast, ga.astype(BF16)], axis=0)
    o_out[...] = outer
    part = gated // 2
    mine_h0 = jnp.where(core == 0, h0[:, :part], h0[:, part:])
    mine_h1 = jnp.where(core == 0, h1[:, :part], h1[:, part:])
    skips = jnp.concatenate([mm_tn(mine_h1, sk), mm_tn(mine_h0[2 * t :, :], sk)], axis=1)
    eighth = gated // 8
    for which, part in enumerate((mm_tn(mine_h1, g2), mm_tn(mine_h0, outer), skips)):
        for q in range(4):
            staged[q, which * eighth : (which + 1) * eighth, :] = part[q * eighth : (q + 1) * eighth, :].astype(BF16)
    split_quarters(staged, mine, by_y, by_x, by_both)


def inner_kernel(
    xin, a, b, x1, dz1, outer, es, cw, rw,
    mine, by_y, by_x, by_both, dz, tail,
    staged, mine_in,
):
    width = xin.shape[1]
    t = dz1.shape[0] // 2
    near = t // 4
    e0 = mm_nt(outer[...], rw[0, :, 0:width])
    e0 = jnp.concatenate([e0[: 2 * t, :], e0[2 * t :, :] + es[...]], axis=0)
    dz0 = jnp.concatenate([e0 * a[...], e0 * b[...]], axis=1).astype(BF16)
    dz[0 : 4 * t, :] = dz0
    dz[4 * t :, :] = jnp.zeros((near, width), BF16)
    tail[...] = mm_nt(dz0[0:near, :], cw[0, 0:width, :]).astype(BF16)
    half = width // 16
    rows = 2 * half
    _, _, core = here()
    mine_in[...] = columns_of(xin[...], core, rows)
    mine_x1 = columns_of(x1[...], core, rows)
    pairs = width // rows // 2
    for base, part0, part1 in (
        (0, mm_tn(mine_in[0 : 4 * t, :], dz0), mm_tn(mine_x1[0 : 2 * t, :], dz1[...])),
        (pairs, mm_tn(mine_in[near:, :], dz0), mm_tn(mine_x1[2 * t :, :], dz1[...])),
    ):
        for block in range(pairs):
            g, x = (base + block) // 2, (base + block) % 2
            for y in range(2):
                src = slice(block * rows + y * half, block * rows + (y + 1) * half)
                staged[2 * x + y, g, 0:half, :] = part0[src, :].astype(BF16)
                staged[2 * x + y, g, half:, :] = part1[src, :].astype(BF16)
    split_quarters(staged, mine, by_y, by_x, by_both)


def signal_kernel(dz, outer, ga, cw, own_out, back_out):
    t = ga.shape[0] // 2
    near = t // 4
    width = ga.shape[1]
    _, _, core = here()
    at = pl.multiple_of(core * t, t)
    long = t + near
    back = dz[pl.ds(at, long), :]
    here_dz = dz[pl.ds(2 * t + at, long), :]
    both = jnp.concatenate([back, here_dz], axis=0)
    wp = mm_nt(both, cw[0, 0:width, :]).astype(BF16)
    wx = mm_nt(both, cw[0, width:, :])
    back_out[...] = (outer[pl.ds(at, t), :].astype(F32) + wx[0:t, :] + wp[near:long, :].astype(F32)).astype(BF16)
    own_out[...] = ga[pl.ds(at, t), :] + wx[long : long + t, :] + wp[long + near :, :].astype(F32)


def total_of(*refs):
    total = refs[0][...].astype(F32)
    for ref in refs[1:]:
        total = total + ref[...].astype(F32)
    return total


def sum_xy_kernel(mine, by_both, by_x, by_y, tail, out):
    rows = mine.shape[0]
    out[0:rows, :] = total_of(mine, by_y, by_x, by_both).astype(BF16)
    out[rows:, :] = tail[...]


def sum_z1_kernel(rows, mine, got, out):
    out[0:rows, :] = total_of(mine.at[0:rows, :], got.at[0:rows, :]).astype(BF16)
    out[rows:, :] = mine[rows:, :]


def sum_z2_kernel(factor, mine, got, out):
    rows = out.shape[0]
    out[...] = (total_of(mine.at[0:rows, :], got.at[0:rows, :]) * factor).astype(BF16)


def scaled_sum_kernel(factor, *refs):
    refs[-1][...] = (total_of(*refs[:-1]) * factor).astype(BF16)


def groups_kernel(mine, by_y, by_x, by_both, keep, send1, send2, send3, staged):
    g, _, _ = here()
    staged[...] = total_of(mine, by_y, by_x, by_both)
    keep[...] = staged[g]
    for k, out in ((1, send1), (2, send2), (3, send3)):
        out[...] = staged[lax.bitwise_xor(g, k)].astype(BF16)


def in_order_kernel(mine, by_y, by_x, by_both, out):
    _, x, _ = here()
    q = 2 * x + lax.axis_index("dp")
    for k, ref in enumerate((mine, by_y, by_x, by_both)):
        out[lax.bitwise_xor(q, k)] = ref[...]


def finish_conv_kernel(mine, other, conv, done):
    done[...] = jnp.zeros_like(done)
    y = lax.axis_index("dp")
    half = mine.shape[0] // 2
    for ref, at in ((mine, y), (other, 1 - y)):
        rows = pl.ds(pl.multiple_of(at * half, half), half)
        conv[0, rows, :] = ref[0:half, :]
        conv[1, rows, :] = ref[half:, :]


def finish_kernel(mine, other, own, come, got1, got2, res, grad):
    _, _, core = here()
    eighth = res.shape[1] // 8
    width, part = mine.shape[2], mine.shape[2] // 2
    for ref, c in ((mine, core), (other, 1 - core)):
        for q in range(4):
            rows = pl.ds(pl.multiple_of((4 * c + q) * eighth, eighth), eighth)
            res[1, rows, 0:width] = ref[q, 0:eighth, :]
            res[0, rows, 0:width] = ref[q, eighth : 2 * eighth, :]
            res[1, rows, width:] = ref[q, 2 * eighth :, 0:part]
            res[0, rows, width:] = ref[q, 2 * eighth :, part:]
    t = own.shape[0]
    near = t // 4
    first = got1.shape[0] - near
    g, _, _ = here()
    total = own[...] + jnp.where(lax.axis_index("tm") < 14, come[...].astype(F32), 0.0)
    grad[0 : t - near, :] = total[0 : t - near, :].astype(BF16)
    last = jnp.where(lax.rem(g, 2) == 0, got1[first:, :], got2[first:, :]).astype(F32)
    last = jnp.where((g < 3) & (core == 1), last, 0.0)
    grad[t - near :, :] = (total[t - near :, :] + last).astype(BF16)


def hold_kernel(a, out):
    out[...] = a[...]


def swap(x, distance):
    return lax.ppermute(x, "tm", [(i, i ^ distance) for i in range(16)])


def swap_streams(x):
    return lax.ppermute(x, "dp", [(0, 1), (1, 0)])


def swap_both(x, distance):
    route = [(16 * y + i, 16 * (1 - y) + (i ^ distance)) for y in range(2) for i in range(16)]
    return lax.ppermute(x, ("dp", "tm"), route)


def shift(x, distance):
    return lax.ppermute(x, "tm", [(i, (i + distance) % 16) for i in range(16)])


def body(signal, conv_weight, res_weight, grad_out, skip_cotangent):
    s_dev, t, width = signal.shape
    gated = res_weight.shape[1]
    near = t // 4
    half = width // 16
    res_rows = 3 * gated // 8
    factor = float(s_dev * t * 32) ** (-0.5)

    far = shift(signal[0], 2)
    own, tail = load(
        load_slab_kernel, [(t, 2 * width + skip_cotangent.shape[2]), (near, width)], 0, "load_slab",
        signal[0], grad_out[0], skip_cotangent[0],
    )
    cw, rw = load(
        load_weights_kernel, [conv_weight.shape, res_weight.shape], 4_000_000_000, "load_weights",
        conv_weight, res_weight,
    )
    own_other = swap(own, 1)
    tail4 = shift(tail, 4)
    (halo,) = call(pack_halo_kernel, [shaped((t + near, width))], far, tail4, after=(cw,), flops=5_000_000_000, name="pack_halo")
    halo_other = swap(halo, 1)

    res = shaped((res_rows, width))
    sig, gin, skin, z_own, e1, es = call(
        own_kernel,
        [
            shaped((2 * t, width)), shaped((2 * t, width)), shaped((2 * t, gated)), shaped((2 * t, 2 * gated), F32),
            shaped((2 * t, gated), F32), shaped((2 * t, gated), F32),
        ],
        own, own_other, cw, rw, vmem=16, flops=2_000_000_000, name="own",
    )
    *rsplit, xin, a, b, x1, dz1, outer, ga = call(
        forward_and_outer_kernel,
        [
            res, res, res, res,
            shaped((4 * t + near, width)), shaped((4 * t, gated), F32), shaped((4 * t, gated), F32),
            shaped((4 * t, width)), shaped((2 * t, width)), shaped((4 * t, width)), shaped((2 * t, width), F32),
        ],
        sig, z_own, e1, gin, skin, halo, halo_other, cw, rw,
        scratch=[pltpu.VMEM((4, res_rows, width), BF16)], vmem=16, name="forward_and_outer",
    )
    piece = (2 * half, width)
    part = shaped((4,) + piece)
    *csplit, dz0, tail = call(
        inner_kernel, [part, part, part, part, shaped((4 * t + near, width)), shaped((near, width))],
        xin, a, b, x1, dz1, outer, es, cw, rw,
        scratch=[pltpu.VMEM((4, 4) + piece, BF16), pltpu.VMEM((4 * t + near, width // 2), BF16)], vmem=16, flops=2_000_000_000, name="inner",
    )
    def around(by_y, by_x, by_both):
        both = swap_both(by_both, 2)
        beside = swap(by_x, 2)
        return swap_streams(by_y), beside, both

    rterms = (rsplit[0],) + around(*rsplit[1:])[::-1]
    cterms = (csplit[0],) + around(*csplit[1:])
    long = shaped((res_rows + near, width))
    (rsum,) = call(sum_xy_kernel, [long], *rterms, tail, after=(csplit[0],), name="res_sum_xy")
    rgot1 = swap(rsum, 4)
    own, back = call(
        signal_kernel, [shaped((t, width), F32), shaped((t, width))], dz0, outer, ga, cw,
        after=(rsum,), vmem=16, flops=1_000_000_000, name="signal",
    )
    (rsum,) = call(functools.partial(sum_z1_kernel, res_rows), [long], rsum, rgot1, name="res_sum_z1")
    rgot2 = swap(rsum, 12)
    ckeep, *csend = call(
        groups_kernel, [shaped(piece, F32)] + [shaped(piece)] * 3, *cterms,
        after=(rsum, back), scratch=[pltpu.VMEM((4,) + piece, F32)], name="conv_groups",
    )
    cgot = [swap(csend[k - 1], 4 * k) for k in (2, 3, 1)]
    (quarter,) = call(
        functools.partial(sum_z2_kernel, factor), [res], rsum, rgot2, after=(ckeep,), name="res_sum_z2"
    )
    rparts = (quarter, swap_streams(quarter), swap(quarter, 2), swap_both(quarter, 2))
    (back,) = call(hold_kernel, [shaped((t, width))], back, after=(ckeep,), name="hold")
    come = shift(back, -2)
    (mine,) = call(
        functools.partial(scaled_sum_kernel, factor), [shaped(piece)], ckeep, *cgot,
        after=(quarter,), flops=10_000_000_000, name="conv_scaled",
    )
    other = swap_streams(mine)
    (ordered,) = call(in_order_kernel, [shaped((4, res_rows, width))], *rparts, after=(mine,), name="res_in_order")
    rgot = swap(ordered, 1)
    conv_grad, conv_done = call(
        finish_conv_kernel, [shaped((2,) + piece), shaped((8, 128), F32)], mine, other,
        flops=10_000_000_000, name="finish_conv",
    )
    res_grad, input_grad = call(
        finish_kernel, [shaped(res_weight.shape), shaped((t, width))], ordered, rgot, own, come, rgot1, rgot2,
        after=(conv_done,), name="finish",
    )
    return (input_grad.reshape(s_dev, t, width), conv_grad, res_grad)


def solution(mesh):
    in_specs = (P("dp", "tm", None), P(), P(), P("dp", "tm", None), P("dp", "tm", None))
    out_specs = (P("dp", "tm", None), P(None, "tm", None), P())
    chosen = body if mesh.shape["dp"] == 2 and mesh.shape["tm"] == 16 else general_body
    return jax.shard_map(chosen, mesh=mesh, in_specs=in_specs, out_specs=out_specs, check_vma=False)
```
